512 devices in a mesh: dom: 64 (over x, z), orb: 8 (over y, core).
Axes of the slice: x: 4, y: 4, z: 16, core: 2. Of those that a mesh axis runs over, the one named last changes fastest.
Arguments:
- orbitals: bfloat16 [3072, 64, 512], P('dom', 'orb'), may hold values from -6 to 6
- adjoint_source: bfloat16 [3072, 64, 512], P('dom', 'orb'), may hold values from -6 to 6
- eigenvalues: float32 [64], P('orb'), may hold values from -1 to -0.25
- cell_scale: float32 [3072], P('dom'), may hold values from 0.4 to 1.6
- base_potential: float32 [3072, 512], P('dom'), may hold values from 0.5 to 1.5
- stiffness: bfloat16 [512, 512], replicated, may hold values from -1.5 to 1.5, as said below
- face_perm: int32 [3072, 64], P('dom'), may hold values from 0 to 63, each once within a row
- restrict: bfloat16 [512, 64], replicated, may hold values from -0.25 to 0.25
- prolong: bfloat16 [64, 512], replicated, may hold values from -0.75 to 0.75
- owner: int32 [3072, 1], P('dom'), may hold values from 0 to 63; in each aligned block of 48 rows (0 to 47, 48 to 95, ...) at most 2 rows name the same one
- pot_slot: int32 [3072], P('dom'), may hold values from 0 to 63
- potential: float32 [4096, 64], P('dom'), may hold values from -6 to 6
Outputs:
- adjoint: bfloat16 [3072, 64, 512], P('dom', 'orb')
- updated: float32 [4096, 64], P('dom')
- applied: bfloat16 [3072, 64, 512], P('dom', 'orb')
The draws below stay inside these ranges and needn't reach their ends.
Inputs may be any that keep to these rules, and one draw needn't show every extreme that they name: In the rows of one device no owner is named by more than 2 cells. `face_perm`: each row is a permutation. `stiffness`: symmetric.
All inputs are finite; a program needn't handle non-finite values.
Results may differ from the reference program's by a relative error of at most 0.0027.
Values sent between devices are 32-bit elements; how exact they have to be, the bound alone decides.
No kernel may reach another device: no remote copies, remote signals or barrier semaphores. Data moves between devices by JAX's collectives and lax.ppermute only.
A program may use at most 64 MiB of HBM per device.

```python
import math
import jax
import jax.numpy as jnp
import numpy as np
from jax import lax

P_SIZE = 512
FACE = 64
PN = 64
ORB = 64
CELL_DEV = 48
CELLS = 3072
POT_DEV = 64
POT_CELLS = 4096
CAP = 2
ITERS = 4
N_DOM = 64


def draw_stiffness(key, part):
    key_diag, key_noise = jax.random.split(jax.random.fold_in(key, 11))
    diagonal = jax.random.uniform(key_diag, (P_SIZE,), jnp.float32, 0.8, 1.2)
    noise = jax.random.normal(key_noise, (P_SIZE, P_SIZE), jnp.float32) * (0.25 / P_SIZE ** 0.5)
    symmetric = (noise + noise.T) * 0.5 ** 0.5
    return (symmetric + jnp.diag(diagonal)).astype(jnp.bfloat16)


def plant(values, own_key, least, top_value):
    dims = values.shape
    spot = [jax.random.randint(jax.random.fold_in(own_key, axis), (), 0, dims[axis]) for axis in range(len(dims))]
    values = values.at[tuple(spot)].set(least)
    longest = dims.index(max(dims))
    spot[longest] = (spot[longest] + 1) % dims[longest]
    return values.at[tuple(spot)].set(top_value)


def block_levels(own_key, shape, cuts, smallest, top_value):
    def one(axis_at, blocks):
        heights = jax.random.uniform(jax.random.fold_in(jax.random.fold_in(own_key, 6), axis_at), (blocks,), jnp.float32, smallest / len(cuts), top_value / len(cuts))
        return jnp.repeat(jnp.exp(heights), shape[axis_at] // blocks).reshape((-1,) + (1,) * (len(shape) - axis_at - 1))

    factor_of = one(*cuts[0])
    for cut in cuts[1:]:
        factor_of = factor_of * one(*cut)
    return factor_of


def assign_block(own_key, own, number, rows, number_of, top, bound, skew):
    ranking = jax.random.permutation(own_key, number_of)
    packed, common = load_shares(number_of, rows * top, bound, skew, True), load_shares(number_of, rows * top, bound, skew, False)
    places = jnp.arange(number_of)

    def named(tallies, offset_by):
        used = int((tallies > 0).sum())
        fixed = max(1, used // 4)
        passed = fixed + (places - fixed + offset_by * (used - fixed)) % max(1, number_of - fixed)
        return jnp.zeros((number_of,), jnp.int32).at[ranking[jnp.where(places < fixed, places, passed)]].set(jnp.asarray(tallies, jnp.int32))

    tallies = jnp.where(number % 4 == 0, named(packed, number // 4), named(common, number - number // 4 - 1))
    mixed = jax.random.permutation(jax.random.fold_in(own, 3), number_of)
    source_of, receiver = mixed[0:number_of // 2 * 2:2], mixed[1:number_of // 2 * 2:2]
    room = jnp.minimum(tallies[source_of] - 1, bound - tallies[receiver]) // 2
    room = jnp.where((source_of == ranking[0]) | (receiver == ranking[0]) | (tallies[receiver] == 0), 0, jnp.maximum(room, 0))
    passed = jax.random.randint(jax.random.fold_in(own, 4), (number_of // 2,), 0, 1 << 20) % (room + 1)
    tallies = tallies.at[source_of].add(-passed).at[receiver].add(passed)
    members = jnp.searchsorted(jnp.cumsum(tallies), jnp.arange(rows * top), side="right").astype(jnp.int32)
    table = members.reshape(top, rows).T
    table = table[jax.random.permutation(jax.random.fold_in(own, 1), rows)]
    offset_by = jax.random.randint(jax.random.fold_in(own, 2), (rows, 1), 0, top)
    return jnp.take_along_axis(table, (jnp.arange(top)[None, :] + offset_by) % top, axis=1)


def load_shares(number_of, total, bound, slope, full):
    loads = [(1 << 20) // math.isqrt(rank ** slope) + 1 for rank in range(1, number_of + 1)]
    largest = bound if full else min(bound, max(-(-total // number_of), total * loads[0] // sum(loads)))
    least = 1 if total - largest >= number_of - 1 else 0
    holding, spare = [largest] + [least] * (number_of - 1), total - largest - least * (number_of - 1)
    while spare > 0:
        free = [i for i in range(1, number_of) if holding[i] < largest] or [i for i in range(1, number_of) if holding[i] < bound]
        pool, budget = sum([loads[i] for i in free]), spare
        for i in free:
            addition = min(bound - holding[i], max(1, budget * loads[i] // pool), spare)
            holding[i] = holding[i] + addition
            spare = spare - addition
    return np.array(holding)


def normal_values(key, extent, spread, reach, shards=(), kind=jnp.bfloat16):
    loudness = block_levels(key, extent, shards, -0.22, 0.18) if shards else 1.0
    values = jax.random.normal(key, extent, jnp.float32) * spread * loudness
    return jnp.minimum(jnp.maximum(values, -reach), reach).astype(kind)


def setup_inputs(seed: int = 0) -> dict:
    keys = jax.random.split(jax.random.key(seed), 13)
    orbitals = normal_values(keys[0], (CELLS, ORB, P_SIZE), 1.0, 6.0, ((0, 64), (1, 8)))
    adjoint_source = normal_values(keys[1], (CELLS, ORB, P_SIZE), 1.0, 6.0, ((0, 64), (1, 8)))
    eigenvalues = jnp.clip(-1.0 + 0.75 * jax.random.uniform(keys[2], (ORB,), jnp.float32) ** block_levels(keys[2], (ORB,), ((0, 8),), -0.2, 0.2), -1.0, -0.25)
    cell_scale = jnp.clip(jnp.exp(math.log(1.6) - 1.3862944 * jax.random.uniform(keys[3], (CELLS,), jnp.float32) ** block_levels(keys[3], (CELLS,), ((0, 64),), -0.2, 0.2)), 0.4, 1.6)
    base_potential = jnp.clip(0.5 + 1.0 * jax.random.uniform(keys[4], (CELLS, P_SIZE), jnp.float32) ** block_levels(keys[4], (CELLS, P_SIZE), ((0, 64),), -0.2, 0.2), 0.5, 1.5)
    stiffness = draw_stiffness(jax.random.fold_in(keys[12], 71), 0)
    face_perm = jax.vmap(lambda own: jax.random.permutation(own, FACE))(jax.random.split(keys[6], CELLS)).reshape((CELLS, FACE)).astype(jnp.int32)
    restrict = normal_values(keys[7], (P_SIZE, PN), P_SIZE ** -0.5, 0.25)
    prolong = normal_values(keys[8], (PN, P_SIZE), PN ** -0.5, 0.75)
    owner_keys = jax.random.split(jax.random.fold_in(keys[9], 1), CELLS // CELL_DEV)
    owner_turns = jax.random.permutation(jax.random.fold_in(keys[9], 3), CELLS // CELL_DEV)
    owner = jax.vmap(lambda own, number: assign_block(jax.random.fold_in(keys[9], 2), own, number, CELL_DEV, N_DOM, 1, CAP, 2))(owner_keys, owner_turns).reshape((CELLS, 1))
    pot_slot = plant(jax.random.randint(keys[10], (CELLS,), 0, POT_DEV), jax.random.fold_in(keys[10], 1), 0, POT_DEV - 1).astype(jnp.int32)
    potential = normal_values(keys[11], (POT_CELLS, PN), 1.0, 6.0, ((0, 64),), jnp.float32)
    return dict(orbitals=orbitals, adjoint_source=adjoint_source, eigenvalues=eigenvalues, cell_scale=cell_scale, base_potential=base_potential, stiffness=stiffness, face_perm=face_perm, restrict=restrict, prolong=prolong, owner=owner, pot_slot=pot_slot, potential=potential)


relax = 0.25
step_rate = 0.1


def face_onehot(face_perm):
    faces = face_perm.shape[1]
    return (face_perm[:, :, None] == jnp.arange(faces, dtype=jnp.int32)[None, None, :]).astype(jnp.float32)


def assemble(partial_sum, onehot):
    faces = onehot.shape[1]
    nodes = partial_sum.shape[2]
    left_face = partial_sum[:, :, :faces]
    right_face = partial_sum[:, :, nodes - faces:]
    sent_right = jnp.einsum('ckj,cok->coj', onehot, right_face, precision=lax.Precision.HIGHEST)
    zero_face = jnp.zeros_like(left_face[:1])
    left_next = jnp.concatenate([left_face[1:], zero_face], 0)
    add_right = jnp.einsum('ckj,coj->cok', onehot, left_next, precision=lax.Precision.HIGHEST)
    add_left = jnp.concatenate([zero_face, sent_right[:-1]], 0)
    return jnp.concatenate([left_face + add_left, partial_sum[:, :, faces:nodes - faces], right_face + add_right], 2)


def cell_operator(values_bf, values_full, shift, cell_scale, stiffness, onehot):
    nodes = stiffness.shape[0]
    kinetic = jnp.dot(values_bf.reshape(-1, nodes), stiffness, preferred_element_type=jnp.float32).reshape(values_full.shape)
    partial_sum = cell_scale[:, None, None] * kinetic + shift * values_full
    return assemble(partial_sum, onehot)


def reference(orbitals, adjoint_source, eigenvalues, cell_scale, base_potential, stiffness, face_perm, restrict, prolong, owner, pot_slot, potential):
    onehot = face_onehot(face_perm)
    width = min(8, ORB)
    blocks = ORB // width

    def solve_block(index):
        start = (index * width).astype(jnp.int32)
        psi_block = lax.dynamic_slice_in_dim(orbitals, start, width, 1)
        source_block = lax.dynamic_slice_in_dim(adjoint_source, start, width, 1).astype(jnp.float32)
        eig_block = lax.dynamic_slice_in_dim(eigenvalues, start, width, 0)
        shift = base_potential[:, None, :] - eig_block[None, :, None]
        iterate = relax * source_block
        for step_index in range(ITERS):
            image = cell_operator(iterate.astype(jnp.bfloat16), iterate, shift, cell_scale, stiffness, onehot)
            iterate = iterate + relax * (source_block - image)
        product = jnp.sum(psi_block.astype(jnp.float32) * iterate, axis=1)
        return iterate.astype(jnp.bfloat16), product

    adjoint_blocks, products = lax.map(solve_block, jnp.arange(blocks, dtype=jnp.int32))
    adjoint = jnp.transpose(adjoint_blocks, (1, 0, 2, 3)).reshape(CELLS, ORB, P_SIZE)
    density_term = jnp.sum(products, 0)
    projected = jnp.dot(density_term, restrict.astype(jnp.float32), precision=lax.Precision.HIGHEST)
    target = (owner[:, 0] * POT_DEV + pot_slot).astype(jnp.int32)
    summed = jax.ops.segment_sum(projected, target, num_segments=POT_DEV * N_DOM)
    updated = potential - step_rate * summed
    cell_pot = updated[target]
    node_potential = jnp.dot(cell_pot, prolong.astype(jnp.float32), precision=lax.Precision.HIGHEST)
    shift_new = (base_potential + node_potential)[:, None, :]

    def apply_block(index):
        start = (index * width).astype(jnp.int32)
        psi_block = lax.dynamic_slice_in_dim(orbitals, start, width, 1)
        result = cell_operator(psi_block, psi_block.astype(jnp.float32), shift_new, cell_scale, stiffness, onehot)
        return result.astype(jnp.bfloat16)

    applied_blocks = lax.map(apply_block, jnp.arange(blocks, dtype=jnp.int32))
    applied = jnp.transpose(applied_blocks, (1, 0, 2, 3)).reshape(CELLS, ORB, P_SIZE)
    return adjoint, updated, applied
```

```python
import jax
import jax.numpy as jnp
import numpy as np
from jax import lax
from jax.experimental import pallas as pl
from jax.experimental.pallas import tpu as pltpu
from jax.sharding import PartitionSpec as P

ITERS = 4
relax = 0.25
step_rate = 0.1

LANES = 128
HALF = 64
NODES = 512
WIDTH = 8
CELLS = 48
HALO = 4
EXT = CELLS + 2 * HALO
F32, BF16 = jnp.float32, jnp.bfloat16


def dot(a, b, contract=((1,), (0,))):
    return lax.dot_general(a, b, (contract, ((), ())), preferred_element_type=F32)


def split(a):
    high = a.astype(BF16)
    return high, (a - high.astype(F32)).astype(BF16)


def lane_below(bound):
    return lax.broadcasted_iota(jnp.int32, (WIDTH, LANES), 1) < bound


SRC_ROWS, ORB_AT, BASE_AT, META_AT, HALO_ROWS = 32, 32, 40, 44, 48
IDX, SCALE, TARGET = slice(0, 128), slice(128, 256), slice(256, 384)


def solve_kernel(edge, src, orb, base, meta, left, right, eig, stiff, restrict_t, group,
                 adjoint_out, projected_out, x, quarter, xb, kin, shifted, factor, index):
    own = slice(HALO * WIDTH, (HALO + CELLS) * WIDTH)
    first, last = slice(0, HALO * WIDTH), slice((HALO + CELLS) * WIDTH, EXT * WIDTH)
    quarter[own] = relax * src[...].astype(F32)
    quarter[first] = relax * left[0:SRC_ROWS]
    quarter[last] = relax * right[0:SRC_ROWS]
    x[...] = quarter[...]
    eig_column = eig[...]
    for e in range(EXT):
        if e < HALO:
            base_row, meta_row = left[BASE_AT + e : BASE_AT + e + 1], left[META_AT + e : META_AT + e + 1]
        elif e < HALO + CELLS:
            base_row, meta_row = base[e - HALO : e - HALO + 1], meta[e - HALO : e - HALO + 1]
        else:
            at = e - HALO - CELLS
            base_row, meta_row = right[BASE_AT + at : BASE_AT + at + 1], right[META_AT + at : META_AT + at + 1]
        rows = slice(e * WIDTH, (e + 1) * WIDTH)
        shifted[rows] = base_row - eig_column
        factor[rows] = jnp.broadcast_to(meta_row[:, SCALE], (WIDTH, LANES))
        index[rows] = jnp.broadcast_to(meta_row[:, IDX].astype(jnp.int32), (WIDTH, LANES))
    low = lane_below(HALF)
    open_left, open_right = edge[0].astype(F32), edge[1].astype(F32)

    def step(_, carry):
        xb[...] = x[...].astype(BF16)
        kin[...] = dot(xb[...], stiff[...])
        part_before = new_before = None
        for e in range(EXT):
            rows = slice(e * WIDTH, (e + 1) * WIDTH)
            scale = factor[rows]
            parts, news = [], []
            for t in range(4):
                cols = slice(t * LANES, (t + 1) * LANES)
                here = x[rows, cols]
                part = scale * kin[rows, cols] + shifted[rows, cols] * here
                parts.append(part)
                news.append(here + quarter[rows, cols] - relax * part)
            if e > 0:
                crossing = jnp.where(low, parts[0], part_before)
                moved = relax * jnp.take_along_axis(
                    crossing, index[(e - 1) * WIDTH : e * WIDTH], axis=1, mode="promise_in_bounds"
                )
                if e == HALO:
                    moved = moved * open_left
                if e == HALO + CELLS:
                    moved = moved * open_right
                news[0] = jnp.where(low, news[0] - moved, news[0])
                x[(e - 1) * WIDTH : e * WIDTH, 3 * LANES :] = jnp.where(low, new_before, new_before - moved)
            for t in range(3):
                x[rows, t * LANES : (t + 1) * LANES] = news[t]
            part_before, new_before = parts[3], news[3]
        x[(EXT - 1) * WIDTH :, 3 * LANES :] = new_before
        return carry

    lax.fori_loop(0, ITERS, step, 0)
    mine = x[own]
    adjoint_out[...] = mine.astype(BF16)
    high, rest = split(orb[...].astype(F32) * mine)
    density = dot(group[...], high) + dot(group[...], rest)
    high, rest = split(density)
    nt = ((1,), (1,))
    projected_out[...] = dot(restrict_t[...], high, nt) + dot(restrict_t[...], rest, nt)


def sum_kernel(gathered, wanted, unpack, out):
    sources = gathered.shape[0] // WIDTH
    values = gathered[...]
    high, rest = split(values)
    ids = dot(high, unpack[...])
    row = lax.broadcasted_iota(jnp.int32, ids.shape, 0) % WIDTH
    lane = lax.broadcasted_iota(jnp.int32, ids.shape, 1)
    ids = jnp.where(lane // 6 == row, ids, 0.0)
    ids = jnp.sum(ids.reshape(sources, WIDTH, LANES), axis=1)
    lane = lax.broadcasted_iota(jnp.int32, ids.shape, 1)
    source = lax.broadcasted_iota(jnp.int32, ids.shape, 0)
    known = (source * HALF + lane - CELLS).astype(F32)
    ids = jnp.where(lane < CELLS, ids, jnp.where(lane < CELLS + HALF, known, -1.0))
    asked = jnp.broadcast_to(wanted[...], (LANES, LANES))
    total = jnp.zeros((2 * WIDTH, LANES), F32)
    for s in range(0, sources, 2):
        hot = [jnp.where(asked == ids[i : i + 1], 1.0, 0.0).astype(BF16) for i in (s, s + 1)]
        both = [
            jnp.concatenate([high[i * WIDTH : (i + 1) * WIDTH], rest[i * WIDTH : (i + 1) * WIDTH]], 0)
            for i in (s, s + 1)
        ]
        total = total + dot(jnp.concatenate(both, 1), jnp.concatenate(hot, 1), ((1,), (1,)))
    result = total[:WIDTH] + total[WIDTH:]
    for r in range(out.shape[0] // WIDTH):
        out[r * WIDTH : (r + 1) * WIDTH] = result


def apply_kernel(edge, columns, orb, base, meta, left, right, stiff, prolong, updated_out, applied_out, ob, kin):
    table = jnp.transpose(columns[...])
    updated_out[...] = table[0:HALF]
    high, rest = split(table[HALF:])
    node = dot(high, prolong[...]) + dot(rest, prolong[...])
    ob[0:16] = jnp.concatenate([left[ORB_AT : ORB_AT + WIDTH], right[ORB_AT : ORB_AT + WIDTH]], 0).astype(BF16)
    ob[16:] = orb[...]
    kin[...] = dot(ob[...], stiff[...])
    low = lane_below(HALF)
    open_left, open_right = edge[0].astype(F32), edge[1].astype(F32)
    part_before = new_before = index_before = None
    finished = []
    for e in range(CELLS + 2):
        if e == 0:
            values, base_row = left[ORB_AT : ORB_AT + WIDTH], left[BASE_AT + HALO - 1 : BASE_AT + HALO]
            meta_row = left[META_AT + HALO - 1 : META_AT + HALO]
            node_row, kin_rows = node[CELLS : CELLS + 1], slice(0, WIDTH)
        elif e <= CELLS:
            c = e - 1
            values = orb[c // 2 * 16 : c // 2 * 16 + 16].astype(F32)[c % 2 * WIDTH : (c % 2 + 1) * WIDTH]
            base_row, meta_row, node_row = base[c : c + 1], meta[c : c + 1], node[c : c + 1]
            kin_rows = slice(16 + c * WIDTH, 16 + (c + 1) * WIDTH)
        else:
            values, base_row = right[ORB_AT : ORB_AT + WIDTH], right[BASE_AT : BASE_AT + 1]
            meta_row = right[META_AT : META_AT + 1]
            node_row, kin_rows = node[CELLS + 1 : CELLS + 2], slice(WIDTH, 2 * WIDTH)
        shift = base_row + node_row
        scale = jnp.broadcast_to(meta_row[:, SCALE], (WIDTH, LANES))
        parts = [
            scale * kin[kin_rows, t * LANES : (t + 1) * LANES]
            + shift[:, t * LANES : (t + 1) * LANES] * values[:, t * LANES : (t + 1) * LANES]
            for t in range(4)
        ]
        if e > 0:
            crossing = jnp.where(low, parts[0], part_before)
            moved = jnp.take_along_axis(crossing, index_before, axis=1, mode="promise_in_bounds")
            if e == 1:
                moved = moved * open_left
            if e == CELLS + 1:
                moved = moved * open_right
            done = jnp.where(low, new_before[3], new_before[3] + moved)
            if e > 1:
                finished.append(jnp.concatenate([*new_before[:3], done], 1))
            news = [jnp.where(low, parts[0] + moved, parts[0]), *parts[1:]]
        else:
            news = parts
        part_before, new_before = parts[3], news
        index_before = jnp.broadcast_to(meta_row[:, IDX].astype(jnp.int32), (WIDTH, LANES))
        if len(finished) == 2:
            c = e - 3
            applied_out[c * WIDTH : (c + 2) * WIDTH] = jnp.concatenate(finished, 0).astype(BF16)
            finished = []


def unpack_table():
    table = np.zeros((LANES, LANES), np.float32)
    for k in range(CELLS):
        table[112 + k % 6, k] = 64.0
        table[118 + k % 6, k] = 1.0
    return table


def group_table():
    table = np.zeros((LANES, CELLS * WIDTH), np.float32)
    for row in range(CELLS * WIDTH):
        table[row // WIDTH, row] = 1.0
    return table


def local(orbitals, adjoint_source, eigenvalues, cell_scale, base_potential, stiffness, face_perm, restrict,
          prolong, owner, pot_slot, potential):
    n_dom, n_orb = lax.axis_size("dom"), lax.axis_size("orb")
    dom, orb_at = lax.axis_index("dom"), lax.axis_index("orb")
    vmem = pl.BlockSpec(memory_space=pltpu.VMEM)
    smem = pl.BlockSpec(memory_space=pltpu.SMEM)

    orb2 = orbitals.reshape(CELLS * WIDTH, NODES)
    src2 = adjoint_source.reshape(CELLS * WIDTH, NODES)
    target = owner[:, 0] * HALF + pot_slot
    faces = jnp.arange(HALF, dtype=jnp.int32)
    inverse = jnp.sum(jnp.where(face_perm[:, :, None] == faces[None, None, :], faces[None, :, None], 0), axis=1)
    meta = jnp.concatenate(
        [
            (HALF + inverse).astype(F32),
            face_perm.astype(F32),
            jnp.broadcast_to(cell_scale[:, None], (CELLS, LANES)),
            jnp.broadcast_to(target.astype(F32)[:, None], (CELLS, 2 * LANES)),
        ],
        1,
    )

    def packed(cells, orb_cell):
        rows = slice(cells.start * WIDTH, cells.stop * WIDTH)
        return jnp.concatenate(
            [
                src2[rows].astype(F32),
                orb2[orb_cell * WIDTH : (orb_cell + 1) * WIDTH].astype(F32),
                base_potential[cells],
                meta[cells],
            ],
            0,
        )

    ahead = [(i, i + 1) for i in range(n_dom - 1)]
    left = lax.ppermute(packed(slice(CELLS - HALO, CELLS), CELLS - 1), "dom", ahead)
    right = lax.ppermute(packed(slice(0, HALO), 0), "dom", [(b, a) for a, b in ahead])

    edge = jnp.stack([dom > 0, dom < n_dom - 1]).astype(jnp.int32)
    pot_columns = lax.dynamic_slice_in_dim(potential, orb_at * WIDTH, WIDTH, 1).T
    static = jnp.concatenate(
        [
            jnp.zeros((WIDTH, CELLS), F32),
            pot_columns,
            owner.reshape(WIDTH, 6).astype(F32),
            pot_slot.reshape(WIDTH, 6).astype(F32),
            jnp.zeros((WIDTH, 4), F32),
        ],
        1,
    )
    group = jnp.asarray(group_table(), BF16)
    unpack = jnp.asarray(unpack_table(), BF16)
    rows = EXT * WIDTH
    adjoint2, projected = pl.pallas_call(
        solve_kernel,
        out_shape=(
            jax.ShapeDtypeStruct((CELLS * WIDTH, NODES), BF16),
            jax.ShapeDtypeStruct((HALF, LANES), F32),
        ),
        in_specs=[smem] + [vmem] * 10,
        out_specs=(vmem, vmem),
        scratch_shapes=[
            pltpu.VMEM((rows, NODES), F32),
            pltpu.VMEM((rows, NODES), F32),
            pltpu.VMEM((rows, NODES), BF16),
            pltpu.VMEM((rows, NODES), F32),
            pltpu.VMEM((rows, NODES), F32),
            pltpu.VMEM((rows, LANES), F32),
            pltpu.VMEM((rows, LANES), jnp.int32),
        ],
        compiler_params=pltpu.CompilerParams(vmem_limit_bytes=32 * 2**20),
    )(edge, src2, orb2, base_potential, meta, left, right, eigenvalues[:, None], stiffness, restrict.T, group)

    mine = lax.all_to_all(projected.reshape(n_orb, WIDTH, LANES), "orb", split_axis=0, concat_axis=0, tiled=True)
    payload = static - step_rate * jnp.sum(mine, axis=0)
    gathered = lax.all_to_all(
        jnp.broadcast_to(payload[None], (n_dom, WIDTH, LANES)), "dom", split_axis=0, concat_axis=0, tiled=True
    )
    halo_ids = jnp.stack([left[META_AT + HALO - 1, 256], right[META_AT, 256]])
    wanted = jnp.concatenate(
        [
            (dom * HALF + faces).astype(F32),
            target.astype(F32),
            halo_ids,
            jnp.full((LANES - HALF - CELLS - 2,), -2.0, F32),
        ]
    )[:, None]
    columns = pl.pallas_call(
        sum_kernel,
        out_shape=jax.ShapeDtypeStruct((n_orb * WIDTH, LANES), F32),
        in_specs=[vmem] * 3,
        out_specs=vmem,
        compiler_params=pltpu.CompilerParams(vmem_limit_bytes=32 * 2**20),
    )(gathered.reshape(n_dom * WIDTH, LANES), wanted, unpack)
    columns = lax.all_to_all(columns.reshape(n_orb, WIDTH, LANES), "orb", split_axis=0, concat_axis=0, tiled=True)
    updated, applied2 = pl.pallas_call(
        apply_kernel,
        out_shape=(
            jax.ShapeDtypeStruct((HALF, HALF), F32),
            jax.ShapeDtypeStruct((CELLS * WIDTH, NODES), BF16),
        ),
        in_specs=[smem] + [vmem] * 8,
        out_specs=(vmem, vmem),
        scratch_shapes=[
            pltpu.VMEM(((CELLS + 2) * WIDTH, NODES), BF16),
            pltpu.VMEM(((CELLS + 2) * WIDTH, NODES), F32),
        ],
        compiler_params=pltpu.CompilerParams(vmem_limit_bytes=32 * 2**20),
    )(edge, columns.reshape(n_orb * WIDTH, LANES), orb2, base_potential, meta, left, right, stiffness, prolong)
    return adjoint2.reshape(orbitals.shape), updated, applied2.reshape(orbitals.shape)


def solution(mesh):
    in_specs = (
        P("dom", "orb", None),
        P("dom", "orb", None),
        P("orb"),
        P("dom"),
        P("dom", None),
        P(),
        P("dom", None),
        P(),
        P(),
        P("dom", None),
        P("dom"),
        P("dom", None),
    )
    out_specs = (P("dom", "orb", None), P("dom", None), P("dom", "orb", None))
    return jax.shard_map(local, mesh=mesh, in_specs=in_specs, out_specs=out_specs, check_vma=False)
```

```python
import jax
import jax.numpy as jnp
import numpy as np
from jax import lax
from jax.experimental import pallas as pl
from jax.experimental.pallas import tpu as pltpu
from jax.sharding import PartitionSpec as P

ITERS = 4
relax = 0.25
step_rate = 0.1

LANES = 128
HALF = 64
NODES = 512
WIDTH = 8
CELLS = 48
HALO = 4
EXT = CELLS + 2 * HALO
F32, BF16 = jnp.float32, jnp.bfloat16


def dot(a, b, contract=((1,), (0,))):
    return lax.dot_general(a, b, (contract, ((), ())), preferred_element_type=F32)


def split(a):
    high = a.astype(BF16)
    return high, (a - high.astype(F32)).astype(BF16)


def lane_below(bound):
    return lax.broadcasted_iota(jnp.int32, (WIDTH, LANES), 1) < bound


SRC_ROWS, ORB_AT, BASE_AT, META_AT, HALO_ROWS = 32, 32, 40, 44, 48
IDX, SCALE, TARGET = slice(0, 128), slice(128, 256), slice(256, 512)
STRIP = 3 * HALO
NT = ((1,), (1,))


def tile(e):
    return slice(e * WIDTH, (e + 1) * WIDTH)


def cols(t):
    return slice(t * LANES, (t + 1) * LANES)


def face_rows(perm, wanted_cells):
    twice = jnp.concatenate([perm, perm], 1).astype(F32)
    columns = jnp.transpose(twice)[0:HALF]
    node = lax.broadcasted_iota(jnp.int32, (HALF, LANES), 0).astype(F32)
    lane = lax.broadcasted_iota(jnp.int32, (HALF, LANES), 1).astype(F32)
    low = lax.broadcasted_iota(jnp.int32, (1, LANES), 1) < HALF
    rows = []
    for c in wanted_cells:
        inverse = jnp.sum(jnp.where(columns[:, c : c + 1] == lane, node, 0.0), axis=0, keepdims=True)
        rows.append(jnp.where(low, inverse + HALF, twice[c : c + 1]))
    return rows


def pack_kernel(scale, owner, slot, src_low, src_high, orb_low, orb_high, base_low, base_high, perm_low, perm_high,
                to_left, to_right):
    def put(out, src, orb, base, perm, first, orb_at, edge_cell):
        inner = 0 if first == 0 else WIDTH - HALO
        out[0:SRC_ROWS] = src[...].astype(F32)
        out[ORB_AT : ORB_AT + WIDTH] = orb[...].astype(F32)[tile(orb_at)]
        out[BASE_AT : BASE_AT + HALO] = base[inner : inner + HALO]
        faces = face_rows(perm[...], range(inner, inner + HALO))
        target = (owner[edge_cell] * HALF + slot[edge_cell]).astype(F32)
        for i in range(HALO):
            at = slice(META_AT + i, META_AT + i + 1)
            out[at, IDX] = faces[i]
            out[at, SCALE] = jnp.full((1, LANES), scale[first + i], F32)
            out[at, TARGET] = jnp.full((1, 2 * LANES), target, F32)

    put(to_left, src_low, orb_low, base_low, perm_low, 0, 0, 0)
    put(to_right, src_high, orb_high, base_high, perm_high, CELLS - HALO, 1, CELLS - 1)


def relaxed(strips, x, quarter, shifted, xb, kin, stiff, factor, index, gates):
    low = lane_below(HALF)
    cells = strips[-1][-1] + 1

    def step(_, carry):
        xb[...] = x[...].astype(BF16)
        kin[...] = dot(xb[...], stiff[...])
        for strip in strips:
            part_before = new_before = None
            for e in strip:
                rows = tile(e)
                scale = factor(e)
                parts, news = [], []
                for t in range(4):
                    here = x[rows, cols(t)]
                    part = scale * kin[rows, cols(t)] + shifted[rows, cols(t)] * here
                    parts.append(part)
                    news.append(here + quarter[rows, cols(t)] - relax * part)
                if e > strip[0]:
                    crossing = jnp.where(low, parts[0], part_before)
                    moved = relax * jnp.take_along_axis(crossing, index[tile(e - 1)], axis=1, mode="promise_in_bounds")
                    if e in gates:
                        moved = moved * gates[e]
                    news[0] = jnp.where(low, news[0] - moved, news[0])
                    x[tile(e - 1), cols(3)] = jnp.where(low, new_before, new_before - moved)
                for t in range(3):
                    x[rows, cols(t)] = news[t]
                part_before, new_before = parts[3], news[3]
            x[tile(strip[-1]), cols(3)] = new_before
        return carry

    lax.fori_loop(0, ITERS, step, 0)


def projection(orb_values, x_values, group, restrict_t):
    high, rest = split(orb_values.astype(F32) * x_values)
    density = dot(group, high) + dot(group, rest)
    high, rest = split(density)
    return dot(restrict_t, high, NT) + dot(restrict_t, rest, NT)


def interior_kernel(place, scale, owner, slot, src, orb, base, perm, eig, stiff, restrict_t, group, potential,
                    adjoint_out, projected_out, linear_out, index_out, static_out,
                    x, quarter, xb, kin, shifted, turned):
    quarter[...] = relax * src[...].astype(F32)
    x[...] = quarter[...]
    eig_column = eig[...]
    faces = face_rows(perm[...], range(CELLS))
    for c in range(CELLS):
        shifted[tile(c)] = base[c : c + 1] - eig_column
        index_out[tile(c)] = jnp.broadcast_to(faces[c].astype(jnp.int32), (WIDTH, LANES))
    relaxed([range(CELLS)], x, quarter, shifted, xb, kin, stiff, lambda c: scale[c], index_out, {})
    inner = slice(HALO * WIDTH, (CELLS - HALO) * WIDTH)
    adjoint_out[...] = x[inner].astype(BF16)
    projected_out[...] = projection(orb[inner], x[inner], group[...], restrict_t[...])
    kin[...] = dot(orb[...], stiff[...])
    for pair in range(CELLS // 2):
        values = orb[pair * 16 : pair * 16 + 16].astype(F32)
        for c in (2 * pair, 2 * pair + 1):
            linear_out[tile(c)] = scale[c] * kin[tile(c)] + base[c : c + 1] * values[tile(c % 2)]
    turned[...] = jnp.transpose(potential[...])
    columns = turned[pl.ds(pl.multiple_of(place[1] * WIDTH, WIDTH), WIDTH)]
    row = lax.broadcasted_iota(jnp.int32, (WIDTH, LANES), 0)
    lane = lax.broadcasted_iota(jnp.int32, (WIDTH, LANES), 1)
    at = jnp.where(lane >= CELLS + HALF, row * 12 + lane - CELLS - HALF, -1)
    at = jnp.where(lane < CELLS + HALF + 12, at, -1)
    static = jnp.concatenate([jnp.zeros((WIDTH, CELLS), F32), columns, jnp.zeros((WIDTH, 16), F32)], 1)
    for c in range(CELLS):
        static = jnp.where(at == c // 6 * 12 + c % 6, owner[c].astype(F32), static)
        static = jnp.where(at == c // 6 * 12 + 6 + c % 6, slot[c].astype(F32), static)
    static_out[...] = static


def boundary_kernel(place, scale, src, orb, base, index_own, left, right, eig, stiff, restrict_t, group, adjoint_mid,
                    projected_mid, adjoint_out, projected_out, ghost_out,
                    x, quarter, xb, kin, shifted, factor, index, ob):
    near, edge = 2 * HALO * WIDTH, HALO * WIDTH
    last = CELLS * WIDTH
    quarter[0:edge] = relax * left[0:SRC_ROWS]
    quarter[edge : edge + near] = relax * src[0:near].astype(F32)
    quarter[edge + near : edge + 2 * near] = relax * src[last - near :].astype(F32)
    quarter[edge + 2 * near :] = relax * right[0:SRC_ROWS]
    x[...] = quarter[...]
    eig_column = eig[...]
    for e in range(2 * STRIP):
        ghost = left if e < HALO else right if e >= 2 * STRIP - HALO else None
        if ghost is None:
            c = e - HALO if e < STRIP else CELLS - 2 * HALO + e - STRIP
            base_row = base[c : c + 1]
            factor[tile(e)] = jnp.full((WIDTH, LANES), scale[c], F32)
            index[tile(e)] = index_own[tile(c)]
        else:
            i = e if e < HALO else e - 2 * STRIP + HALO
            base_row = ghost[BASE_AT + i : BASE_AT + i + 1]
            meta_row = ghost[META_AT + i : META_AT + i + 1]
            factor[tile(e)] = jnp.broadcast_to(meta_row[:, SCALE], (WIDTH, LANES))
            index[tile(e)] = jnp.broadcast_to(meta_row[:, IDX].astype(jnp.int32), (WIDTH, LANES))
        shifted[tile(e)] = base_row - eig_column
    gates = {
        HALO: jnp.where(place[0] > 0, 1.0, 0.0),
        2 * STRIP - HALO: jnp.where(place[0] < place[2] - 1, 1.0, 0.0),
    }
    relaxed([range(STRIP), range(STRIP, 2 * STRIP)], x, quarter, shifted, xb, kin, stiff,
            lambda e: factor[tile(e)], index, gates)
    low_cells, high_cells = x[edge : 2 * edge], x[4 * edge : 5 * edge]
    adjoint_out[0:edge] = low_cells.astype(BF16)
    adjoint_out[edge : last - edge] = adjoint_mid[...]
    adjoint_out[last - edge :] = high_cells.astype(BF16)
    own_orb = jnp.concatenate([orb[0:edge], orb[last - edge :]], 0)
    own_x = jnp.concatenate([low_cells, high_cells], 0)
    projected_out[...] = projected_mid[...] + projection(own_orb, own_x, group[...], restrict_t[...])
    ghosts = jnp.concatenate([left[ORB_AT : ORB_AT + WIDTH], right[ORB_AT : ORB_AT + WIDTH]], 0)
    ob[...] = ghosts.astype(BF16)
    ghost_kin = dot(ob[...], stiff[...])
    for i, e, base_row in (
        (0, HALO - 1, left[BASE_AT + HALO - 1 : BASE_AT + HALO]),
        (1, 2 * STRIP - HALO, right[BASE_AT : BASE_AT + 1]),
    ):
        for t in range(4):
            ghost_out[tile(i), cols(t)] = (
                factor[tile(e)] * ghost_kin[tile(i), cols(t)] + base_row[:, cols(t)] * ghosts[tile(i), cols(t)]
            )


def sum_kernel(place, owner, slot, gathered, left, right, unpack, out, asked):
    sources = gathered.shape[0] // WIDTH
    own = lax.broadcasted_iota(jnp.int32, (HALF, LANES), 0) + place[0] * HALF
    asked[0:HALF] = own.astype(F32)
    for c in range(CELLS):
        asked[HALF + c : HALF + c + 1] = jnp.full((1, LANES), (owner[c] * HALF + slot[c]).astype(F32), F32)
    asked[HALF + CELLS : HALF + CELLS + 1] = left[META_AT + HALO - 1 : META_AT + HALO, 256:384]
    asked[HALF + CELLS + 1 : HALF + CELLS + 2] = right[META_AT : META_AT + 1, 256:384]
    asked[HALF + CELLS + 2 :] = jnp.full((LANES - HALF - CELLS - 2, LANES), -2.0, F32)
    values = gathered[...]
    high, rest = split(values)
    ids = dot(high, unpack[...])
    row = lax.broadcasted_iota(jnp.int32, ids.shape, 0) % WIDTH
    lane = lax.broadcasted_iota(jnp.int32, ids.shape, 1)
    ids = jnp.where(lane // 6 == row, ids, 0.0)
    ids = jnp.sum(ids.reshape(sources, WIDTH, LANES), axis=1)
    lane = lax.broadcasted_iota(jnp.int32, ids.shape, 1)
    source = lax.broadcasted_iota(jnp.int32, ids.shape, 0)
    known = (source * HALF + lane - CELLS).astype(F32)
    ids = jnp.where(lane < CELLS, ids, jnp.where(lane < CELLS + HALF, known, -1.0))
    wanted = asked[...]
    total = jnp.zeros((2 * WIDTH, LANES), F32)
    for s in range(0, sources, 2):
        hot = [jnp.where(wanted == ids[i : i + 1], 1.0, 0.0).astype(BF16) for i in (s, s + 1)]
        both = [jnp.concatenate([high[tile(i)], rest[tile(i)]], 0) for i in (s, s + 1)]
        total = total + dot(jnp.concatenate(both, 1), jnp.concatenate(hot, 1), NT)
    result = total[:WIDTH] + total[WIDTH:]
    for r in range(out.shape[0] // WIDTH):
        out[tile(r)] = result


def apply_kernel(place, columns, orb, linear, ghost, left, right, index, prolong, updated_out, applied_out):
    table = jnp.transpose(columns[...])
    updated_out[...] = table[0:HALF]
    high, rest = split(table[HALF:])
    node = dot(high, prolong[...]) + dot(rest, prolong[...])
    low = lane_below(HALF)
    part_before = new_before = index_before = None
    finished = []
    for e in range(CELLS + 2):
        c = e - 1
        if e == 0:
            values, start, node_at = left[ORB_AT : ORB_AT + WIDTH], ghost[tile(0)], CELLS
        elif e <= CELLS:
            values = orb[c // 2 * 16 : c // 2 * 16 + 16].astype(F32)[tile(c % 2)]
            start, node_at = linear[tile(c)], c
        else:
            values, start, node_at = right[ORB_AT : ORB_AT + WIDTH], ghost[tile(1)], CELLS + 1
        whole = start + node[node_at : node_at + 1] * values
        parts = [whole[:, cols(t)] for t in range(4)]
        if e > 0:
            crossing = jnp.where(low, parts[0], part_before)
            moved = jnp.take_along_axis(crossing, index_before, axis=1, mode="promise_in_bounds")
            if e == 1:
                moved = moved * jnp.where(place[0] > 0, 1.0, 0.0)
            if e == CELLS + 1:
                moved = moved * jnp.where(place[0] < place[2] - 1, 1.0, 0.0)
            done = jnp.where(low, new_before[3], new_before[3] + moved)
            if e > 1:
                finished.append(jnp.concatenate([*new_before[:3], done], 1))
            news = [jnp.where(low, parts[0] + moved, parts[0]), *parts[1:]]
        else:
            news = parts
        part_before, new_before = parts[3], news
        if e == 0:
            meta_row = left[META_AT + HALO - 1 : META_AT + HALO]
            index_before = jnp.broadcast_to(meta_row[:, IDX].astype(jnp.int32), (WIDTH, LANES))
        elif e <= CELLS:
            index_before = index[tile(c)]
        if len(finished) == 2:
            applied_out[(e - 3) * WIDTH : (e - 1) * WIDTH] = jnp.concatenate(finished, 0).astype(BF16)
            finished = []


def unpack_table():
    table = np.zeros((LANES, LANES), np.float32)
    for k in range(CELLS):
        table[112 + k % 6, k] = 64.0
        table[118 + k % 6, k] = 1.0
    return table


def group_table(cells):
    table = np.zeros((LANES, len(cells) * WIDTH), np.float32)
    for at, cell in enumerate(cells):
        table[cell, at * WIDTH : (at + 1) * WIDTH] = 1.0
    return table


def local(orbitals, adjoint_source, eigenvalues, cell_scale, base_potential, stiffness, face_perm, restrict,
          prolong, owner, pot_slot, potential):
    n_dom, n_orb = lax.axis_size("dom"), lax.axis_size("orb")
    dom, orb_at = lax.axis_index("dom"), lax.axis_index("orb")
    vmem = pl.BlockSpec(memory_space=pltpu.VMEM)
    smem = pl.BlockSpec(memory_space=pltpu.SMEM)
    params = pltpu.CompilerParams(vmem_limit_bytes=32 * 2**20)
    struct = jax.ShapeDtypeStruct

    orb2 = orbitals.reshape(CELLS * WIDTH, NODES)
    src2 = adjoint_source.reshape(CELLS * WIDTH, NODES)
    owner1 = owner.reshape(CELLS)
    place = jnp.stack([dom, orb_at, jnp.int32(n_dom)])

    def ends(shape, blocks):
        return [pl.BlockSpec(shape, lambda i: (0, 0)), pl.BlockSpec(shape, lambda i: (blocks - 1, 0))]

    whole = pl.BlockSpec((HALO_ROWS, NODES), lambda i: (0, 0))
    to_left, to_right = pl.pallas_call(
        pack_kernel,
        grid=(1,),
        out_shape=(struct((HALO_ROWS, NODES), F32),) * 2,
        in_specs=[smem] * 3
        + ends((SRC_ROWS, NODES), CELLS // HALO)
        + ends((16, NODES), CELLS // 2)
        + ends((WIDTH, NODES), CELLS // WIDTH)
        + ends((WIDTH, HALF), CELLS // WIDTH),
        out_specs=(whole, whole),
        compiler_params=params,
    )(cell_scale, owner1, pot_slot, src2, src2, orb2, orb2, base_potential, base_potential, face_perm, face_perm)

    ahead = [(i, i + 1) for i in range(n_dom - 1)]
    left = lax.ppermute(to_right, "dom", ahead)
    right = lax.ppermute(to_left, "dom", [(b, a) for a, b in ahead])

    eig = eigenvalues[:, None]
    restrict_t = restrict.T
    rows = CELLS * WIDTH
    inner = rows - 2 * HALO * WIDTH

    def scratch(n):
        return [
            pltpu.VMEM((n, NODES), F32),
            pltpu.VMEM((n, NODES), F32),
            pltpu.VMEM((n, NODES), BF16),
            pltpu.VMEM((n, NODES), F32),
            pltpu.VMEM((n, NODES), F32),
        ]

    adjoint_mid, projected_mid, linear, index, static = pl.pallas_call(
        interior_kernel,
        out_shape=(
            struct((inner, NODES), BF16),
            struct((HALF, LANES), F32),
            struct((rows, NODES), F32),
            struct((rows, LANES), jnp.int32),
            struct((WIDTH, LANES), F32),
        ),
        in_specs=[smem] * 4 + [vmem] * 9,
        out_specs=(vmem,) * 5,
        scratch_shapes=scratch(rows) + [pltpu.VMEM((HALF, HALF), F32)],
        compiler_params=params,
        cost_estimate=pl.CostEstimate(flops=5 * 2 * rows * NODES * NODES, bytes_accessed=4 * 2**20, transcendentals=0),
    )(place, cell_scale, owner1, pot_slot, src2, orb2, base_potential, face_perm, eig, stiffness, restrict_t,
      jnp.asarray(group_table(range(HALO, CELLS - HALO)), BF16), potential)

    edge_cells = [*range(HALO), *range(CELLS - HALO, CELLS)]
    strip_rows = 2 * STRIP * WIDTH
    adjoint2, projected, ghost = pl.pallas_call(
        boundary_kernel,
        out_shape=(
            struct((rows, NODES), BF16),
            struct((HALF, LANES), F32),
            struct((2 * WIDTH, NODES), F32),
        ),
        in_specs=[smem] * 2 + [vmem] * 12,
        out_specs=(vmem,) * 3,
        scratch_shapes=scratch(strip_rows)
        + [
            pltpu.VMEM((strip_rows, LANES), F32),
            pltpu.VMEM((strip_rows, LANES), jnp.int32),
            pltpu.VMEM((2 * WIDTH, NODES), BF16),
        ],
        compiler_params=params,
    )(place, cell_scale, src2, orb2, base_potential, index, left, right, eig, stiffness, restrict_t,
      jnp.asarray(group_table(edge_cells), BF16), adjoint_mid, projected_mid)

    mine = lax.all_to_all(projected.reshape(n_orb, WIDTH, LANES), "orb", split_axis=0, concat_axis=0, tiled=True)
    payload = static - step_rate * jnp.sum(mine, axis=0)
    gathered = lax.all_to_all(
        jnp.broadcast_to(payload[None], (n_dom, WIDTH, LANES)), "dom", split_axis=0, concat_axis=0, tiled=True
    )
    columns = pl.pallas_call(
        sum_kernel,
        out_shape=struct((n_orb * WIDTH, LANES), F32),
        in_specs=[smem] * 3 + [vmem] * 4,
        out_specs=vmem,
        scratch_shapes=[pltpu.VMEM((LANES, LANES), F32)],
        compiler_params=params,
    )(place, owner1, pot_slot, gathered.reshape(n_dom * WIDTH, LANES), left, right, jnp.asarray(unpack_table(), BF16))
    columns = lax.all_to_all(columns.reshape(n_orb, WIDTH, LANES), "orb", split_axis=0, concat_axis=0, tiled=True)
    updated, applied2 = pl.pallas_call(
        apply_kernel,
        out_shape=(struct((HALF, HALF), F32), struct((rows, NODES), BF16)),
        in_specs=[smem] + [vmem] * 8,
        out_specs=(vmem, vmem),
        compiler_params=params,
    )(place, columns.reshape(n_orb * WIDTH, LANES), orb2, linear, ghost, left, right, index, prolong)
    return adjoint2.reshape(orbitals.shape), updated, applied2.reshape(orbitals.shape)


def solution(mesh):
    in_specs = (
        P("dom", "orb", None),
        P("dom", "orb", None),
        P("orb"),
        P("dom"),
        P("dom", None),
        P(),
        P("dom", None),
        P(),
        P(),
        P("dom", None),
        P("dom"),
        P("dom", None),
    )
    out_specs = (P("dom", "orb", None), P("dom", None), P("dom", "orb", None))
    return jax.shard_map(local, mesh=mesh, in_specs=in_specs, out_specs=out_specs, check_vma=False)
```

```python
import jax
import jax.numpy as jnp
import numpy as np
from jax import lax
from jax.experimental import pallas as pl
from jax.experimental.pallas import tpu as pltpu
from jax.sharding import PartitionSpec as P

ITERS = 4
relax = 0.25
step_rate = 0.1

LANES = 128
HALF = 64
NODES = 512
WIDTH = 8
CELLS = 48
HALO = 4
EXT = CELLS + 2 * HALO
F32, BF16 = jnp.float32, jnp.bfloat16


def dot(a, b, contract=((1,), (0,))):
    return lax.dot_general(a, b, (contract, ((), ())), preferred_element_type=F32)


def split(a):
    high = a.astype(BF16)
    return high, (a - high.astype(F32)).astype(BF16)


def lane_below(bound):
    return lax.broadcasted_iota(jnp.int32, (WIDTH, LANES), 1) < bound


SRC_ROWS, ORB_AT, BASE_AT, META_AT, HALO_ROWS = 32, 32, 40, 44, 48
IDX, SCALE, TARGET = slice(0, 128), slice(128, 256), slice(256, 512)
STRIP = 3 * HALO
NT = ((1,), (1,))


def tile(e):
    return slice(e * WIDTH, (e + 1) * WIDTH)


def cols(t):
    return slice(t * LANES, (t + 1) * LANES)


def face_rows(perm, wanted_cells):
    twice = jnp.concatenate([perm, perm], 1).astype(F32)
    columns = jnp.transpose(twice)[0:HALF]
    node = lax.broadcasted_iota(jnp.int32, (HALF, LANES), 0).astype(F32)
    lane = lax.broadcasted_iota(jnp.int32, (HALF, LANES), 1).astype(F32)
    low = lax.broadcasted_iota(jnp.int32, (1, LANES), 1) < HALF
    rows = []
    for c in wanted_cells:
        inverse = jnp.sum(jnp.where(columns[:, c : c + 1] == lane, node, 0.0), axis=0, keepdims=True)
        rows.append(jnp.where(low, inverse + HALF, twice[c : c + 1]))
    return rows


def in_hbm(array):
    return pltpu.with_memory_space_constraint(array, pltpu.HBM)


def pack_kernel(scale_hbm, owner_hbm, slot_hbm, src_hbm, orb_hbm, base_hbm, perm_hbm, to_left, to_right,
                scale, owner, slot, src, orb, base, perm, sems):
    top, rows = CELLS - WIDTH, CELLS * WIDTH
    copies = [(scale_hbm, scale), (owner_hbm, owner), (slot_hbm, slot)]
    for hbm, here, size, end in (
        (src_hbm, src, SRC_ROWS, rows), (orb_hbm, orb, 16, rows), (base_hbm, base, WIDTH, CELLS), (perm_hbm, perm, WIDTH, CELLS)
    ):
        copies.append((hbm.at[0:size], here.at[0]))
        copies.append((hbm.at[end - size : end], here.at[1]))
    copies = [pltpu.make_async_copy(one, two, sems.at[i]) for i, (one, two) in enumerate(copies)]
    for copy in copies:
        copy.start()
    for copy in copies:
        copy.wait()
    for end, out in enumerate((to_left, to_right)):
        inner, first = (0, 0) if end == 0 else (HALO, CELLS - HALO)
        edge_cell = end * (CELLS - 1)
        out[0:SRC_ROWS] = src[end].astype(F32)
        out[ORB_AT : ORB_AT + WIDTH] = orb[end].astype(F32)[tile(end)]
        out[BASE_AT : BASE_AT + HALO] = base[end, inner : inner + HALO]
        faces = face_rows(perm[end], range(inner, inner + HALO))
        target = (owner[edge_cell] * HALF + slot[edge_cell]).astype(F32)
        for i in range(HALO):
            at = slice(META_AT + i, META_AT + i + 1)
            out[at, IDX] = faces[i]
            out[at, SCALE] = jnp.full((1, LANES), scale[first + i], F32)
            out[at, TARGET] = jnp.full((1, 2 * LANES), target, F32)


def relaxed(strips, x, quarter, shifted, xb, kin, stiff, factor, index, gates):
    low = lane_below(HALF)
    cells = strips[-1][-1] + 1

    def step(_, carry):
        xb[...] = x[...].astype(BF16)
        kin[...] = dot(xb[...], stiff[...])
        for strip in strips:
            part_before = new_before = None
            for e in strip:
                rows = tile(e)
                scale = factor(e)
                parts, news = [], []
                for t in range(4):
                    here = x[rows, cols(t)]
                    part = scale * kin[rows, cols(t)] + shifted[rows, cols(t)] * here
                    parts.append(part)
                    news.append(here + quarter[rows, cols(t)] - relax * part)
                if e > strip[0]:
                    crossing = jnp.where(low, parts[0], part_before)
                    moved = relax * jnp.take_along_axis(crossing, index[tile(e - 1)], axis=1, mode="promise_in_bounds")
                    if e in gates:
                        moved = moved * gates[e]
                    news[0] = jnp.where(low, news[0] - moved, news[0])
                    x[tile(e - 1), cols(3)] = jnp.where(low, new_before, new_before - moved)
                for t in range(3):
                    x[rows, cols(t)] = news[t]
                part_before, new_before = parts[3], news[3]
            x[tile(strip[-1]), cols(3)] = new_before
        return carry

    lax.fori_loop(0, ITERS, step, 0)


def projection(orb_values, x_values, group, restrict_t):
    high, rest = split(orb_values.astype(F32) * x_values)
    density = dot(group, high) + dot(group, rest)
    high, rest = split(density)
    return dot(restrict_t, high, NT) + dot(restrict_t, rest, NT)


def interior_kernel(place, scale, owner, slot, src, orb, base, perm, eig, stiff_hbm, restrict_hbm, group_hbm,
                    potential_hbm, adjoint_out, projected_out, linear_out, index_out, static_out,
                    x, quarter, xb, kin, shifted, turned, stiff, restrict_t, group, potential, sems):
    pairs = ((stiff_hbm, stiff), (restrict_hbm, restrict_t), (group_hbm, group), (potential_hbm, potential))
    copies = [pltpu.make_async_copy(one, two, sems.at[i]) for i, (one, two) in enumerate(pairs)]
    for copy in copies:
        copy.start()
    quarter[...] = relax * src[...].astype(F32)
    x[...] = quarter[...]
    eig_column = eig[...]
    faces = face_rows(perm[...], range(CELLS))
    for c in range(CELLS):
        shifted[tile(c)] = base[c : c + 1] - eig_column
        index_out[tile(c)] = jnp.broadcast_to(faces[c].astype(jnp.int32), (WIDTH, LANES))
    for copy in copies:
        copy.wait()
    relaxed([range(CELLS)], x, quarter, shifted, xb, kin, stiff, lambda c: scale[c], index_out, {})
    inner = slice(HALO * WIDTH, (CELLS - HALO) * WIDTH)
    adjoint_out[...] = x[inner].astype(BF16)
    projected_out[...] = projection(orb[inner], x[inner], group[...], restrict_t[...])
    kin[...] = dot(orb[...], stiff[...])
    for pair in range(CELLS // 2):
        values = orb[pair * 16 : pair * 16 + 16].astype(F32)
        for c in (2 * pair, 2 * pair + 1):
            linear_out[tile(c)] = scale[c] * kin[tile(c)] + base[c : c + 1] * values[tile(c % 2)]
    turned[...] = jnp.transpose(potential[...])
    columns = turned[pl.ds(pl.multiple_of(place[1] * WIDTH, WIDTH), WIDTH)]
    row = lax.broadcasted_iota(jnp.int32, (WIDTH, LANES), 0)
    lane = lax.broadcasted_iota(jnp.int32, (WIDTH, LANES), 1)
    at = jnp.where(lane >= CELLS + HALF, row * 12 + lane - CELLS - HALF, -1)
    at = jnp.where(lane < CELLS + HALF + 12, at, -1)
    static = jnp.concatenate([jnp.zeros((WIDTH, CELLS), F32), columns, jnp.zeros((WIDTH, 16), F32)], 1)
    for c in range(CELLS):
        static = jnp.where(at == c // 6 * 12 + c % 6, owner[c].astype(F32), static)
        static = jnp.where(at == c // 6 * 12 + 6 + c % 6, slot[c].astype(F32), static)
    static_out[...] = static


def boundary_kernel(place, scale, src, orb, base, index_own, left, right, eig, stiff, restrict_t, group, adjoint_mid,
                    projected_mid, adjoint_out, projected_out, ghost_out,
                    x, quarter, xb, kin, shifted, factor, index, ob, adjoint_ends, sems):
    near, edge = 2 * HALO * WIDTH, HALO * WIDTH
    last = CELLS * WIDTH
    copies = [
        pltpu.make_async_copy(adjoint_mid, adjoint_out.at[edge : last - edge], sems.at[0]),
        pltpu.make_async_copy(adjoint_ends.at[0], adjoint_out.at[0:edge], sems.at[1]),
        pltpu.make_async_copy(adjoint_ends.at[1], adjoint_out.at[last - edge : last], sems.at[2]),
    ]
    copies[0].start()
    quarter[0:edge] = relax * left[0:SRC_ROWS]
    quarter[edge : edge + near] = relax * src[0:near].astype(F32)
    quarter[edge + near : edge + 2 * near] = relax * src[last - near :].astype(F32)
    quarter[edge + 2 * near :] = relax * right[0:SRC_ROWS]
    x[...] = quarter[...]
    eig_column = eig[...]
    for e in range(2 * STRIP):
        ghost = left if e < HALO else right if e >= 2 * STRIP - HALO else None
        if ghost is None:
            c = e - HALO if e < STRIP else CELLS - 2 * HALO + e - STRIP
            base_row = base[c : c + 1]
            factor[tile(e)] = jnp.full((WIDTH, LANES), scale[c], F32)
            index[tile(e)] = index_own[tile(c)]
        else:
            i = e if e < HALO else e - 2 * STRIP + HALO
            base_row = ghost[BASE_AT + i : BASE_AT + i + 1]
            meta_row = ghost[META_AT + i : META_AT + i + 1]
            factor[tile(e)] = jnp.broadcast_to(meta_row[:, SCALE], (WIDTH, LANES))
            index[tile(e)] = jnp.broadcast_to(meta_row[:, IDX].astype(jnp.int32), (WIDTH, LANES))
        shifted[tile(e)] = base_row - eig_column
    gates = {
        HALO: jnp.where(place[0] > 0, 1.0, 0.0),
        2 * STRIP - HALO: jnp.where(place[0] < place[2] - 1, 1.0, 0.0),
    }
    relaxed([range(STRIP), range(STRIP, 2 * STRIP)], x, quarter, shifted, xb, kin, stiff,
            lambda e: factor[tile(e)], index, gates)
    low_cells, high_cells = x[edge : 2 * edge], x[4 * edge : 5 * edge]
    adjoint_ends[0] = low_cells.astype(BF16)
    adjoint_ends[1] = high_cells.astype(BF16)
    copies[1].start()
    copies[2].start()
    own_orb = jnp.concatenate([orb[0:edge], orb[last - edge :]], 0)
    own_x = jnp.concatenate([low_cells, high_cells], 0)
    projected_out[...] = projected_mid[...] + projection(own_orb, own_x, group[...], restrict_t[...])
    ghosts = jnp.concatenate([left[ORB_AT : ORB_AT + WIDTH], right[ORB_AT : ORB_AT + WIDTH]], 0)
    ob[...] = ghosts.astype(BF16)
    ghost_kin = dot(ob[...], stiff[...])
    for i, e, base_row in (
        (0, HALO - 1, left[BASE_AT + HALO - 1 : BASE_AT + HALO]),
        (1, 2 * STRIP - HALO, right[BASE_AT : BASE_AT + 1]),
    ):
        for t in range(4):
            ghost_out[tile(i), cols(t)] = (
                factor[tile(e)] * ghost_kin[tile(i), cols(t)] + base_row[:, cols(t)] * ghosts[tile(i), cols(t)]
            )
    for copy in copies:
        copy.wait()


def sum_kernel(place, owner, slot, gathered, left, right, unpack, out, asked):
    sources = gathered.shape[0] // WIDTH
    own = lax.broadcasted_iota(jnp.int32, (HALF, LANES), 0) + place[0] * HALF
    asked[0:HALF] = own.astype(F32)
    for c in range(CELLS):
        asked[HALF + c : HALF + c + 1] = jnp.full((1, LANES), (owner[c] * HALF + slot[c]).astype(F32), F32)
    asked[HALF + CELLS : HALF + CELLS + 1] = left[META_AT + HALO - 1 : META_AT + HALO, 256:384]
    asked[HALF + CELLS + 1 : HALF + CELLS + 2] = right[META_AT : META_AT + 1, 256:384]
    asked[HALF + CELLS + 2 :] = jnp.full((LANES - HALF - CELLS - 2, LANES), -2.0, F32)
    values = gathered[...]
    high, rest = split(values)
    ids = dot(high, unpack[...])
    row = lax.broadcasted_iota(jnp.int32, ids.shape, 0) % WIDTH
    lane = lax.broadcasted_iota(jnp.int32, ids.shape, 1)
    ids = jnp.where(lane // 6 == row, ids, 0.0)
    ids = jnp.sum(ids.reshape(sources, WIDTH, LANES), axis=1)
    lane = lax.broadcasted_iota(jnp.int32, ids.shape, 1)
    source = lax.broadcasted_iota(jnp.int32, ids.shape, 0)
    known = (source * HALF + lane - CELLS).astype(F32)
    ids = jnp.where(lane < CELLS, ids, jnp.where(lane < CELLS + HALF, known, -1.0))
    wanted = asked[...]
    total = jnp.zeros((2 * WIDTH, LANES), F32)
    for s in range(0, sources, 2):
        hot = [jnp.where(wanted == ids[i : i + 1], 1.0, 0.0).astype(BF16) for i in (s, s + 1)]
        both = [jnp.concatenate([high[tile(i)], rest[tile(i)]], 0) for i in (s, s + 1)]
        total = total + dot(jnp.concatenate(both, 1), jnp.concatenate(hot, 1), NT)
    result = total[:WIDTH] + total[WIDTH:]
    for r in range(out.shape[0] // WIDTH):
        out[tile(r)] = result


def apply_kernel(place, columns, orb, linear, ghost, left, right, index, prolong, updated_out, applied_out):
    table = jnp.transpose(columns[...])
    updated_out[...] = table[0:HALF]
    high, rest = split(table[HALF:])
    node = dot(high, prolong[...]) + dot(rest, prolong[...])
    low = lane_below(HALF)
    part_before = new_before = index_before = None
    finished = []
    for e in range(CELLS + 2):
        c = e - 1
        if e == 0:
            values, start, node_at = left[ORB_AT : ORB_AT + WIDTH], ghost[tile(0)], CELLS
        elif e <= CELLS:
            values = orb[c // 2 * 16 : c // 2 * 16 + 16].astype(F32)[tile(c % 2)]
            start, node_at = linear[tile(c)], c
        else:
            values, start, node_at = right[ORB_AT : ORB_AT + WIDTH], ghost[tile(1)], CELLS + 1
        whole = start + node[node_at : node_at + 1] * values
        parts = [whole[:, cols(t)] for t in range(4)]
        if e > 0:
            crossing = jnp.where(low, parts[0], part_before)
            moved = jnp.take_along_axis(crossing, index_before, axis=1, mode="promise_in_bounds")
            if e == 1:
                moved = moved * jnp.where(place[0] > 0, 1.0, 0.0)
            if e == CELLS + 1:
                moved = moved * jnp.where(place[0] < place[2] - 1, 1.0, 0.0)
            done = jnp.where(low, new_before[3], new_before[3] + moved)
            if e > 1:
                finished.append(jnp.concatenate([*new_before[:3], done], 1))
            news = [jnp.where(low, parts[0] + moved, parts[0]), *parts[1:]]
        else:
            news = parts
        part_before, new_before = parts[3], news
        if e == 0:
            meta_row = left[META_AT + HALO - 1 : META_AT + HALO]
            index_before = jnp.broadcast_to(meta_row[:, IDX].astype(jnp.int32), (WIDTH, LANES))
        elif e <= CELLS:
            index_before = index[tile(c)]
        if len(finished) == 2:
            applied_out[(e - 3) * WIDTH : (e - 1) * WIDTH] = jnp.concatenate(finished, 0).astype(BF16)
            finished = []


def unpack_table():
    table = np.zeros((LANES, LANES), np.float32)
    for k in range(CELLS):
        table[112 + k % 6, k] = 64.0
        table[118 + k % 6, k] = 1.0
    return table


def group_table(cells):
    table = np.zeros((LANES, len(cells) * WIDTH), np.float32)
    for at, cell in enumerate(cells):
        table[cell, at * WIDTH : (at + 1) * WIDTH] = 1.0
    return table


def local(orbitals, adjoint_source, eigenvalues, cell_scale, base_potential, stiffness, face_perm, restrict,
          prolong, owner, pot_slot, potential):
    n_dom, n_orb = lax.axis_size("dom"), lax.axis_size("orb")
    dom, orb_at = lax.axis_index("dom"), lax.axis_index("orb")
    vmem = pl.BlockSpec(memory_space=pltpu.VMEM)
    smem = pl.BlockSpec(memory_space=pltpu.SMEM)
    params = pltpu.CompilerParams(vmem_limit_bytes=32 * 2**20)
    struct = jax.ShapeDtypeStruct

    orb2 = orbitals.reshape(CELLS * WIDTH, NODES)
    src2 = adjoint_source.reshape(CELLS * WIDTH, NODES)
    owner1 = owner.reshape(CELLS)
    place = jnp.stack([dom, orb_at, jnp.int32(n_dom)])

    hbm = pl.BlockSpec(memory_space=pltpu.HBM)
    to_left, to_right = pl.pallas_call(
        pack_kernel,
        out_shape=(struct((HALO_ROWS, NODES), F32),) * 2,
        in_specs=[hbm] * 7,
        out_specs=(vmem, vmem),
        scratch_shapes=[
            pltpu.SMEM((CELLS,), F32),
            pltpu.SMEM((CELLS,), jnp.int32),
            pltpu.SMEM((CELLS,), jnp.int32),
            pltpu.VMEM((2, SRC_ROWS, NODES), BF16),
            pltpu.VMEM((2, 16, NODES), BF16),
            pltpu.VMEM((2, WIDTH, NODES), F32),
            pltpu.VMEM((2, WIDTH, HALF), jnp.int32),
            pltpu.SemaphoreType.DMA((11,)),
        ],
        compiler_params=params,
    )(*map(in_hbm, (cell_scale, owner1, pot_slot, src2, orb2, base_potential, face_perm)))

    ahead = [(i, i + 1) for i in range(n_dom - 1)]
    left = lax.ppermute(to_right, "dom", ahead)
    right = lax.ppermute(to_left, "dom", [(b, a) for a, b in ahead])

    eig = eigenvalues[:, None]
    restrict_t = restrict.T
    rows = CELLS * WIDTH
    inner = rows - 2 * HALO * WIDTH

    def scratch(n):
        return [
            pltpu.VMEM((n, NODES), F32),
            pltpu.VMEM((n, NODES), F32),
            pltpu.VMEM((n, NODES), BF16),
            pltpu.VMEM((n, NODES), F32),
            pltpu.VMEM((n, NODES), F32),
        ]

    adjoint_mid, projected_mid, linear, index, static = pl.pallas_call(
        interior_kernel,
        out_shape=(
            struct((inner, NODES), BF16),
            struct((HALF, LANES), F32),
            struct((rows, NODES), F32),
            struct((rows, LANES), jnp.int32),
            struct((WIDTH, LANES), F32),
        ),
        in_specs=[smem] * 4 + [vmem] * 5 + [hbm] * 4,
        out_specs=(vmem,) * 5,
        scratch_shapes=scratch(rows)
        + [
            pltpu.VMEM((HALF, HALF), F32),
            pltpu.VMEM((NODES, NODES), BF16),
            pltpu.VMEM((HALF, NODES), BF16),
            pltpu.VMEM((LANES, inner), BF16),
            pltpu.VMEM((HALF, HALF), F32),
            pltpu.SemaphoreType.DMA((4,)),
        ],
        compiler_params=params,
        cost_estimate=pl.CostEstimate(flops=5 * 2 * rows * NODES * NODES, bytes_accessed=4 * 2**20, transcendentals=0),
    )(place, cell_scale, owner1, pot_slot, src2, orb2, base_potential, face_perm, eig, *map(
          in_hbm, (stiffness, restrict_t, jnp.asarray(group_table(range(HALO, CELLS - HALO)), BF16), potential)
      ))

    edge_cells = [*range(HALO), *range(CELLS - HALO, CELLS)]
    strip_rows = 2 * STRIP * WIDTH
    adjoint2, projected, ghost = pl.pallas_call(
        boundary_kernel,
        out_shape=(
            struct((rows, NODES), BF16),
            struct((HALF, LANES), F32),
            struct((2 * WIDTH, NODES), F32),
        ),
        in_specs=[smem] * 2 + [vmem] * 12,
        out_specs=(hbm, vmem, vmem),
        scratch_shapes=scratch(strip_rows)
        + [
            pltpu.VMEM((strip_rows, LANES), F32),
            pltpu.VMEM((strip_rows, LANES), jnp.int32),
            pltpu.VMEM((2 * WIDTH, NODES), BF16),
            pltpu.VMEM((2, HALO * WIDTH, NODES), BF16),
            pltpu.SemaphoreType.DMA((3,)),
        ],
        compiler_params=params,
    )(place, cell_scale, src2, orb2, base_potential, index, left, right, eig, stiffness, restrict_t,
      jnp.asarray(group_table(edge_cells), BF16), adjoint_mid, projected_mid)

    mine = lax.all_to_all(projected.reshape(n_orb, WIDTH, LANES), "orb", split_axis=0, concat_axis=0, tiled=True)
    payload = static - step_rate * jnp.sum(mine, axis=0)
    gathered = lax.all_to_all(
        jnp.broadcast_to(payload[None], (n_dom, WIDTH, LANES)), "dom", split_axis=0, concat_axis=0, tiled=True
    )
    columns = pl.pallas_call(
        sum_kernel,
        out_shape=struct((n_orb * WIDTH, LANES), F32),
        in_specs=[smem] * 3 + [vmem] * 4,
        out_specs=vmem,
        scratch_shapes=[pltpu.VMEM((LANES, LANES), F32)],
        compiler_params=params,
    )(place, owner1, pot_slot, gathered.reshape(n_dom * WIDTH, LANES), left, right, jnp.asarray(unpack_table(), BF16))
    columns = lax.all_to_all(columns.reshape(n_orb, WIDTH, LANES), "orb", split_axis=0, concat_axis=0, tiled=True)
    updated, applied2 = pl.pallas_call(
        apply_kernel,
        out_shape=(struct((HALF, HALF), F32), struct((rows, NODES), BF16)),
        in_specs=[smem] + [vmem] * 8,
        out_specs=(vmem, vmem),
        compiler_params=params,
    )(place, columns.reshape(n_orb * WIDTH, LANES), orb2, linear, ghost, left, right, index, prolong)
    return adjoint2.reshape(orbitals.shape), updated, applied2.reshape(orbitals.shape)


def solution(mesh):
    in_specs = (
        P("dom", "orb", None),
        P("dom", "orb", None),
        P("orb"),
        P("dom"),
        P("dom", None),
        P(),
        P("dom", None),
        P(),
        P(),
        P("dom", None),
        P("dom"),
        P("dom", None),
    )
    out_specs = (P("dom", "orb", None), P("dom", None), P("dom", "orb", None))
    return jax.shard_map(local, mesh=mesh, in_specs=in_specs, out_specs=out_specs, check_vma=False)
```

```python
import jax
import jax.numpy as jnp
import numpy as np
from jax import lax
from jax.experimental import pallas as pl
from jax.experimental.pallas import tpu as pltpu
from jax.sharding import PartitionSpec as P

ITERS = 4
relax = 0.25
step_rate = 0.1

LANES = 128
HALF = 64
NODES = 512
WIDTH = 8
CELLS = 48
HALO = 4
EXT = CELLS + 2 * HALO
F32, BF16 = jnp.float32, jnp.bfloat16


def dot(a, b, contract=((1,), (0,))):
    return lax.dot_general(a, b, (contract, ((), ())), preferred_element_type=F32)


def split(a):
    high = a.astype(BF16)
    return high, (a - high.astype(F32)).astype(BF16)


def lane_below(bound):
    return lax.broadcasted_iota(jnp.int32, (WIDTH, LANES), 1) < bound


SRC_ROWS, ORB_AT, BASE_AT, META_AT, HALO_ROWS = 32, 32, 40, 44, 48
IDX, SCALE, OWNER, SLOT = slice(0, 128), slice(128, 256), slice(256, 384), slice(384, 512)
POT, IDS, GHOST_IDS = CELLS, CELLS + HALF, CELLS + HALF + 12
X, Z, Y, CORES = 4, 16, 4, 2
DOM, ORB, OUTER = ("x", "z"), ("y", "core"), ("x", "y", "core")
COPIES = Y * CORES
STRIP = 3 * HALO
NT = ((1,), (1,))


def tile(e):
    return slice(e * WIDTH, (e + 1) * WIDTH)


def cols(t):
    return slice(t * LANES, (t + 1) * LANES)


def face_rows(perm, wanted_cells):
    twice = jnp.concatenate([perm, perm], 1).astype(F32)
    columns = jnp.transpose(twice)[0:HALF]
    node = lax.broadcasted_iota(jnp.int32, (HALF, LANES), 0).astype(F32)
    lane = lax.broadcasted_iota(jnp.int32, (HALF, LANES), 1).astype(F32)
    low = lax.broadcasted_iota(jnp.int32, (1, LANES), 1) < HALF
    rows = []
    for c in wanted_cells:
        inverse = jnp.sum(jnp.where(columns[:, c : c + 1] == lane, node, 0.0), axis=0, keepdims=True)
        rows.append(jnp.where(low, inverse + HALF, twice[c : c + 1]))
    return rows


def in_hbm(array):
    return pltpu.with_memory_space_constraint(array, pltpu.HBM)


def pack_kernel(scale_hbm, owner_hbm, slot_hbm, src_hbm, orb_hbm, base_hbm, perm_hbm, to_left, to_right,
                scale, owner, slot, src, orb, base, perm, sems):
    top, rows = CELLS - WIDTH, CELLS * WIDTH
    copies = [(scale_hbm, scale), (owner_hbm, owner), (slot_hbm, slot)]
    for hbm, here, size, end in (
        (src_hbm, src, SRC_ROWS, rows), (orb_hbm, orb, 16, rows), (base_hbm, base, WIDTH, CELLS), (perm_hbm, perm, WIDTH, CELLS)
    ):
        copies.append((hbm.at[0:size], here.at[0]))
        copies.append((hbm.at[end - size : end], here.at[1]))
    copies = [pltpu.make_async_copy(one, two, sems.at[i]) for i, (one, two) in enumerate(copies)]
    for copy in copies:
        copy.start()
    for copy in copies:
        copy.wait()
    for end, out in enumerate((to_left, to_right)):
        inner, first = (0, 0) if end == 0 else (HALO, CELLS - HALO)
        edge_cell = end * (CELLS - 1)
        out[0:SRC_ROWS] = src[end].astype(F32)
        out[ORB_AT : ORB_AT + WIDTH] = orb[end].astype(F32)[tile(end)]
        out[BASE_AT : BASE_AT + HALO] = base[end, inner : inner + HALO]
        faces = face_rows(perm[end], range(inner, inner + HALO))
        for i in range(HALO):
            at = slice(META_AT + i, META_AT + i + 1)
            out[at, IDX] = faces[i]
            out[at, SCALE] = jnp.full((1, LANES), scale[first + i], F32)
            out[at, OWNER] = jnp.full((1, LANES), owner[edge_cell].astype(F32), F32)
            out[at, SLOT] = jnp.full((1, LANES), slot[edge_cell].astype(F32), F32)


def relaxed(strips, x, quarter, shifted, xb, kin, stiff, factor, index, gates):
    low = lane_below(HALF)
    cells = strips[-1][-1] + 1

    def step(_, carry):
        xb[...] = x[...].astype(BF16)
        kin[...] = dot(xb[...], stiff[...])
        for strip in strips:
            part_before = new_before = None
            for e in strip:
                rows = tile(e)
                scale = factor(e)
                parts, news = [], []
                for t in range(4):
                    here = x[rows, cols(t)]
                    part = scale * kin[rows, cols(t)] + shifted[rows, cols(t)] * here
                    parts.append(part)
                    news.append(here + quarter[rows, cols(t)] - relax * part)
                if e > strip[0]:
                    crossing = jnp.where(low, parts[0], part_before)
                    moved = relax * jnp.take_along_axis(crossing, index[tile(e - 1)], axis=1, mode="promise_in_bounds")
                    if e in gates:
                        moved = moved * gates[e]
                    news[0] = jnp.where(low, news[0] - moved, news[0])
                    x[tile(e - 1), cols(3)] = jnp.where(low, new_before, new_before - moved)
                for t in range(3):
                    x[rows, cols(t)] = news[t]
                part_before, new_before = parts[3], news[3]
            x[tile(strip[-1]), cols(3)] = new_before
        return carry

    lax.fori_loop(0, ITERS, step, 0)


def projection(orb_values, x_values, group, restrict_t):
    high, rest = split(orb_values.astype(F32) * x_values)
    density = dot(group, high) + dot(group, rest)
    high, rest = split(density)
    return dot(restrict_t, high, NT) + dot(restrict_t, rest, NT)


def interior_kernel(place, scale, owner, slot, src, orb, base, perm, eig, stiff_hbm, restrict_hbm, group_hbm,
                    potential_hbm, adjoint_out, projected_out, linear_out, index_out,
                    x, quarter, xb, kin, shifted, stiff, restrict_t, group, potential, sems):
    pairs = ((stiff_hbm, stiff), (restrict_hbm, restrict_t), (group_hbm, group), (potential_hbm, potential))
    copies = [pltpu.make_async_copy(one, two, sems.at[i]) for i, (one, two) in enumerate(pairs)]
    for copy in copies:
        copy.start()
    quarter[...] = relax * src[...].astype(F32)
    x[...] = quarter[...]
    eig_column = eig[...]
    faces = face_rows(perm[...], range(CELLS))
    for c in range(CELLS):
        shifted[tile(c)] = base[c : c + 1] - eig_column
        index_out[tile(c)] = jnp.broadcast_to(faces[c].astype(jnp.int32), (WIDTH, LANES))
    for copy in copies:
        copy.wait()
    relaxed([range(CELLS)], x, quarter, shifted, xb, kin, stiff, lambda c: scale[c], index_out, {})
    inner = slice(HALO * WIDTH, (CELLS - HALO) * WIDTH)
    adjoint_out[...] = x[inner].astype(BF16)
    kin[...] = dot(orb[...], stiff[...])
    for pair in range(CELLS // 2):
        values = orb[pair * 16 : pair * 16 + 16].astype(F32)
        for c in (2 * pair, 2 * pair + 1):
            linear_out[tile(c)] = scale[c] * kin[tile(c)] + base[c : c + 1] * values[tile(c % 2)]
    row = lax.broadcasted_iota(jnp.int32, (WIDTH, LANES), 0)
    lane = lax.broadcasted_iota(jnp.int32, (WIDTH, LANES), 1)
    at = jnp.where((lane >= IDS) & (lane < GHOST_IDS), row * 12 + lane - IDS, -1)
    ids = jnp.zeros((WIDTH, LANES), F32)
    for c in range(CELLS):
        ids = jnp.where(at == c // 6 * 12 + c % 6, owner[c].astype(F32), ids)
        ids = jnp.where(at == c // 6 * 12 + 6 + c % 6, slot[c].astype(F32), ids)
    turned = jnp.transpose(potential[...])
    static = jnp.concatenate([jnp.zeros((HALF, CELLS), F32), turned, jnp.zeros((HALF, 16), F32)], 1)
    static = (static + jnp.concatenate([ids] * (HALF // WIDTH), 0)) * (1.0 / COPIES)
    projected_out[...] = static - step_rate * projection(orb[inner], x[inner], group[...], restrict_t[...])


def boundary_kernel(place, scale, src, orb, base, index_own, left, right, eig, stiff, restrict_t, group, adjoint_mid,
                    projected_mid, adjoint_out, projected_out, ghost_out,
                    x, quarter, xb, kin, shifted, factor, index, ob, adjoint_ends, sems):
    near, edge = 2 * HALO * WIDTH, HALO * WIDTH
    last = CELLS * WIDTH
    copies = [
        pltpu.make_async_copy(adjoint_mid, adjoint_out.at[edge : last - edge], sems.at[0]),
        pltpu.make_async_copy(adjoint_ends.at[0], adjoint_out.at[0:edge], sems.at[1]),
        pltpu.make_async_copy(adjoint_ends.at[1], adjoint_out.at[last - edge : last], sems.at[2]),
    ]
    copies[0].start()
    quarter[0:edge] = relax * left[0:SRC_ROWS]
    quarter[edge : edge + near] = relax * src[0:near].astype(F32)
    quarter[edge + near : edge + 2 * near] = relax * src[last - near :].astype(F32)
    quarter[edge + 2 * near :] = relax * right[0:SRC_ROWS]
    x[...] = quarter[...]
    eig_column = eig[...]
    for e in range(2 * STRIP):
        ghost = left if e < HALO else right if e >= 2 * STRIP - HALO else None
        if ghost is None:
            c = e - HALO if e < STRIP else CELLS - 2 * HALO + e - STRIP
            base_row = base[c : c + 1]
            factor[tile(e)] = jnp.full((WIDTH, LANES), scale[c], F32)
            index[tile(e)] = index_own[tile(c)]
        else:
            i = e if e < HALO else e - 2 * STRIP + HALO
            base_row = ghost[BASE_AT + i : BASE_AT + i + 1]
            meta_row = ghost[META_AT + i : META_AT + i + 1]
            factor[tile(e)] = jnp.broadcast_to(meta_row[:, SCALE], (WIDTH, LANES))
            index[tile(e)] = jnp.broadcast_to(meta_row[:, IDX].astype(jnp.int32), (WIDTH, LANES))
        shifted[tile(e)] = base_row - eig_column
    gates = {
        HALO: jnp.where(place[0] > 0, 1.0, 0.0),
        2 * STRIP - HALO: jnp.where(place[0] < X * Z - 1, 1.0, 0.0),
    }
    relaxed([range(STRIP), range(STRIP, 2 * STRIP)], x, quarter, shifted, xb, kin, stiff,
            lambda e: factor[tile(e)], index, gates)
    low_cells, high_cells = x[edge : 2 * edge], x[4 * edge : 5 * edge]
    adjoint_ends[0] = low_cells.astype(BF16)
    adjoint_ends[1] = high_cells.astype(BF16)
    copies[1].start()
    copies[2].start()
    own_orb = jnp.concatenate([orb[0:edge], orb[last - edge :]], 0)
    own_x = jnp.concatenate([low_cells, high_cells], 0)
    lane = lax.broadcasted_iota(jnp.int32, (1, LANES), 1)
    ghost_ids = jnp.zeros((1, LANES), F32)
    for i, row in enumerate((left[META_AT + HALO - 1 : META_AT + HALO], right[META_AT : META_AT + 1])):
        ghost_ids = jnp.where(lane == GHOST_IDS + 2 * i, row[:, OWNER], ghost_ids)
        ghost_ids = jnp.where(lane == GHOST_IDS + 2 * i + 1, row[:, SLOT], ghost_ids)
    added = projection(own_orb, own_x, group[...], restrict_t[...])
    whole = projected_mid[...] + ghost_ids * (1.0 / COPIES) - step_rate * added
    for i in range(X):
        projected_out[i * HALF : (i + 1) * HALF] = whole
    ghosts = jnp.concatenate([left[ORB_AT : ORB_AT + WIDTH], right[ORB_AT : ORB_AT + WIDTH]], 0)
    ob[...] = ghosts.astype(BF16)
    ghost_kin = dot(ob[...], stiff[...])
    for i, e, base_row in (
        (0, HALO - 1, left[BASE_AT + HALO - 1 : BASE_AT + HALO]),
        (1, 2 * STRIP - HALO, right[BASE_AT : BASE_AT + 1]),
    ):
        for t in range(4):
            ghost_out[tile(i), cols(t)] = (
                factor[tile(e)] * ghost_kin[tile(i), cols(t)] + base_row[:, cols(t)] * ghosts[tile(i), cols(t)]
            )
    for copy in copies:
        copy.wait()


def sum_kernel(place, gathered, asking, unpack, out):
    high, rest = split(gathered[...])
    ids = dot(jnp.concatenate([high, asking[...].astype(BF16)], 0), unpack[...])
    row = lax.broadcasted_iota(jnp.int32, ids.shape, 0) % WIDTH
    lane = lax.broadcasted_iota(jnp.int32, ids.shape, 1)
    ids = jnp.where(jnp.where(lane < CELLS, lane // 6, 0) == row, ids, 0.0)
    ids = jnp.sum(ids.reshape(Z + X, WIDTH, LANES), axis=1)
    lane = lax.broadcasted_iota(jnp.int32, ids.shape, 1)
    row = lax.broadcasted_iota(jnp.int32, ids.shape, 0)
    dom = jnp.where(row < Z, place[1] * Z + row, (row - Z) * Z + place[2])
    slots = (dom * HALF + lane - POT).astype(F32)
    ids = jnp.where((lane >= POT) & (lane < IDS), slots, ids)
    known = jnp.where(lane[:Z] < IDS, ids[:Z], -1.0)
    wanted = jnp.where(lane[Z:] < IDS + 2, ids[Z:], -2.0)
    known = jnp.transpose(jnp.concatenate([known, jnp.zeros((LANES - Z, LANES), F32)], 0))
    total = jnp.zeros((2 * WIDTH, X * LANES), F32)
    for s in range(0, Z, 2):
        hot = [
            jnp.concatenate(
                [jnp.where(known[:, i : i + 1] == wanted[m : m + 1], 1.0, 0.0).astype(BF16) for m in range(X)], 1
            )
            for i in (s, s + 1)
        ]
        both = [jnp.concatenate([high[tile(i)], rest[tile(i)]], 0) for i in (s, s + 1)]
        total = total + dot(jnp.concatenate(both, 1), jnp.concatenate(hot, 0))
    result = total[:WIDTH] + total[WIDTH:]
    for m in range(X):
        for i in range(COPIES):
            out[tile(m * COPIES + i)] = result[:, cols(m)]


def apply_kernel(place, columns, orb, linear, ghost, left, right, index, prolong, updated_out, applied_out):
    summed = columns[0:HALF]
    for i in range(1, X):
        summed = summed + columns[i * HALF : (i + 1) * HALF]
    table = jnp.transpose(summed)
    updated_out[...] = table[POT:IDS]
    high, rest = split(table)
    node = dot(high, prolong[...]) + dot(rest, prolong[...])
    low = lane_below(HALF)
    part_before = new_before = index_before = None
    finished = []
    for e in range(CELLS + 2):
        c = e - 1
        if e == 0:
            values, start, node_at = left[ORB_AT : ORB_AT + WIDTH], ghost[tile(0)], IDS
        elif e <= CELLS:
            values = orb[c // 2 * 16 : c // 2 * 16 + 16].astype(F32)[tile(c % 2)]
            start, node_at = linear[tile(c)], c
        else:
            values, start, node_at = right[ORB_AT : ORB_AT + WIDTH], ghost[tile(1)], IDS + 1
        whole = start + node[node_at : node_at + 1] * values
        parts = [whole[:, cols(t)] for t in range(4)]
        if e > 0:
            crossing = jnp.where(low, parts[0], part_before)
            moved = jnp.take_along_axis(crossing, index_before, axis=1, mode="promise_in_bounds")
            if e == 1:
                moved = moved * jnp.where(place[0] > 0, 1.0, 0.0)
            if e == CELLS + 1:
                moved = moved * jnp.where(place[0] < X * Z - 1, 1.0, 0.0)
            done = jnp.where(low, new_before[3], new_before[3] + moved)
            if e > 1:
                finished.append(jnp.concatenate([*new_before[:3], done], 1))
            news = [jnp.where(low, parts[0] + moved, parts[0]), *parts[1:]]
        else:
            news = parts
        part_before, new_before = parts[3], news
        if e == 0:
            meta_row = left[META_AT + HALO - 1 : META_AT + HALO]
            index_before = jnp.broadcast_to(meta_row[:, IDX].astype(jnp.int32), (WIDTH, LANES))
        elif e <= CELLS:
            index_before = index[tile(c)]
        if len(finished) == 2:
            applied_out[(e - 3) * WIDTH : (e - 1) * WIDTH] = jnp.concatenate(finished, 0).astype(BF16)
            finished = []


def unpack_table():
    table = np.zeros((LANES, LANES), np.float32)
    for k in range(CELLS):
        table[112 + k % 6, k] = 64.0
        table[118 + k % 6, k] = 1.0
    for i in range(2):
        table[GHOST_IDS + 2 * i, IDS + i] = 64.0
        table[GHOST_IDS + 2 * i + 1, IDS + i] = 1.0
    return table


def group_table(cells):
    table = np.zeros((LANES, len(cells) * WIDTH), np.float32)
    for at, cell in enumerate(cells):
        table[cell, at * WIDTH : (at + 1) * WIDTH] = 1.0
    return table


def local(orbitals, adjoint_source, eigenvalues, cell_scale, base_potential, stiffness, face_perm, restrict,
          prolong, owner, pot_slot, potential):
    x_at, z_at = lax.axis_index("x"), lax.axis_index("z")
    vmem = pl.BlockSpec(memory_space=pltpu.VMEM)
    smem = pl.BlockSpec(memory_space=pltpu.SMEM)
    params = pltpu.CompilerParams(vmem_limit_bytes=32 * 2**20)
    struct = jax.ShapeDtypeStruct

    orb2 = orbitals.reshape(CELLS * WIDTH, NODES)
    src2 = adjoint_source.reshape(CELLS * WIDTH, NODES)
    owner1 = owner.reshape(CELLS)
    place = jnp.stack([x_at * Z + z_at, x_at, z_at])

    hbm = pl.BlockSpec(memory_space=pltpu.HBM)
    to_left, to_right = pl.pallas_call(
        pack_kernel,
        out_shape=(struct((HALO_ROWS, NODES), F32),) * 2,
        in_specs=[hbm] * 7,
        out_specs=(vmem, vmem),
        scratch_shapes=[
            pltpu.SMEM((CELLS,), F32),
            pltpu.SMEM((CELLS,), jnp.int32),
            pltpu.SMEM((CELLS,), jnp.int32),
            pltpu.VMEM((2, SRC_ROWS, NODES), BF16),
            pltpu.VMEM((2, 16, NODES), BF16),
            pltpu.VMEM((2, WIDTH, NODES), F32),
            pltpu.VMEM((2, WIDTH, HALF), jnp.int32),
            pltpu.SemaphoreType.DMA((11,)),
        ],
        compiler_params=params,
    )(*map(in_hbm, (cell_scale, owner1, pot_slot, src2, orb2, base_potential, face_perm)))

    ahead = [(i, i + 1) for i in range(X * Z - 1)]
    left = lax.ppermute(to_right, DOM, ahead)
    right = lax.ppermute(to_left, DOM, [(b, a) for a, b in ahead])

    eig = eigenvalues[:, None]
    restrict_t = restrict.T
    rows = CELLS * WIDTH
    inner = rows - 2 * HALO * WIDTH

    def scratch(n):
        return [
            pltpu.VMEM((n, NODES), F32),
            pltpu.VMEM((n, NODES), F32),
            pltpu.VMEM((n, NODES), BF16),
            pltpu.VMEM((n, NODES), F32),
            pltpu.VMEM((n, NODES), F32),
        ]

    adjoint_mid, projected_mid, linear, index = pl.pallas_call(
        interior_kernel,
        out_shape=(
            struct((inner, NODES), BF16),
            struct((HALF, LANES), F32),
            struct((rows, NODES), F32),
            struct((rows, LANES), jnp.int32),
        ),
        in_specs=[smem] * 4 + [vmem] * 5 + [hbm] * 4,
        out_specs=(vmem,) * 4,
        scratch_shapes=scratch(rows)
        + [
            pltpu.VMEM((NODES, NODES), BF16),
            pltpu.VMEM((HALF, NODES), BF16),
            pltpu.VMEM((LANES, inner), BF16),
            pltpu.VMEM((HALF, HALF), F32),
            pltpu.SemaphoreType.DMA((4,)),
        ],
        compiler_params=params,
        cost_estimate=pl.CostEstimate(flops=5 * 2 * rows * NODES * NODES, bytes_accessed=4 * 2**20, transcendentals=0),
    )(place, cell_scale, owner1, pot_slot, src2, orb2, base_potential, face_perm, eig, *map(
          in_hbm, (stiffness, restrict_t, jnp.asarray(group_table(range(HALO, CELLS - HALO)), BF16), potential)
      ))

    edge_cells = [*range(HALO), *range(CELLS - HALO, CELLS)]
    strip_rows = 2 * STRIP * WIDTH
    adjoint2, projected, ghost = pl.pallas_call(
        boundary_kernel,
        out_shape=(
            struct((rows, NODES), BF16),
            struct((X * HALF, LANES), F32),
            struct((2 * WIDTH, NODES), F32),
        ),
        in_specs=[smem] * 2 + [vmem] * 12,
        out_specs=(hbm, vmem, vmem),
        scratch_shapes=scratch(strip_rows)
        + [
            pltpu.VMEM((strip_rows, LANES), F32),
            pltpu.VMEM((strip_rows, LANES), jnp.int32),
            pltpu.VMEM((2 * WIDTH, NODES), BF16),
            pltpu.VMEM((2, HALO * WIDTH, NODES), BF16),
            pltpu.SemaphoreType.DMA((3,)),
        ],
        compiler_params=params,
    )(place, cell_scale, src2, orb2, base_potential, index, left, right, eig, stiffness, restrict_t,
      jnp.asarray(group_table(edge_cells), BF16), adjoint_mid, projected_mid)

    def exchanged(array, axes):
        return lax.all_to_all(array, axes, split_axis=0, concat_axis=0, tiled=True)

    tiles = exchanged(projected.reshape(X * COPIES, WIDTH, LANES), OUTER)
    tiles = jnp.sum(tiles.reshape(X, COPIES, WIDTH, LANES), axis=1)
    mine = lax.dynamic_slice(tiles, (x_at, 0, 0), (1, WIDTH, LANES), allow_negative_indices=False)
    gathered = exchanged(jnp.broadcast_to(mine, (Z, WIDTH, LANES)), ("z",))
    columns = pl.pallas_call(
        sum_kernel,
        out_shape=struct((X * HALF, LANES), F32),
        in_specs=[smem] + [vmem] * 3,
        out_specs=vmem,
        compiler_params=params,
    )(place, gathered.reshape(Z * WIDTH, LANES), tiles.reshape(X * WIDTH, LANES), jnp.asarray(unpack_table(), BF16))
    columns = exchanged(columns.reshape(X * COPIES, WIDTH, LANES), OUTER)
    updated, applied2 = pl.pallas_call(
        apply_kernel,
        out_shape=(struct((HALF, HALF), F32), struct((rows, NODES), BF16)),
        in_specs=[smem] + [vmem] * 8,
        out_specs=(vmem, vmem),
        compiler_params=params,
    )(place, columns.reshape(X * HALF, LANES), orb2, linear, ghost, left, right, index, prolong)
    return adjoint2.reshape(orbitals.shape), updated, applied2.reshape(orbitals.shape)


def solution(mesh):
    axes = jax.sharding.Mesh(mesh.devices.reshape(X, Z, Y, CORES), ("x", "z", "y", "core"))
    in_specs = (
        P(DOM, ORB, None),
        P(DOM, ORB, None),
        P(ORB),
        P(DOM),
        P(DOM, None),
        P(),
        P(DOM, None),
        P(),
        P(),
        P(DOM, None),
        P(DOM),
        P(DOM, None),
    )
    out_specs = (P(DOM, ORB, None), P(DOM, None), P(DOM, ORB, None))
    return jax.shard_map(local, mesh=axes, in_specs=in_specs, out_specs=out_specs, check_vma=False)
```

```python
import jax
import jax.numpy as jnp
import numpy as np
from jax import lax
from jax.experimental import pallas as pl
from jax.experimental.pallas import tpu as pltpu
from jax.sharding import PartitionSpec as P

ITERS = 4
relax = 0.25
step_rate = 0.1

LANES = 128
HALF = 64
NODES = 512
WIDTH = 8
CELLS = 48
HALO = 4
EXT = CELLS + 2 * HALO
F32, BF16 = jnp.float32, jnp.bfloat16


def dot(a, b, contract=((1,), (0,))):
    return lax.dot_general(a, b, (contract, ((), ())), preferred_element_type=F32)


def split(a):
    high = a.astype(BF16)
    return high, (a - high.astype(F32)).astype(BF16)


def lane_below(bound):
    return lax.broadcasted_iota(jnp.int32, (WIDTH, LANES), 1) < bound


SRC_ROWS, ORB_AT, BASE_AT, META_AT, HALO_ROWS = 32, 32, 40, 44, 48
IDX, SCALE, OWNER, SLOT = slice(0, 128), slice(128, 256), slice(256, 384), slice(384, 512)
POT, IDS, GHOST_IDS = CELLS, CELLS + HALF, CELLS + HALF + 12
X, Z, Y, CORES = 4, 16, 4, 2
DOM, ORB, OUTER = ("x", "z"), ("y", "core"), ("x", "y", "core")
COPIES = Y * CORES
STRIP = 3 * HALO
NT = ((1,), (1,))


def tile(e):
    return slice(e * WIDTH, (e + 1) * WIDTH)


def cols(t):
    return slice(t * LANES, (t + 1) * LANES)


def face_rows(perm, wanted_cells):
    twice = jnp.concatenate([perm, perm], 1).astype(F32)
    columns = jnp.transpose(twice)[0:HALF]
    node = lax.broadcasted_iota(jnp.int32, (HALF, LANES), 0).astype(F32)
    lane = lax.broadcasted_iota(jnp.int32, (HALF, LANES), 1).astype(F32)
    low = lax.broadcasted_iota(jnp.int32, (1, LANES), 1) < HALF
    rows = []
    for c in wanted_cells:
        inverse = jnp.sum(jnp.where(columns[:, c : c + 1] == lane, node, 0.0), axis=0, keepdims=True)
        rows.append(jnp.where(low, inverse + HALF, twice[c : c + 1]))
    return rows


def face_tiles(perm):
    half = CELLS // 2
    perm = perm.astype(F32)
    pairs = jnp.concatenate([perm[:half], perm[half:]], 1)
    twice = jnp.concatenate([perm, perm], 1)
    node = lax.broadcasted_iota(jnp.int32, (HALF, LANES), 0).astype(F32)
    row = lax.broadcasted_iota(jnp.int32, (WIDTH, LANES), 0)
    lane = lax.broadcasted_iota(jnp.int32, (WIDTH, LANES), 1)
    counts = jnp.where(lane // HALF == row, lane % HALF, 0).astype(F32).astype(BF16)
    empty = jnp.zeros((HALF, LANES), BF16)
    tiles = [None] * CELLS
    for p in range(half):
        hot = jnp.where(pairs[p : p + 1] == node, 1.0, 0.0).astype(BF16)
        inverse = dot(counts, jnp.concatenate([hot, empty], 0), NT)
        for i, c in enumerate((p, p + half)):
            rows = jnp.where(lane[:1] < HALF, inverse[i : i + 1] + HALF, twice[c : c + 1])
            tiles[c] = jnp.broadcast_to(rows.astype(jnp.int32), (WIDTH, LANES))
    return tiles


def in_hbm(array):
    return pltpu.with_memory_space_constraint(array, pltpu.HBM)


def pack_kernel(scale_hbm, owner_hbm, slot_hbm, src_hbm, orb_hbm, base_hbm, perm_hbm, stiff_hbm, eig_hbm,
                to_left, to_right, factor_out, eig_out, stiff_out, scale, owner, slot, src, orb, base, perm, eig, sems):
    top, rows = CELLS - WIDTH, CELLS * WIDTH
    copies = [(scale_hbm, scale), (owner_hbm, owner), (slot_hbm, slot)]
    for hbm, here, size, end in (
        (src_hbm, src, SRC_ROWS, rows), (orb_hbm, orb, 16, rows), (base_hbm, base, WIDTH, CELLS), (perm_hbm, perm, WIDTH, CELLS)
    ):
        copies.append((hbm.at[0:size], here.at[0]))
        copies.append((hbm.at[end - size : end], here.at[1]))
    copies += [(eig_hbm, eig), (stiff_hbm, stiff_out)]
    copies = [pltpu.make_async_copy(one, two, sems.at[i]) for i, (one, two) in enumerate(copies)]
    for copy in copies:
        copy.start()
    for copy in copies[:-1]:
        copy.wait()
    row = lax.broadcasted_iota(jnp.int32, (WIDTH, LANES), 0)
    eig_tile = jnp.zeros((WIDTH, LANES), F32)
    for i in range(WIDTH):
        eig_tile = jnp.where(row == i, eig[i], eig_tile)
    eig_out[...] = eig_tile
    for c in range(CELLS):
        factor_out[c : c + 1] = jnp.full((1, LANES), scale[c], F32)
    for end, out in enumerate((to_left, to_right)):
        inner, first = (0, 0) if end == 0 else (HALO, CELLS - HALO)
        edge_cell = end * (CELLS - 1)
        out[0:SRC_ROWS] = src[end].astype(F32)
        out[ORB_AT : ORB_AT + WIDTH] = orb[end].astype(F32)[tile(end)]
        out[BASE_AT : BASE_AT + HALO] = base[end, inner : inner + HALO]
        faces = face_rows(perm[end], range(inner, inner + HALO))
        for i in range(HALO):
            at = slice(META_AT + i, META_AT + i + 1)
            out[at, IDX] = faces[i]
            out[at, SCALE] = jnp.full((1, LANES), scale[first + i], F32)
            out[at, OWNER] = jnp.full((1, LANES), owner[edge_cell].astype(F32), F32)
            mark = slot[edge_cell].astype(F32) if i == end * (HALO - 1) else 1.0
            out[at, SLOT] = jnp.full((1, LANES), mark, F32)
    copies[-1].wait()


def relax_step(strips, x, quarter, shifted, kin, stiff, factor, index, gates):
    low = lane_below(HALF)
    held = [x[strip[0] * WIDTH : (strip[-1] + 1) * WIDTH].astype(BF16) for strip in strips]
    held = held[0] if len(held) == 1 else jnp.concatenate(held, 0)
    kin[0 : held.shape[0]] = dot(held, stiff[...])
    at = 0
    for strip in strips:
        part_before = new_before = None
        for e in strip:
            rows = tile(e)
            scale = factor(e)
            parts, news = [], []
            for t in range(4):
                here = x[rows, cols(t)]
                part = scale * kin[tile(at), cols(t)] + shifted[rows, cols(t)] * here
                parts.append(part)
                news.append(here + quarter[rows, cols(t)] - relax * part)
            at += 1
            if e > strip[0]:
                crossing = jnp.where(low, parts[0], part_before)
                moved = relax * jnp.take_along_axis(crossing, index[tile(e - 1)], axis=1, mode="promise_in_bounds")
                if e in gates:
                    moved = moved * gates[e]
                news[0] = jnp.where(low, news[0] - moved, news[0])
                x[tile(e - 1), cols(3)] = jnp.where(low, new_before, new_before - moved)
            for t in range(3):
                x[rows, cols(t)] = news[t]
            part_before, new_before = parts[3], news[3]
        x[tile(strip[-1]), cols(3)] = new_before


def group_of(row_cells):
    shape = (LANES, len(row_cells) * WIDTH)
    cell = lax.broadcasted_iota(jnp.int32, shape, 0)
    at = lax.broadcasted_iota(jnp.int32, shape, 1) // WIDTH
    gap = [i for i in range(1, len(row_cells)) if row_cells[i] != row_cells[i - 1] + 1]
    owner = at + row_cells[0]
    for i in gap:
        owner = owner + jnp.where(at >= i, row_cells[i] - row_cells[i - 1] - 1, 0)
    return jnp.where(cell == owner, 1.0, 0.0).astype(BF16)


def projection(orb_values, x_values, group, restrict_t):
    high, rest = split(orb_values.astype(F32) * x_values)
    density = dot(group, high) + dot(group, rest)
    high, rest = split(density)
    return dot(restrict_t, high, NT) + dot(restrict_t, rest, NT)


def interior_kernel(owner_hbm, slot_hbm, restrict_hbm, potential_hbm, src, orb, base, perm, factor, eig, stiff,
                    adjoint_out, projected_out, linear_out, index_out, restrict_t,
                    x, quarter, kin, shifted, owner, slot, potential, sems):
    pairs = ((restrict_hbm, restrict_t), (potential_hbm, potential), (owner_hbm, owner), (slot_hbm, slot))
    copies = [pltpu.make_async_copy(one, two, sems.at[i]) for i, (one, two) in enumerate(pairs)]
    for copy in copies:
        copy.start()
    quarter[...] = relax * src[...].astype(F32)
    x[...] = quarter[...]
    faces = face_tiles(perm[...])
    eig_tile = eig[...]

    def scale(c):
        return jnp.broadcast_to(factor[c : c + 1], (WIDTH, LANES))

    for c in range(CELLS):
        for t in range(4):
            shifted[tile(c), cols(t)] = base[c : c + 1, cols(t)] - eig_tile
        index_out[tile(c)] = faces[c]

    def step(_, carry):
        relax_step([range(CELLS)], x, quarter, shifted, kin, stiff, scale, index_out, {})
        return carry

    lax.fori_loop(0, ITERS, step, 0)
    for copy in copies:
        copy.wait()
    inner = slice(HALO * WIDTH, (CELLS - HALO) * WIDTH)
    adjoint_out[...] = x[inner].astype(BF16)
    kin[...] = dot(orb[...], stiff[...])
    for pair in range(CELLS // 2):
        values = orb[pair * 16 : pair * 16 + 16].astype(F32)
        for c in (2 * pair, 2 * pair + 1):
            for t in range(4):
                linear_out[tile(c), cols(t)] = (
                    scale(c) * kin[tile(c), cols(t)] + base[c : c + 1, cols(t)] * values[tile(c % 2), cols(t)]
                )
    row = lax.broadcasted_iota(jnp.int32, (WIDTH, LANES), 0)
    lane = lax.broadcasted_iota(jnp.int32, (WIDTH, LANES), 1)
    at = jnp.where((lane >= IDS) & (lane < GHOST_IDS), row * 12 + lane - IDS, -1)
    ids = jnp.zeros((WIDTH, LANES), F32)
    for c in range(CELLS):
        ids = jnp.where(at == c // 6 * 12 + c % 6, owner[c].astype(F32), ids)
        ids = jnp.where(at == c // 6 * 12 + 6 + c % 6, slot[c].astype(F32), ids)
    turned = jnp.transpose(potential[...])
    static = jnp.concatenate([jnp.zeros((HALF, CELLS), F32), turned, jnp.zeros((HALF, 16), F32)], 1)
    static = (static + jnp.concatenate([ids] * (HALF // WIDTH), 0)) * (1.0 / COPIES)
    projected_out[...] = static - step_rate * projection(
        orb[inner], x[inner], group_of(range(HALO, CELLS - HALO)), restrict_t[...]
    )


def boundary_kernel(src, orb, base, index_own, factor_own, eig, left, right, stiff, restrict_t, adjoint_mid, projected_mid,
                    adjoint_out, projected_out, ghost_out,
                    x, quarter, kin, shifted, factor, index, adjoint_ends, sems):
    near, edge = 2 * HALO * WIDTH, HALO * WIDTH
    last = CELLS * WIDTH
    copies = [
        pltpu.make_async_copy(adjoint_mid, adjoint_out.at[edge : last - edge], sems.at[0]),
        pltpu.make_async_copy(adjoint_ends.at[0], adjoint_out.at[0:edge], sems.at[1]),
        pltpu.make_async_copy(adjoint_ends.at[1], adjoint_out.at[last - edge : last], sems.at[2]),
    ]
    copies[0].start()
    quarter[0:edge] = relax * left[0:SRC_ROWS]
    quarter[edge : edge + near] = relax * src[0:near].astype(F32)
    quarter[edge + near : edge + 2 * near] = relax * src[last - near :].astype(F32)
    quarter[edge + 2 * near :] = relax * right[0:SRC_ROWS]
    x[...] = quarter[...]
    eig_tile = eig[...]
    for e in range(2 * STRIP):
        ghost = left if e < HALO else right if e >= 2 * STRIP - HALO else None
        if ghost is None:
            c = e - HALO if e < STRIP else CELLS - 2 * HALO + e - STRIP
            base_row = base[c : c + 1]
            factor[tile(e)] = jnp.broadcast_to(factor_own[c : c + 1], (WIDTH, LANES))
            index[tile(e)] = index_own[tile(c)]
        else:
            i = e if e < HALO else e - 2 * STRIP + HALO
            base_row = ghost[BASE_AT + i : BASE_AT + i + 1]
            meta_row = ghost[META_AT + i : META_AT + i + 1]
            factor[tile(e)] = jnp.broadcast_to(meta_row[:, SCALE], (WIDTH, LANES))
            index[tile(e)] = jnp.broadcast_to(meta_row[:, IDX].astype(jnp.int32), (WIDTH, LANES))
        for t in range(4):
            shifted[tile(e), cols(t)] = base_row[:, cols(t)] - eig_tile
    gates = {HALO: left[META_AT : META_AT + 1, SLOT], 2 * STRIP - HALO: right[HALO_ROWS - 1 : HALO_ROWS, SLOT]}
    for k in range(ITERS):
        strips = [range(k, STRIP - k), range(STRIP + k, 2 * STRIP - k)]
        relax_step(strips, x, quarter, shifted, kin, stiff, lambda e: factor[tile(e)], index, gates)
    low_cells, high_cells = x[edge : 2 * edge], x[4 * edge : 5 * edge]
    adjoint_ends[0] = low_cells.astype(BF16)
    adjoint_ends[1] = high_cells.astype(BF16)
    copies[1].start()
    copies[2].start()
    own_orb = jnp.concatenate([orb[0:edge], orb[last - edge :]], 0)
    own_x = jnp.concatenate([low_cells, high_cells], 0)
    lane = lax.broadcasted_iota(jnp.int32, (1, LANES), 1)
    ghost_ids = jnp.zeros((1, LANES), F32)
    for i, row in enumerate((left[META_AT + HALO - 1 : META_AT + HALO], right[META_AT : META_AT + 1])):
        ghost_ids = jnp.where(lane == GHOST_IDS + 2 * i, row[:, OWNER], ghost_ids)
        ghost_ids = jnp.where(lane == GHOST_IDS + 2 * i + 1, row[:, SLOT], ghost_ids)
    added = projection(own_orb, own_x, group_of([*range(HALO), *range(CELLS - HALO, CELLS)]), restrict_t[...])
    whole = projected_mid[...] + ghost_ids * (1.0 / COPIES) - step_rate * added
    for i in range(X):
        projected_out[i * HALF : (i + 1) * HALF] = whole
    ghosts = jnp.concatenate([left[ORB_AT : ORB_AT + WIDTH], right[ORB_AT : ORB_AT + WIDTH]], 0)
    ghost_kin = dot(ghosts.astype(BF16), stiff[...])
    for i, e, base_row in (
        (0, HALO - 1, left[BASE_AT + HALO - 1 : BASE_AT + HALO]),
        (1, 2 * STRIP - HALO, right[BASE_AT : BASE_AT + 1]),
    ):
        for t in range(4):
            ghost_out[tile(i), cols(t)] = (
                factor[tile(e)] * ghost_kin[tile(i), cols(t)] + base_row[:, cols(t)] * ghosts[tile(i), cols(t)]
            )
    for copy in copies:
        copy.wait()


def sum_kernel(place, gathered, asking, unpack, out):
    high, rest = split(gathered[...])
    ids = dot(jnp.concatenate([high, asking[...].astype(BF16)], 0), unpack[...])
    row = lax.broadcasted_iota(jnp.int32, ids.shape, 0) % WIDTH
    lane = lax.broadcasted_iota(jnp.int32, ids.shape, 1)
    ids = jnp.where(jnp.where(lane < CELLS, lane // 6, 0) == row, ids, 0.0)
    ids = jnp.sum(ids.reshape(Z + X, WIDTH, LANES), axis=1)
    lane = lax.broadcasted_iota(jnp.int32, ids.shape, 1)
    row = lax.broadcasted_iota(jnp.int32, ids.shape, 0)
    mine = jnp.where(row < Z, place[0:1], place[1:2])
    slots = mine + (jnp.where(row < Z, row, (row - Z) * Z) * HALF + lane - POT).astype(F32)
    ids = jnp.where((lane >= POT) & (lane < IDS), slots, ids)
    known = jnp.where(lane[:Z] < IDS, ids[:Z], -1.0)
    wanted = jnp.where(lane[Z:] < IDS + 2, ids[Z:], -2.0)
    known = jnp.transpose(jnp.concatenate([known, jnp.zeros((LANES - Z, LANES), F32)], 0))
    total = jnp.zeros((2 * WIDTH, X * LANES), F32)
    for s in range(0, Z, 2):
        hot = [
            jnp.concatenate(
                [jnp.where(known[:, i : i + 1] == wanted[m : m + 1], 1.0, 0.0).astype(BF16) for m in range(X)], 1
            )
            for i in (s, s + 1)
        ]
        both = [jnp.concatenate([high[tile(i)], rest[tile(i)]], 0) for i in (s, s + 1)]
        total = total + dot(jnp.concatenate(both, 1), jnp.concatenate(hot, 0))
    result = total[:WIDTH] + total[WIDTH:]
    for m in range(X):
        for i in range(COPIES):
            out[tile(m * COPIES + i)] = result[:, cols(m)]


def apply_kernel(columns, orb, linear, ghost, left, right, index, prolong, updated_out, applied_out):
    summed = columns[0:HALF]
    for i in range(1, X):
        summed = summed + columns[i * HALF : (i + 1) * HALF]
    table = jnp.transpose(summed)
    updated_out[...] = table[POT:IDS]
    high, rest = split(table)
    node = dot(high, prolong[...]) + dot(rest, prolong[...])
    low = lane_below(HALF)
    part_before = new_before = index_before = None
    finished = []
    for e in range(CELLS + 2):
        c = e - 1
        if e == 0:
            values, start, node_at = left[ORB_AT : ORB_AT + WIDTH], ghost[tile(0)], IDS
        elif e <= CELLS:
            values = orb[c // 2 * 16 : c // 2 * 16 + 16].astype(F32)[tile(c % 2)]
            start, node_at = linear[tile(c)], c
        else:
            values, start, node_at = right[ORB_AT : ORB_AT + WIDTH], ghost[tile(1)], IDS + 1
        whole = start + node[node_at : node_at + 1] * values
        parts = [whole[:, cols(t)] for t in range(4)]
        if e > 0:
            crossing = jnp.where(low, parts[0], part_before)
            moved = jnp.take_along_axis(crossing, index_before, axis=1, mode="promise_in_bounds")
            if e == 1:
                moved = moved * left[META_AT : META_AT + 1, SLOT]
            if e == CELLS + 1:
                moved = moved * right[HALO_ROWS - 1 : HALO_ROWS, SLOT]
            done = jnp.where(low, new_before[3], new_before[3] + moved)
            if e > 1:
                finished.append(jnp.concatenate([*new_before[:3], done], 1))
            news = [jnp.where(low, parts[0] + moved, parts[0]), *parts[1:]]
        else:
            news = parts
        part_before, new_before = parts[3], news
        if e == 0:
            meta_row = left[META_AT + HALO - 1 : META_AT + HALO]
            index_before = jnp.broadcast_to(meta_row[:, IDX].astype(jnp.int32), (WIDTH, LANES))
        elif e <= CELLS:
            index_before = index[tile(c)]
        if len(finished) == 2:
            applied_out[(e - 3) * WIDTH : (e - 1) * WIDTH] = jnp.concatenate(finished, 0).astype(BF16)
            finished = []


def unpack_table():
    table = np.zeros((LANES, LANES), np.float32)
    for k in range(CELLS):
        table[112 + k % 6, k] = 64.0
        table[118 + k % 6, k] = 1.0
    for i in range(2):
        table[GHOST_IDS + 2 * i, IDS + i] = 64.0
        table[GHOST_IDS + 2 * i + 1, IDS + i] = 1.0
    return table


def local(orbitals, adjoint_source, eigenvalues, cell_scale, base_potential, stiffness, face_perm, restrict,
          prolong, owner, pot_slot, potential):
    x_at, z_at = lax.axis_index("x"), lax.axis_index("z")
    vmem = pl.BlockSpec(memory_space=pltpu.VMEM)
    params = pltpu.CompilerParams(vmem_limit_bytes=32 * 2**20)
    struct = jax.ShapeDtypeStruct

    orb2 = orbitals.reshape(CELLS * WIDTH, NODES)
    src2 = adjoint_source.reshape(CELLS * WIDTH, NODES)
    owner1 = owner.reshape(CELLS)
    first = jnp.stack([x_at * Z, z_at]) * HALF
    place = jnp.broadcast_to(first.astype(F32)[:, None], (2, LANES))

    hbm = pl.BlockSpec(memory_space=pltpu.HBM)
    to_left, to_right, factor, eig, stiff = pl.pallas_call(
        pack_kernel,
        out_shape=(
            struct((HALO_ROWS, NODES), F32),
            struct((HALO_ROWS, NODES), F32),
            struct((CELLS, LANES), F32),
            struct((WIDTH, LANES), F32),
            struct((NODES, NODES), BF16),
        ),
        in_specs=[hbm] * 9,
        out_specs=(vmem,) * 5,
        scratch_shapes=[
            pltpu.SMEM((CELLS,), F32),
            pltpu.SMEM((CELLS,), jnp.int32),
            pltpu.SMEM((CELLS,), jnp.int32),
            pltpu.VMEM((2, SRC_ROWS, NODES), BF16),
            pltpu.VMEM((2, 16, NODES), BF16),
            pltpu.VMEM((2, WIDTH, NODES), F32),
            pltpu.VMEM((2, WIDTH, HALF), jnp.int32),
            pltpu.SMEM((WIDTH,), F32),
            pltpu.SemaphoreType.DMA((13,)),
        ],
        compiler_params=params,
    )(*map(in_hbm, (cell_scale, owner1, pot_slot, src2, orb2, base_potential, face_perm, stiffness, eigenvalues)))

    ahead = [(i, i + 1) for i in range(X * Z - 1)]
    left = lax.ppermute(to_right, DOM, ahead)
    right = lax.ppermute(to_left, DOM, [(b, a) for a, b in ahead])

    rows = CELLS * WIDTH
    inner = rows - 2 * HALO * WIDTH
    adjoint_mid, projected_mid, linear, index, restrict_t = pl.pallas_call(
        interior_kernel,
        out_shape=(
            struct((inner, NODES), BF16),
            struct((HALF, LANES), F32),
            struct((rows, NODES), F32),
            struct((rows, LANES), jnp.int32),
            struct((HALF, NODES), BF16),
        ),
        in_specs=[hbm] * 4 + [vmem] * 7,
        out_specs=(vmem,) * 5,
        scratch_shapes=[pltpu.VMEM((rows, NODES), F32)] * 4
        + [
            pltpu.SMEM((CELLS,), jnp.int32),
            pltpu.SMEM((CELLS,), jnp.int32),
            pltpu.VMEM((HALF, HALF), F32),
            pltpu.SemaphoreType.DMA((4,)),
        ],
        compiler_params=params,
        cost_estimate=pl.CostEstimate(flops=5 * 2 * rows * NODES * NODES, bytes_accessed=4 * 2**20, transcendentals=0),
    )(*map(in_hbm, (owner1, pot_slot, restrict.T, potential)), src2, orb2, base_potential, face_perm, factor, eig, stiff)

    strip_rows = 2 * STRIP * WIDTH
    adjoint2, projected, ghost = pl.pallas_call(
        boundary_kernel,
        out_shape=(
            struct((rows, NODES), BF16),
            struct((X * HALF, LANES), F32),
            struct((2 * WIDTH, NODES), F32),
        ),
        in_specs=[vmem] * 12,
        out_specs=(hbm, vmem, vmem),
        scratch_shapes=[pltpu.VMEM((strip_rows, NODES), F32)] * 4
        + [
            pltpu.VMEM((strip_rows, LANES), F32),
            pltpu.VMEM((strip_rows, LANES), jnp.int32),
            pltpu.VMEM((2, HALO * WIDTH, NODES), BF16),
            pltpu.SemaphoreType.DMA((3,)),
        ],
        compiler_params=params,
    )(src2, orb2, base_potential, index, factor, eig, left, right, stiff, restrict_t, adjoint_mid, projected_mid)

    def exchanged(array, axes):
        return lax.all_to_all(array, axes, split_axis=0, concat_axis=0, tiled=True)

    projected, place, x_at = lax.optimization_barrier((projected, place, x_at))
    tiles = exchanged(projected.reshape(X * COPIES, WIDTH, LANES), OUTER)
    tiles = jnp.sum(tiles.reshape(X, COPIES, WIDTH, LANES), axis=1)
    mine = lax.dynamic_slice(tiles, (x_at, 0, 0), (1, WIDTH, LANES), allow_negative_indices=False)
    gathered = exchanged(jnp.broadcast_to(mine, (Z, WIDTH, LANES)), ("z",))
    columns = pl.pallas_call(
        sum_kernel,
        out_shape=struct((X * HALF, LANES), F32),
        in_specs=[vmem] * 4,
        out_specs=vmem,
        compiler_params=params,
    )(place, gathered.reshape(Z * WIDTH, LANES), tiles.reshape(X * WIDTH, LANES), jnp.asarray(unpack_table(), BF16))
    columns = exchanged(columns.reshape(X * COPIES, WIDTH, LANES), OUTER)
    updated, applied2 = pl.pallas_call(
        apply_kernel,
        out_shape=(struct((HALF, HALF), F32), struct((rows, NODES), BF16)),
        in_specs=[vmem] * 8,
        out_specs=(vmem, vmem),
        compiler_params=params,
    )(columns.reshape(X * HALF, LANES), orb2, linear, ghost, left, right, index, prolong)
    return adjoint2.reshape(orbitals.shape), updated, applied2.reshape(orbitals.shape)


def solution(mesh):
    axes = jax.sharding.Mesh(mesh.devices.reshape(X, Z, Y, CORES), ("x", "z", "y", "core"))
    in_specs = (
        P(DOM, ORB, None),
        P(DOM, ORB, None),
        P(ORB),
        P(DOM),
        P(DOM, None),
        P(),
        P(DOM, None),
        P(),
        P(),
        P(DOM, None),
        P(DOM),
        P(DOM, None),
    )
    out_specs = (P(DOM, ORB, None), P(DOM, None), P(DOM, ORB, None))
    return jax.shard_map(local, mesh=axes, in_specs=in_specs, out_specs=out_specs, check_vma=False)
```

```python
import jax
import jax.numpy as jnp
import numpy as np
from jax import lax
from jax.experimental import pallas as pl
from jax.experimental.pallas import tpu as pltpu
from jax.sharding import PartitionSpec as P

ITERS = 4
relax = 0.25
step_rate = 0.1

LANES = 128
HALF = 64
NODES = 512
WIDTH = 8
CELLS = 48
HALO = 4
EXT = CELLS + 2 * HALO
F32, BF16 = jnp.float32, jnp.bfloat16


def dot(a, b, contract=((1,), (0,))):
    return lax.dot_general(a, b, (contract, ((), ())), preferred_element_type=F32)


def split(a):
    high = a.astype(BF16)
    return high, (a - high.astype(F32)).astype(BF16)


def lane_below(bound):
    return lax.broadcasted_iota(jnp.int32, (WIDTH, LANES), 1) < bound


SRC_ROWS, ORB_AT, BASE_AT, META_AT, HALO_ROWS = 32, 32, 40, 44, 48
IDX, SCALE, OWNER, SLOT = slice(0, 128), slice(128, 256), slice(256, 384), slice(384, 512)
POT, IDS, GHOST_IDS = CELLS, CELLS + HALF, CELLS + HALF + 12
X, Z, Y, CORES = 4, 16, 4, 2
DOM, ORB, OUTER = ("x", "z"), ("y", "core"), ("x", "y", "core")
COPIES = Y * CORES
STRIP = 3 * HALO
NT = ((1,), (1,))


def tile(e):
    return slice(e * WIDTH, (e + 1) * WIDTH)


def cols(t):
    return slice(t * LANES, (t + 1) * LANES)


def face_rows(perm, wanted_cells):
    twice = jnp.concatenate([perm, perm], 1).astype(F32)
    columns = jnp.transpose(twice)[0:HALF]
    node = lax.broadcasted_iota(jnp.int32, (HALF, LANES), 0).astype(F32)
    lane = lax.broadcasted_iota(jnp.int32, (HALF, LANES), 1).astype(F32)
    low = lax.broadcasted_iota(jnp.int32, (1, LANES), 1) < HALF
    rows = []
    for c in wanted_cells:
        inverse = jnp.sum(jnp.where(columns[:, c : c + 1] == lane, node, 0.0), axis=0, keepdims=True)
        rows.append(jnp.where(low, inverse + HALF, twice[c : c + 1]))
    return rows


def face_tiles(perm):
    half = CELLS // 2
    perm = perm.astype(F32)
    pairs = jnp.concatenate([perm[:half], perm[half:]], 1)
    twice = jnp.concatenate([perm, perm], 1)
    node = lax.broadcasted_iota(jnp.int32, (HALF, LANES), 0).astype(F32)
    row = lax.broadcasted_iota(jnp.int32, (WIDTH, LANES), 0)
    lane = lax.broadcasted_iota(jnp.int32, (WIDTH, LANES), 1)
    counts = jnp.where(lane // HALF == row, lane % HALF, 0).astype(F32).astype(BF16)
    empty = jnp.zeros((HALF, LANES), BF16)
    tiles = [None] * CELLS
    for p in range(half):
        hot = jnp.where(pairs[p : p + 1] == node, 1.0, 0.0).astype(BF16)
        inverse = dot(counts, jnp.concatenate([hot, empty], 0), NT)
        for i, c in enumerate((p, p + half)):
            rows = jnp.where(lane[:1] < HALF, inverse[i : i + 1] + HALF, twice[c : c + 1])
            tiles[c] = jnp.broadcast_to(rows.astype(jnp.int32), (WIDTH, LANES))
    return tiles


def in_hbm(array):
    return pltpu.with_memory_space_constraint(array, pltpu.HBM)


def pack_kernel(scale_hbm, owner_hbm, slot_hbm, src_hbm, orb_hbm, base_hbm, perm_hbm, stiff_hbm, eig_hbm,
                to_left, to_right, factor_out, eig_out, stiff_out, scale, owner, slot, src, orb, base, perm, eig, sems):
    top, rows = CELLS - WIDTH, CELLS * WIDTH
    copies = [(scale_hbm, scale), (owner_hbm, owner), (slot_hbm, slot)]
    for hbm, here, size, end in (
        (src_hbm, src, SRC_ROWS, rows), (orb_hbm, orb, 16, rows), (base_hbm, base, WIDTH, CELLS), (perm_hbm, perm, WIDTH, CELLS)
    ):
        copies.append((hbm.at[0:size], here.at[0]))
        copies.append((hbm.at[end - size : end], here.at[1]))
    copies += [(eig_hbm, eig), (stiff_hbm, stiff_out)]
    copies = [pltpu.make_async_copy(one, two, sems.at[i]) for i, (one, two) in enumerate(copies)]
    for copy in copies:
        copy.start()
    for copy in copies[:-1]:
        copy.wait()
    row = lax.broadcasted_iota(jnp.int32, (WIDTH, LANES), 0)
    eig_tile = jnp.zeros((WIDTH, LANES), F32)
    for i in range(WIDTH):
        eig_tile = jnp.where(row == i, eig[i], eig_tile)
    eig_out[...] = eig_tile
    for c in range(CELLS):
        factor_out[c : c + 1] = jnp.full((1, LANES), scale[c], F32)
    for end, out in enumerate((to_left, to_right)):
        inner, first = (0, 0) if end == 0 else (HALO, CELLS - HALO)
        edge_cell = end * (CELLS - 1)
        out[0:SRC_ROWS] = src[end].astype(F32)
        out[ORB_AT : ORB_AT + WIDTH] = orb[end].astype(F32)[tile(end)]
        out[BASE_AT : BASE_AT + HALO] = base[end, inner : inner + HALO]
        faces = face_rows(perm[end], range(inner, inner + HALO))
        for i in range(HALO):
            at = slice(META_AT + i, META_AT + i + 1)
            out[at, IDX] = faces[i]
            out[at, SCALE] = jnp.full((1, LANES), scale[first + i], F32)
            out[at, OWNER] = jnp.full((1, LANES), owner[edge_cell].astype(F32), F32)
            mark = slot[edge_cell].astype(F32) if i == end * (HALO - 1) else 1.0
            out[at, SLOT] = jnp.full((1, LANES), mark, F32)
    copies[-1].wait()


def relax_step(strips, x, quarter, shifted, kin, stiff, factor, index, gates):
    low = lane_below(HALF)
    held = [x[strip[0] * WIDTH : (strip[-1] + 1) * WIDTH].astype(BF16) for strip in strips]
    held = held[0] if len(held) == 1 else jnp.concatenate(held, 0)
    kin[0 : held.shape[0]] = dot(held, stiff[...])
    at = 0
    for strip in strips:
        part_before = new_before = None
        for e in strip:
            rows = tile(e)
            scale = factor(e)
            parts, news = [], []
            for t in range(4):
                here = x[rows, cols(t)]
                part = scale * kin[tile(at), cols(t)] + shifted[rows, cols(t)] * here
                parts.append(part)
                news.append(here + quarter[rows, cols(t)] - relax * part)
            at += 1
            if e > strip[0]:
                crossing = jnp.where(low, parts[0], part_before)
                moved = relax * jnp.take_along_axis(crossing, index[tile(e - 1)], axis=1, mode="promise_in_bounds")
                if e in gates:
                    moved = moved * gates[e]
                news[0] = jnp.where(low, news[0] - moved, news[0])
                x[tile(e - 1), cols(3)] = jnp.where(low, new_before, new_before - moved)
            for t in range(3):
                x[rows, cols(t)] = news[t]
            part_before, new_before = parts[3], news[3]
        x[tile(strip[-1]), cols(3)] = new_before


def group_of(row_cells):
    shape = (LANES, len(row_cells) * WIDTH)
    cell = lax.broadcasted_iota(jnp.int32, shape, 0)
    at = lax.broadcasted_iota(jnp.int32, shape, 1) // WIDTH
    gap = [i for i in range(1, len(row_cells)) if row_cells[i] != row_cells[i - 1] + 1]
    owner = at + row_cells[0]
    for i in gap:
        owner = owner + jnp.where(at >= i, row_cells[i] - row_cells[i - 1] - 1, 0)
    return jnp.where(cell == owner, 1.0, 0.0).astype(BF16)


def projection(orb_values, x_values, group, restrict_t):
    high, rest = split(orb_values.astype(F32) * x_values)
    density = dot(group, high) + dot(group, rest)
    high, rest = split(density)
    return dot(restrict_t, high, NT) + dot(restrict_t, rest, NT)


def interior_kernel(owner_hbm, slot_hbm, restrict_hbm, potential_hbm, src, orb, base, perm, factor, eig, stiff,
                    adjoint_out, projected_out, linear_out, index_out, restrict_t,
                    x, quarter, kin, shifted, owner, slot, potential, sems):
    pairs = ((restrict_hbm, restrict_t), (potential_hbm, potential), (owner_hbm, owner), (slot_hbm, slot))
    copies = [pltpu.make_async_copy(one, two, sems.at[i]) for i, (one, two) in enumerate(pairs)]
    for copy in copies:
        copy.start()
    quarter[...] = relax * src[...].astype(F32)
    x[...] = quarter[...]
    faces = face_tiles(perm[...])
    eig_tile = eig[...]

    def scale(c):
        return jnp.broadcast_to(factor[c : c + 1], (WIDTH, LANES))

    for c in range(CELLS):
        for t in range(4):
            shifted[tile(c), cols(t)] = base[c : c + 1, cols(t)] - eig_tile
        index_out[tile(c)] = faces[c]

    def step(_, carry):
        relax_step([range(CELLS)], x, quarter, shifted, kin, stiff, scale, index_out, {})
        return carry

    lax.fori_loop(0, ITERS, step, 0)
    for copy in copies:
        copy.wait()
    inner = slice(HALO * WIDTH, (CELLS - HALO) * WIDTH)
    adjoint_out[...] = x[inner].astype(BF16)
    kin[...] = dot(orb[...], stiff[...])
    for pair in range(CELLS // 2):
        values = orb[pair * 16 : pair * 16 + 16].astype(F32)
        for c in (2 * pair, 2 * pair + 1):
            for t in range(4):
                linear_out[tile(c), cols(t)] = (
                    scale(c) * kin[tile(c), cols(t)] + base[c : c + 1, cols(t)] * values[tile(c % 2), cols(t)]
                )
    row = lax.broadcasted_iota(jnp.int32, (WIDTH, LANES), 0)
    lane = lax.broadcasted_iota(jnp.int32, (WIDTH, LANES), 1)
    at = jnp.where((lane >= IDS) & (lane < GHOST_IDS), row * 12 + lane - IDS, -1)
    ids = jnp.zeros((WIDTH, LANES), F32)
    for c in range(CELLS):
        ids = jnp.where(at == c // 6 * 12 + c % 6, owner[c].astype(F32), ids)
        ids = jnp.where(at == c // 6 * 12 + 6 + c % 6, slot[c].astype(F32), ids)
    turned = jnp.transpose(potential[...])
    static = jnp.concatenate([jnp.zeros((HALF, CELLS), F32), turned, jnp.zeros((HALF, 16), F32)], 1)
    static = (static + jnp.concatenate([ids] * (HALF // WIDTH), 0)) * (1.0 / COPIES)
    projected_out[...] = static - step_rate * projection(
        orb[inner], x[inner], group_of(range(HALO, CELLS - HALO)), restrict_t[...]
    )


def boundary_kernel(src, orb, base, index_own, factor_own, eig, left, right, stiff, restrict_t, adjoint_mid, projected_mid,
                    adjoint_out, projected_out, ghost_out,
                    x, quarter, kin, shifted, factor, index, adjoint_ends, sems):
    near, edge = 2 * HALO * WIDTH, HALO * WIDTH
    last = CELLS * WIDTH
    copies = [
        pltpu.make_async_copy(adjoint_mid, adjoint_out.at[edge : last - edge], sems.at[0]),
        pltpu.make_async_copy(adjoint_ends.at[0], adjoint_out.at[0:edge], sems.at[1]),
        pltpu.make_async_copy(adjoint_ends.at[1], adjoint_out.at[last - edge : last], sems.at[2]),
    ]
    copies[0].start()
    quarter[0:edge] = relax * left[0:SRC_ROWS]
    quarter[edge : edge + near] = relax * src[0:near].astype(F32)
    quarter[edge + near : edge + 2 * near] = relax * src[last - near :].astype(F32)
    quarter[edge + 2 * near :] = relax * right[0:SRC_ROWS]
    x[...] = quarter[...]
    eig_tile = eig[...]
    for e in range(2 * STRIP):
        ghost = left if e < HALO else right if e >= 2 * STRIP - HALO else None
        if ghost is None:
            c = e - HALO if e < STRIP else CELLS - 2 * HALO + e - STRIP
            base_row = base[c : c + 1]
            factor[tile(e)] = jnp.broadcast_to(factor_own[c : c + 1], (WIDTH, LANES))
            index[tile(e)] = index_own[tile(c)]
        else:
            i = e if e < HALO else e - 2 * STRIP + HALO
            base_row = ghost[BASE_AT + i : BASE_AT + i + 1]
            meta_row = ghost[META_AT + i : META_AT + i + 1]
            factor[tile(e)] = jnp.broadcast_to(meta_row[:, SCALE], (WIDTH, LANES))
            index[tile(e)] = jnp.broadcast_to(meta_row[:, IDX].astype(jnp.int32), (WIDTH, LANES))
        for t in range(4):
            shifted[tile(e), cols(t)] = base_row[:, cols(t)] - eig_tile
    gates = {HALO: left[META_AT : META_AT + 1, SLOT], 2 * STRIP - HALO: right[HALO_ROWS - 1 : HALO_ROWS, SLOT]}
    for k in range(ITERS):
        strips = [range(k, STRIP - k), range(STRIP + k, 2 * STRIP - k)]
        relax_step(strips, x, quarter, shifted, kin, stiff, lambda e: factor[tile(e)], index, gates)
    low_cells, high_cells = x[edge : 2 * edge], x[4 * edge : 5 * edge]
    adjoint_ends[0] = low_cells.astype(BF16)
    adjoint_ends[1] = high_cells.astype(BF16)
    copies[1].start()
    copies[2].start()
    own_orb = jnp.concatenate([orb[0:edge], orb[last - edge :]], 0)
    own_x = jnp.concatenate([low_cells, high_cells], 0)
    lane = lax.broadcasted_iota(jnp.int32, (1, LANES), 1)
    ghost_ids = jnp.zeros((1, LANES), F32)
    for i, row in enumerate((left[META_AT + HALO - 1 : META_AT + HALO], right[META_AT : META_AT + 1])):
        ghost_ids = jnp.where(lane == GHOST_IDS + 2 * i, row[:, OWNER], ghost_ids)
        ghost_ids = jnp.where(lane == GHOST_IDS + 2 * i + 1, row[:, SLOT], ghost_ids)
    added = projection(own_orb, own_x, group_of([*range(HALO), *range(CELLS - HALO, CELLS)]), restrict_t[...])
    whole = projected_mid[...] + ghost_ids * (1.0 / COPIES) - step_rate * added
    for i in range(X):
        projected_out[i * HALF : (i + 1) * HALF] = whole
    ghosts = jnp.concatenate([left[ORB_AT : ORB_AT + WIDTH], right[ORB_AT : ORB_AT + WIDTH]], 0)
    ghost_kin = dot(ghosts.astype(BF16), stiff[...])
    for i, e, base_row in (
        (0, HALO - 1, left[BASE_AT + HALO - 1 : BASE_AT + HALO]),
        (1, 2 * STRIP - HALO, right[BASE_AT : BASE_AT + 1]),
    ):
        for t in range(4):
            ghost_out[tile(i), cols(t)] = (
                factor[tile(e)] * ghost_kin[tile(i), cols(t)] + base_row[:, cols(t)] * ghosts[tile(i), cols(t)]
            )
    for copy in copies:
        copy.wait()


def sum_kernel(place, gathered, asking, unpack, out):
    high, rest = split(gathered[...])
    ids = dot(jnp.concatenate([high, asking[...].astype(BF16)], 0), unpack[...])
    row = lax.broadcasted_iota(jnp.int32, ids.shape, 0) % WIDTH
    lane = lax.broadcasted_iota(jnp.int32, ids.shape, 1)
    ids = jnp.where(jnp.where(lane < CELLS, lane // 6, 0) == row, ids, 0.0)
    ids = jnp.sum(ids.reshape(X * Z + 1, WIDTH, LANES), axis=1)
    known, wanted = ids[: X * Z], ids[X * Z :]
    lane = lax.broadcasted_iota(jnp.int32, known.shape, 1)
    row = lax.broadcasted_iota(jnp.int32, known.shape, 0)
    slots = ((row % X * Z + row // X) * HALF + lane - POT).astype(F32)
    known = jnp.where(lane < POT, known, jnp.where(lane < IDS, slots, -1.0))
    lane = lane[:1]
    wanted = jnp.where((lane >= POT) & (lane < IDS), place[...] + (lane - POT).astype(F32), wanted)
    wanted = jnp.where(lane < IDS + 2, wanted, -2.0)
    wanted = jnp.transpose(jnp.broadcast_to(wanted, (LANES, LANES)))
    total = jnp.zeros((2 * WIDTH, LANES), F32)
    for s in range(0, X * Z, 2):
        hot = [jnp.where(wanted == known[i : i + 1], 1.0, 0.0).astype(BF16) for i in (s, s + 1)]
        both = [jnp.concatenate([high[tile(i)], rest[tile(i)]], 0) for i in (s, s + 1)]
        total = total + dot(jnp.concatenate(both, 1), jnp.concatenate(hot, 1), NT)
    result = total[:WIDTH] + total[WIDTH:]
    for i in range(COPIES):
        out[tile(i)] = result


def apply_kernel(columns, orb, linear, ghost, left, right, index, prolong, updated_out, applied_out):
    table = jnp.transpose(columns[...])
    updated_out[...] = table[POT:IDS]
    high, rest = split(table)
    node = dot(high, prolong[...]) + dot(rest, prolong[...])
    low = lane_below(HALF)
    part_before = new_before = index_before = None
    finished = []
    for e in range(CELLS + 2):
        c = e - 1
        if e == 0:
            values, start, node_at = left[ORB_AT : ORB_AT + WIDTH], ghost[tile(0)], IDS
        elif e <= CELLS:
            values = orb[c // 2 * 16 : c // 2 * 16 + 16].astype(F32)[tile(c % 2)]
            start, node_at = linear[tile(c)], c
        else:
            values, start, node_at = right[ORB_AT : ORB_AT + WIDTH], ghost[tile(1)], IDS + 1
        whole = start + node[node_at : node_at + 1] * values
        parts = [whole[:, cols(t)] for t in range(4)]
        if e > 0:
            crossing = jnp.where(low, parts[0], part_before)
            moved = jnp.take_along_axis(crossing, index_before, axis=1, mode="promise_in_bounds")
            if e == 1:
                moved = moved * left[META_AT : META_AT + 1, SLOT]
            if e == CELLS + 1:
                moved = moved * right[HALO_ROWS - 1 : HALO_ROWS, SLOT]
            done = jnp.where(low, new_before[3], new_before[3] + moved)
            if e > 1:
                finished.append(jnp.concatenate([*new_before[:3], done], 1))
            news = [jnp.where(low, parts[0] + moved, parts[0]), *parts[1:]]
        else:
            news = parts
        part_before, new_before = parts[3], news
        if e == 0:
            meta_row = left[META_AT + HALO - 1 : META_AT + HALO]
            index_before = jnp.broadcast_to(meta_row[:, IDX].astype(jnp.int32), (WIDTH, LANES))
        elif e <= CELLS:
            index_before = index[tile(c)]
        if len(finished) == 2:
            applied_out[(e - 3) * WIDTH : (e - 1) * WIDTH] = jnp.concatenate(finished, 0).astype(BF16)
            finished = []


def unpack_table():
    table = np.zeros((LANES, LANES), np.float32)
    for k in range(CELLS):
        table[112 + k % 6, k] = 64.0
        table[118 + k % 6, k] = 1.0
    for i in range(2):
        table[GHOST_IDS + 2 * i, IDS + i] = 64.0
        table[GHOST_IDS + 2 * i + 1, IDS + i] = 1.0
    return table


def local(orbitals, adjoint_source, eigenvalues, cell_scale, base_potential, stiffness, face_perm, restrict,
          prolong, owner, pot_slot, potential):
    x_at, z_at = lax.axis_index("x"), lax.axis_index("z")
    vmem = pl.BlockSpec(memory_space=pltpu.VMEM)
    params = pltpu.CompilerParams(vmem_limit_bytes=32 * 2**20)
    struct = jax.ShapeDtypeStruct

    orb2 = orbitals.reshape(CELLS * WIDTH, NODES)
    src2 = adjoint_source.reshape(CELLS * WIDTH, NODES)
    owner1 = owner.reshape(CELLS)
    place = jnp.full((1, LANES), ((x_at * Z + z_at) * HALF).astype(F32))

    hbm = pl.BlockSpec(memory_space=pltpu.HBM)
    to_left, to_right, factor, eig, stiff = pl.pallas_call(
        pack_kernel,
        out_shape=(
            struct((HALO_ROWS, NODES), F32),
            struct((HALO_ROWS, NODES), F32),
            struct((CELLS, LANES), F32),
            struct((WIDTH, LANES), F32),
            struct((NODES, NODES), BF16),
        ),
        in_specs=[hbm] * 9,
        out_specs=(vmem,) * 5,
        scratch_shapes=[
            pltpu.SMEM((CELLS,), F32),
            pltpu.SMEM((CELLS,), jnp.int32),
            pltpu.SMEM((CELLS,), jnp.int32),
            pltpu.VMEM((2, SRC_ROWS, NODES), BF16),
            pltpu.VMEM((2, 16, NODES), BF16),
            pltpu.VMEM((2, WIDTH, NODES), F32),
            pltpu.VMEM((2, WIDTH, HALF), jnp.int32),
            pltpu.SMEM((WIDTH,), F32),
            pltpu.SemaphoreType.DMA((13,)),
        ],
        compiler_params=params,
    )(*map(in_hbm, (cell_scale, owner1, pot_slot, src2, orb2, base_potential, face_perm, stiffness, eigenvalues)))

    ahead = [(i, i + 1) for i in range(X * Z - 1)]
    left = lax.ppermute(to_right, DOM, ahead)
    right = lax.ppermute(to_left, DOM, [(b, a) for a, b in ahead])

    rows = CELLS * WIDTH
    inner = rows - 2 * HALO * WIDTH
    adjoint_mid, projected_mid, linear, index, restrict_t = pl.pallas_call(
        interior_kernel,
        out_shape=(
            struct((inner, NODES), BF16),
            struct((HALF, LANES), F32),
            struct((rows, NODES), F32),
            struct((rows, LANES), jnp.int32),
            struct((HALF, NODES), BF16),
        ),
        in_specs=[hbm] * 4 + [vmem] * 7,
        out_specs=(vmem,) * 5,
        scratch_shapes=[pltpu.VMEM((rows, NODES), F32)] * 4
        + [
            pltpu.SMEM((CELLS,), jnp.int32),
            pltpu.SMEM((CELLS,), jnp.int32),
            pltpu.VMEM((HALF, HALF), F32),
            pltpu.SemaphoreType.DMA((4,)),
        ],
        compiler_params=params,
        cost_estimate=pl.CostEstimate(flops=5 * 2 * rows * NODES * NODES, bytes_accessed=4 * 2**20, transcendentals=0),
    )(*map(in_hbm, (owner1, pot_slot, restrict.T, potential)), src2, orb2, base_potential, face_perm, factor, eig, stiff)

    strip_rows = 2 * STRIP * WIDTH
    adjoint2, projected, ghost = pl.pallas_call(
        boundary_kernel,
        out_shape=(
            struct((rows, NODES), BF16),
            struct((X * HALF, LANES), F32),
            struct((2 * WIDTH, NODES), F32),
        ),
        in_specs=[vmem] * 12,
        out_specs=(hbm, vmem, vmem),
        scratch_shapes=[pltpu.VMEM((strip_rows, NODES), F32)] * 4
        + [
            pltpu.VMEM((strip_rows, LANES), F32),
            pltpu.VMEM((strip_rows, LANES), jnp.int32),
            pltpu.VMEM((2, HALO * WIDTH, NODES), BF16),
            pltpu.SemaphoreType.DMA((3,)),
        ],
        compiler_params=params,
    )(src2, orb2, base_potential, index, factor, eig, left, right, stiff, restrict_t, adjoint_mid, projected_mid)

    def exchanged(array, axes):
        return lax.all_to_all(array, axes, split_axis=0, concat_axis=0, tiled=True)

    projected, place, x_at = lax.optimization_barrier((projected, place, x_at))
    tiles = exchanged(projected.reshape(X * COPIES, WIDTH, LANES), OUTER)
    tiles = jnp.sum(tiles.reshape(X, COPIES, WIDTH, LANES), axis=1)
    mine = lax.dynamic_slice(tiles, (x_at, 0, 0), (1, WIDTH, LANES), allow_negative_indices=False)
    tiles, mine = lax.optimization_barrier((tiles, mine))
    gathered = exchanged(jnp.broadcast_to(tiles.reshape(1, X * WIDTH, LANES), (Z, X * WIDTH, LANES)), ("z",))
    columns = pl.pallas_call(
        sum_kernel,
        out_shape=struct((HALF, LANES), F32),
        in_specs=[vmem] * 4,
        out_specs=vmem,
        compiler_params=params,
    )(place, gathered.reshape(X * Z * WIDTH, LANES), mine.reshape(WIDTH, LANES), jnp.asarray(unpack_table(), BF16))
    columns = exchanged(columns.reshape(COPIES, WIDTH, LANES), ORB)
    updated, applied2 = pl.pallas_call(
        apply_kernel,
        out_shape=(struct((HALF, HALF), F32), struct((rows, NODES), BF16)),
        in_specs=[vmem] * 8,
        out_specs=(vmem, vmem),
        compiler_params=params,
    )(columns.reshape(HALF, LANES), orb2, linear, ghost, left, right, index, prolong)
    return adjoint2.reshape(orbitals.shape), updated, applied2.reshape(orbitals.shape)


def solution(mesh):
    axes = jax.sharding.Mesh(mesh.devices.reshape(X, Z, Y, CORES), ("x", "z", "y", "core"))
    in_specs = (
        P(DOM, ORB, None),
        P(DOM, ORB, None),
        P(ORB),
        P(DOM),
        P(DOM, None),
        P(),
        P(DOM, None),
        P(),
        P(),
        P(DOM, None),
        P(DOM),
        P(DOM, None),
    )
    out_specs = (P(DOM, ORB, None), P(DOM, None), P(DOM, ORB, None))
    return jax.shard_map(local, mesh=axes, in_specs=in_specs, out_specs=out_specs, check_vma=False)
```

```python
import jax
import jax.numpy as jnp
import numpy as np
from jax import lax
from jax.experimental import pallas as pl
from jax.experimental.pallas import tpu as pltpu
from jax.sharding import PartitionSpec as P

ITERS = 4
relax = 0.25
step_rate = 0.1

LANES = 128
HALF = 64
NODES = 512
WIDTH = 8
CELLS = 48
HALO = 4
EXT = CELLS + 2 * HALO
F32, BF16 = jnp.float32, jnp.bfloat16


def dot(a, b, contract=((1,), (0,))):
    return lax.dot_general(a, b, (contract, ((), ())), preferred_element_type=F32)


def split(a):
    high = a.astype(BF16)
    return high, (a - high.astype(F32)).astype(BF16)


def lane_below(bound):
    return lax.broadcasted_iota(jnp.int32, (WIDTH, LANES), 1) < bound


SRC_ROWS, ORB_AT, BASE_AT, META_AT, HALO_ROWS = 32, 32, 40, 44, 48
IDX, SCALE, OWNER, SLOT = slice(0, 128), slice(128, 256), slice(256, 384), slice(384, 512)
POT, IDS, GHOST_IDS = CELLS, CELLS + HALF, CELLS + HALF + 12
X, Z, Y, CORES = 4, 16, 4, 2
DOM, ORB, OUTER = ("x", "z"), ("y", "core"), ("x", "y", "core")
COPIES = Y * CORES
STRIP = 3 * HALO
NT = ((1,), (1,))


def tile(e):
    return slice(e * WIDTH, (e + 1) * WIDTH)


def cols(t):
    return slice(t * LANES, (t + 1) * LANES)


def face_rows(perm, wanted_cells):
    twice = jnp.concatenate([perm, perm], 1).astype(F32)
    columns = jnp.transpose(twice)[0:HALF]
    node = lax.broadcasted_iota(jnp.int32, (HALF, LANES), 0).astype(F32)
    lane = lax.broadcasted_iota(jnp.int32, (HALF, LANES), 1).astype(F32)
    low = lax.broadcasted_iota(jnp.int32, (1, LANES), 1) < HALF
    rows = []
    for c in wanted_cells:
        inverse = jnp.sum(jnp.where(columns[:, c : c + 1] == lane, node, 0.0), axis=0, keepdims=True)
        rows.append(jnp.where(low, inverse + HALF, twice[c : c + 1]))
    return rows


def face_tiles(perm):
    half = CELLS // 2
    perm = perm.astype(F32)
    pairs = jnp.concatenate([perm[:half], perm[half:]], 1)
    twice = jnp.concatenate([perm, perm], 1)
    node = lax.broadcasted_iota(jnp.int32, (HALF, LANES), 0).astype(F32)
    row = lax.broadcasted_iota(jnp.int32, (WIDTH, LANES), 0)
    lane = lax.broadcasted_iota(jnp.int32, (WIDTH, LANES), 1)
    counts = jnp.where(lane // HALF == row, lane % HALF, 0).astype(F32).astype(BF16)
    empty = jnp.zeros((HALF, LANES), BF16)
    tiles = [None] * CELLS
    for p in range(half):
        hot = jnp.where(pairs[p : p + 1] == node, 1.0, 0.0).astype(BF16)
        inverse = dot(counts, jnp.concatenate([hot, empty], 0), NT)
        for i, c in enumerate((p, p + half)):
            rows = jnp.where(lane[:1] < HALF, inverse[i : i + 1] + HALF, twice[c : c + 1])
            tiles[c] = jnp.broadcast_to(rows.astype(jnp.int32), (WIDTH, LANES))
    return tiles


def in_hbm(array):
    return pltpu.with_memory_space_constraint(array, pltpu.HBM)


def pack_kernel(scale_hbm, owner_hbm, slot_hbm, src_hbm, orb_hbm, base_hbm, perm_hbm, stiff_hbm, eig_hbm,
                to_mate, to_other, factor_out, eig_out, stiff_out,
                scale, owner, slot, src, orb, base, perm, eig, to_left, to_right, sems):
    top, rows = CELLS - WIDTH, CELLS * WIDTH
    copies = [(scale_hbm, scale), (owner_hbm, owner), (slot_hbm, slot)]
    for hbm, here, size, end in (
        (src_hbm, src, SRC_ROWS, rows), (orb_hbm, orb, 16, rows), (base_hbm, base, WIDTH, CELLS), (perm_hbm, perm, WIDTH, CELLS)
    ):
        copies.append((hbm.at[0:size], here.at[0]))
        copies.append((hbm.at[end - size : end], here.at[1]))
    copies += [(eig_hbm, eig), (stiff_hbm, stiff_out)]
    copies = [pltpu.make_async_copy(one, two, sems.at[i]) for i, (one, two) in enumerate(copies)]
    for copy in copies:
        copy.start()
    for copy in copies[:-1]:
        copy.wait()
    row = lax.broadcasted_iota(jnp.int32, (WIDTH, LANES), 0)
    eig_tile = jnp.zeros((WIDTH, LANES), F32)
    for i in range(WIDTH):
        eig_tile = jnp.where(row == i, eig[i], eig_tile)
    eig_out[...] = eig_tile
    for c in range(CELLS):
        factor_out[c : c + 1] = jnp.full((1, LANES), scale[c], F32)
    for end, out in enumerate((to_left, to_right)):
        inner, first = (0, 0) if end == 0 else (HALO, CELLS - HALO)
        edge_cell = end * (CELLS - 1)
        out[0:SRC_ROWS] = src[end].astype(F32)
        out[ORB_AT : ORB_AT + WIDTH] = orb[end].astype(F32)[tile(end)]
        out[BASE_AT : BASE_AT + HALO] = base[end, inner : inner + HALO]
        faces = face_rows(perm[end], range(inner, inner + HALO))
        for i in range(HALO):
            at = slice(META_AT + i, META_AT + i + 1)
            out[at, IDX] = faces[i]
            out[at, SCALE] = jnp.full((1, LANES), scale[first + i], F32)
            out[at, OWNER] = jnp.full((1, LANES), owner[edge_cell].astype(F32), F32)
            mark = slot[edge_cell].astype(F32) if i == end * (HALO - 1) else 1.0
            out[at, SLOT] = jnp.full((1, LANES), mark, F32)
    even = lax.axis_index("z") % 2 == 0
    to_mate[...] = jnp.where(even, to_right[...], to_left[...])
    to_other[...] = jnp.where(even, to_left[...], to_right[...])
    copies[-1].wait()


def relax_step(strips, x, quarter, shifted, kin, stiff, factor, index, gates):
    low = lane_below(HALF)
    held = [x[strip[0] * WIDTH : (strip[-1] + 1) * WIDTH].astype(BF16) for strip in strips]
    held = held[0] if len(held) == 1 else jnp.concatenate(held, 0)
    kin[0 : held.shape[0]] = dot(held, stiff[...])
    at = 0
    for strip in strips:
        part_before = new_before = None
        for e in strip:
            rows = tile(e)
            scale = factor(e)
            parts, news = [], []
            for t in range(4):
                here = x[rows, cols(t)]
                part = scale * kin[tile(at), cols(t)] + shifted[rows, cols(t)] * here
                parts.append(part)
                news.append(here + quarter[rows, cols(t)] - relax * part)
            at += 1
            if e > strip[0]:
                crossing = jnp.where(low, parts[0], part_before)
                moved = relax * jnp.take_along_axis(crossing, index[tile(e - 1)], axis=1, mode="promise_in_bounds")
                if e in gates:
                    moved = moved * gates[e]
                news[0] = jnp.where(low, news[0] - moved, news[0])
                x[tile(e - 1), cols(3)] = jnp.where(low, new_before, new_before - moved)
            for t in range(3):
                x[rows, cols(t)] = news[t]
            part_before, new_before = parts[3], news[3]
        x[tile(strip[-1]), cols(3)] = new_before


def group_of(row_cells):
    shape = (LANES, len(row_cells) * WIDTH)
    cell = lax.broadcasted_iota(jnp.int32, shape, 0)
    at = lax.broadcasted_iota(jnp.int32, shape, 1) // WIDTH
    gap = [i for i in range(1, len(row_cells)) if row_cells[i] != row_cells[i - 1] + 1]
    owner = at + row_cells[0]
    for i in gap:
        owner = owner + jnp.where(at >= i, row_cells[i] - row_cells[i - 1] - 1, 0)
    return jnp.where(cell == owner, 1.0, 0.0).astype(BF16)


def projection(orb_values, x_values, group, restrict_t):
    high, rest = split(orb_values.astype(F32) * x_values)
    density = dot(group, high) + dot(group, rest)
    high, rest = split(density)
    return dot(restrict_t, high, NT) + dot(restrict_t, rest, NT)


def interior_kernel(owner_hbm, slot_hbm, restrict_hbm, potential_hbm, src, orb, base, perm, factor, eig, stiff,
                    adjoint_out, projected_out, linear_out, index_out, restrict_t,
                    x, quarter, kin, shifted, owner, slot, potential, sems):
    pairs = ((restrict_hbm, restrict_t), (potential_hbm, potential), (owner_hbm, owner), (slot_hbm, slot))
    copies = [pltpu.make_async_copy(one, two, sems.at[i]) for i, (one, two) in enumerate(pairs)]
    for copy in copies:
        copy.start()
    quarter[...] = relax * src[...].astype(F32)
    x[...] = quarter[...]
    faces = face_tiles(perm[...])
    eig_tile = eig[...]

    def scale(c):
        return jnp.broadcast_to(factor[c : c + 1], (WIDTH, LANES))

    for c in range(CELLS):
        for t in range(4):
            shifted[tile(c), cols(t)] = base[c : c + 1, cols(t)] - eig_tile
        index_out[tile(c)] = faces[c]

    def step(_, carry):
        relax_step([range(CELLS)], x, quarter, shifted, kin, stiff, scale, index_out, {})
        return carry

    lax.fori_loop(0, ITERS, step, 0)
    for copy in copies:
        copy.wait()
    inner = slice(HALO * WIDTH, (CELLS - HALO) * WIDTH)
    adjoint_out[...] = x[inner].astype(BF16)
    kin[...] = dot(orb[...], stiff[...])
    for pair in range(CELLS // 2):
        values = orb[pair * 16 : pair * 16 + 16].astype(F32)
        for c in (2 * pair, 2 * pair + 1):
            for t in range(4):
                linear_out[tile(c), cols(t)] = (
                    scale(c) * kin[tile(c), cols(t)] + base[c : c + 1, cols(t)] * values[tile(c % 2), cols(t)]
                )
    row = lax.broadcasted_iota(jnp.int32, (WIDTH, LANES), 0)
    lane = lax.broadcasted_iota(jnp.int32, (WIDTH, LANES), 1)
    at = jnp.where((lane >= IDS) & (lane < GHOST_IDS), row * 12 + lane - IDS, -1)
    ids = jnp.zeros((WIDTH, LANES), F32)
    for c in range(CELLS):
        ids = jnp.where(at == c // 6 * 12 + c % 6, owner[c].astype(F32), ids)
        ids = jnp.where(at == c // 6 * 12 + 6 + c % 6, slot[c].astype(F32), ids)
    turned = jnp.transpose(potential[...])
    static = jnp.concatenate([jnp.zeros((HALF, CELLS), F32), turned, jnp.zeros((HALF, 16), F32)], 1)
    static = (static + jnp.concatenate([ids] * (HALF // WIDTH), 0)) * (1.0 / COPIES)
    projected_out[...] = static - step_rate * projection(
        orb[inner], x[inner], group_of(range(HALO, CELLS - HALO)), restrict_t[...]
    )


def boundary_kernel(src, orb, base, index_own, factor_own, eig, of_mate, of_other, stiff, restrict_t, adjoint_mid,
                    projected_mid, adjoint_out, projected_out, ghost_out, left, right,
                    x, quarter, kin, shifted, factor, index, adjoint_ends, sems):
    near, edge = 2 * HALO * WIDTH, HALO * WIDTH
    last = CELLS * WIDTH
    copies = [
        pltpu.make_async_copy(adjoint_mid, adjoint_out.at[edge : last - edge], sems.at[0]),
        pltpu.make_async_copy(adjoint_ends.at[0], adjoint_out.at[0:edge], sems.at[1]),
        pltpu.make_async_copy(adjoint_ends.at[1], adjoint_out.at[last - edge : last], sems.at[2]),
    ]
    copies[0].start()
    even = lax.axis_index("z") % 2 == 0
    left[...] = jnp.where(even, of_other[...], of_mate[...])
    right[...] = jnp.where(even, of_mate[...], of_other[...])
    quarter[0:edge] = relax * left[0:SRC_ROWS]
    quarter[edge : edge + near] = relax * src[0:near].astype(F32)
    quarter[edge + near : edge + 2 * near] = relax * src[last - near :].astype(F32)
    quarter[edge + 2 * near :] = relax * right[0:SRC_ROWS]
    x[...] = quarter[...]
    eig_tile = eig[...]
    for e in range(2 * STRIP):
        ghost = left if e < HALO else right if e >= 2 * STRIP - HALO else None
        if ghost is None:
            c = e - HALO if e < STRIP else CELLS - 2 * HALO + e - STRIP
            base_row = base[c : c + 1]
            factor[tile(e)] = jnp.broadcast_to(factor_own[c : c + 1], (WIDTH, LANES))
            index[tile(e)] = index_own[tile(c)]
        else:
            i = e if e < HALO else e - 2 * STRIP + HALO
            base_row = ghost[BASE_AT + i : BASE_AT + i + 1]
            meta_row = ghost[META_AT + i : META_AT + i + 1]
            factor[tile(e)] = jnp.broadcast_to(meta_row[:, SCALE], (WIDTH, LANES))
            index[tile(e)] = jnp.broadcast_to(meta_row[:, IDX].astype(jnp.int32), (WIDTH, LANES))
        for t in range(4):
            shifted[tile(e), cols(t)] = base_row[:, cols(t)] - eig_tile
    gates = {HALO: left[META_AT : META_AT + 1, SLOT], 2 * STRIP - HALO: right[HALO_ROWS - 1 : HALO_ROWS, SLOT]}
    for k in range(ITERS):
        strips = [range(k, STRIP - k), range(STRIP + k, 2 * STRIP - k)]
        relax_step(strips, x, quarter, shifted, kin, stiff, lambda e: factor[tile(e)], index, gates)
    low_cells, high_cells = x[edge : 2 * edge], x[4 * edge : 5 * edge]
    adjoint_ends[0] = low_cells.astype(BF16)
    adjoint_ends[1] = high_cells.astype(BF16)
    copies[1].start()
    copies[2].start()
    own_orb = jnp.concatenate([orb[0:edge], orb[last - edge :]], 0)
    own_x = jnp.concatenate([low_cells, high_cells], 0)
    lane = lax.broadcasted_iota(jnp.int32, (1, LANES), 1)
    ghost_ids = jnp.zeros((1, LANES), F32)
    for i, row in enumerate((left[META_AT + HALO - 1 : META_AT + HALO], right[META_AT : META_AT + 1])):
        ghost_ids = jnp.where(lane == GHOST_IDS + 2 * i, row[:, OWNER], ghost_ids)
        ghost_ids = jnp.where(lane == GHOST_IDS + 2 * i + 1, row[:, SLOT], ghost_ids)
    added = projection(own_orb, own_x, group_of([*range(HALO), *range(CELLS - HALO, CELLS)]), restrict_t[...])
    whole = projected_mid[...] + ghost_ids * (1.0 / COPIES) - step_rate * added
    for i in range(X):
        projected_out[i * HALF : (i + 1) * HALF] = whole
    ghosts = jnp.concatenate([left[ORB_AT : ORB_AT + WIDTH], right[ORB_AT : ORB_AT + WIDTH]], 0)
    ghost_kin = dot(ghosts.astype(BF16), stiff[...])
    for i, e, base_row in (
        (0, HALO - 1, left[BASE_AT + HALO - 1 : BASE_AT + HALO]),
        (1, 2 * STRIP - HALO, right[BASE_AT : BASE_AT + 1]),
    ):
        for t in range(4):
            ghost_out[tile(i), cols(t)] = (
                factor[tile(e)] * ghost_kin[tile(i), cols(t)] + base_row[:, cols(t)] * ghosts[tile(i), cols(t)]
            )
    for copy in copies:
        copy.wait()


def sum_kernel(place, gathered, asking, unpack, out):
    high, rest = split(gathered[...])
    ids = dot(jnp.concatenate([high, asking[...].astype(BF16)], 0), unpack[...])
    row = lax.broadcasted_iota(jnp.int32, ids.shape, 0) % WIDTH
    lane = lax.broadcasted_iota(jnp.int32, ids.shape, 1)
    ids = jnp.where(jnp.where(lane < CELLS, lane // 6, 0) == row, ids, 0.0)
    ids = jnp.sum(ids.reshape(Z + X, WIDTH, LANES), axis=1)
    lane = lax.broadcasted_iota(jnp.int32, ids.shape, 1)
    row = lax.broadcasted_iota(jnp.int32, ids.shape, 0)
    mine = jnp.where(row < Z, place[0:1], place[1:2])
    slots = mine + (jnp.where(row < Z, row, (row - Z) * Z) * HALF + lane - POT).astype(F32)
    ids = jnp.where((lane >= POT) & (lane < IDS), slots, ids)
    known = jnp.where(lane[:Z] < IDS, ids[:Z], -1.0)
    wanted = jnp.where(lane[Z:] < IDS + 2, ids[Z:], -2.0)
    known = jnp.transpose(jnp.concatenate([known, jnp.zeros((LANES - Z, LANES), F32)], 0))
    total = jnp.zeros((2 * WIDTH, X * LANES), F32)
    for s in range(0, Z, 2):
        hot = [
            jnp.concatenate(
                [jnp.where(known[:, i : i + 1] == wanted[m : m + 1], 1.0, 0.0).astype(BF16) for m in range(X)], 1
            )
            for i in (s, s + 1)
        ]
        both = [jnp.concatenate([high[tile(i)], rest[tile(i)]], 0) for i in (s, s + 1)]
        total = total + dot(jnp.concatenate(both, 1), jnp.concatenate(hot, 0))
    result = total[:WIDTH] + total[WIDTH:]
    for m in range(X):
        for i in range(COPIES):
            out[tile(m * COPIES + i)] = result[:, cols(m)]


def apply_kernel(columns, orb, linear, ghost, left, right, index, prolong, updated_out, applied_out):
    summed = columns[0:HALF]
    for i in range(1, X):
        summed = summed + columns[i * HALF : (i + 1) * HALF]
    table = jnp.transpose(summed)
    updated_out[...] = table[POT:IDS]
    high, rest = split(table)
    node = dot(high, prolong[...]) + dot(rest, prolong[...])
    low = lane_below(HALF)
    part_before = new_before = index_before = None
    finished = []
    for e in range(CELLS + 2):
        c = e - 1
        if e == 0:
            values, start, node_at = left[ORB_AT : ORB_AT + WIDTH], ghost[tile(0)], IDS
        elif e <= CELLS:
            values = orb[c // 2 * 16 : c // 2 * 16 + 16].astype(F32)[tile(c % 2)]
            start, node_at = linear[tile(c)], c
        else:
            values, start, node_at = right[ORB_AT : ORB_AT + WIDTH], ghost[tile(1)], IDS + 1
        whole = start + node[node_at : node_at + 1] * values
        parts = [whole[:, cols(t)] for t in range(4)]
        if e > 0:
            crossing = jnp.where(low, parts[0], part_before)
            moved = jnp.take_along_axis(crossing, index_before, axis=1, mode="promise_in_bounds")
            if e == 1:
                moved = moved * left[META_AT : META_AT + 1, SLOT]
            if e == CELLS + 1:
                moved = moved * right[HALO_ROWS - 1 : HALO_ROWS, SLOT]
            done = jnp.where(low, new_before[3], new_before[3] + moved)
            if e > 1:
                finished.append(jnp.concatenate([*new_before[:3], done], 1))
            news = [jnp.where(low, parts[0] + moved, parts[0]), *parts[1:]]
        else:
            news = parts
        part_before, new_before = parts[3], news
        if e == 0:
            meta_row = left[META_AT + HALO - 1 : META_AT + HALO]
            index_before = jnp.broadcast_to(meta_row[:, IDX].astype(jnp.int32), (WIDTH, LANES))
        elif e <= CELLS:
            index_before = index[tile(c)]
        if len(finished) == 2:
            applied_out[(e - 3) * WIDTH : (e - 1) * WIDTH] = jnp.concatenate(finished, 0).astype(BF16)
            finished = []


def unpack_table():
    table = np.zeros((LANES, LANES), np.float32)
    for k in range(CELLS):
        table[112 + k % 6, k] = 64.0
        table[118 + k % 6, k] = 1.0
    for i in range(2):
        table[GHOST_IDS + 2 * i, IDS + i] = 64.0
        table[GHOST_IDS + 2 * i + 1, IDS + i] = 1.0
    return table


def local(orbitals, adjoint_source, eigenvalues, cell_scale, base_potential, stiffness, face_perm, restrict,
          prolong, owner, pot_slot, potential):
    x_at, z_at = lax.axis_index("x"), lax.axis_index("z")
    vmem = pl.BlockSpec(memory_space=pltpu.VMEM)
    params = pltpu.CompilerParams(vmem_limit_bytes=32 * 2**20)
    struct = jax.ShapeDtypeStruct

    orb2 = orbitals.reshape(CELLS * WIDTH, NODES)
    src2 = adjoint_source.reshape(CELLS * WIDTH, NODES)
    owner1 = owner.reshape(CELLS)
    first = jnp.stack([x_at * Z, z_at]) * HALF
    place = jnp.broadcast_to(first.astype(F32)[:, None], (2, LANES))

    hbm = pl.BlockSpec(memory_space=pltpu.HBM)
    to_mate, to_other, factor, eig, stiff = pl.pallas_call(
        pack_kernel,
        out_shape=(
            struct((HALO_ROWS, NODES), F32),
            struct((HALO_ROWS, NODES), F32),
            struct((CELLS, LANES), F32),
            struct((WIDTH, LANES), F32),
            struct((NODES, NODES), BF16),
        ),
        in_specs=[hbm] * 9,
        out_specs=(vmem,) * 5,
        scratch_shapes=[
            pltpu.SMEM((CELLS,), F32),
            pltpu.SMEM((CELLS,), jnp.int32),
            pltpu.SMEM((CELLS,), jnp.int32),
            pltpu.VMEM((2, SRC_ROWS, NODES), BF16),
            pltpu.VMEM((2, 16, NODES), BF16),
            pltpu.VMEM((2, WIDTH, NODES), F32),
            pltpu.VMEM((2, WIDTH, HALF), jnp.int32),
            pltpu.SMEM((WIDTH,), F32),
            pltpu.VMEM((HALO_ROWS, NODES), F32),
            pltpu.VMEM((HALO_ROWS, NODES), F32),
            pltpu.SemaphoreType.DMA((13,)),
        ],
        compiler_params=params,
    )(*map(in_hbm, (cell_scale, owner1, pot_slot, src2, orb2, base_potential, face_perm, stiffness, eigenvalues)))

    of_mate = lax.ppermute(to_mate, DOM, [(i, i ^ 1) for i in range(X * Z)])
    of_other = lax.ppermute(to_other, DOM, [(i, i + 1 if i % 2 else i - 1) for i in range(1, X * Z - 1)])

    rows = CELLS * WIDTH
    inner = rows - 2 * HALO * WIDTH
    adjoint_mid, projected_mid, linear, index, restrict_t = pl.pallas_call(
        interior_kernel,
        out_shape=(
            struct((inner, NODES), BF16),
            struct((HALF, LANES), F32),
            struct((rows, NODES), F32),
            struct((rows, LANES), jnp.int32),
            struct((HALF, NODES), BF16),
        ),
        in_specs=[hbm] * 4 + [vmem] * 7,
        out_specs=(vmem,) * 5,
        scratch_shapes=[pltpu.VMEM((rows, NODES), F32)] * 4
        + [
            pltpu.SMEM((CELLS,), jnp.int32),
            pltpu.SMEM((CELLS,), jnp.int32),
            pltpu.VMEM((HALF, HALF), F32),
            pltpu.SemaphoreType.DMA((4,)),
        ],
        compiler_params=params,
        cost_estimate=pl.CostEstimate(flops=5 * 2 * rows * NODES * NODES, bytes_accessed=4 * 2**20, transcendentals=0),
    )(*map(in_hbm, (owner1, pot_slot, restrict.T, potential)), src2, orb2, base_potential, face_perm, factor, eig, stiff)

    strip_rows = 2 * STRIP * WIDTH
    adjoint2, projected, ghost, left, right = pl.pallas_call(
        boundary_kernel,
        out_shape=(
            struct((rows, NODES), BF16),
            struct((X * HALF, LANES), F32),
            struct((2 * WIDTH, NODES), F32),
            struct((HALO_ROWS, NODES), F32),
            struct((HALO_ROWS, NODES), F32),
        ),
        in_specs=[vmem] * 12,
        out_specs=(hbm, vmem, vmem, vmem, vmem),
        scratch_shapes=[pltpu.VMEM((strip_rows, NODES), F32)] * 4
        + [
            pltpu.VMEM((strip_rows, LANES), F32),
            pltpu.VMEM((strip_rows, LANES), jnp.int32),
            pltpu.VMEM((2, HALO * WIDTH, NODES), BF16),
            pltpu.SemaphoreType.DMA((3,)),
        ],
        compiler_params=params,
    )(src2, orb2, base_potential, index, factor, eig, of_mate, of_other, stiff, restrict_t, adjoint_mid,
      projected_mid)

    def exchanged(array, axes):
        return lax.all_to_all(array, axes, split_axis=0, concat_axis=0, tiled=True)

    projected, place, x_at = lax.optimization_barrier((projected, place, x_at))
    tiles = exchanged(projected.reshape(X * COPIES, WIDTH, LANES), OUTER)
    tiles = jnp.sum(tiles.reshape(X, COPIES, WIDTH, LANES), axis=1)
    mine = lax.dynamic_slice(tiles, (x_at, 0, 0), (1, WIDTH, LANES), allow_negative_indices=False)
    gathered = exchanged(jnp.broadcast_to(mine, (Z, WIDTH, LANES)), ("z",))
    columns = pl.pallas_call(
        sum_kernel,
        out_shape=struct((X * HALF, LANES), F32),
        in_specs=[vmem] * 4,
        out_specs=vmem,
        compiler_params=params,
    )(place, gathered.reshape(Z * WIDTH, LANES), tiles.reshape(X * WIDTH, LANES), jnp.asarray(unpack_table(), BF16))
    columns = exchanged(columns.reshape(X * COPIES, WIDTH, LANES), OUTER)
    updated, applied2 = pl.pallas_call(
        apply_kernel,
        out_shape=(struct((HALF, HALF), F32), struct((rows, NODES), BF16)),
        in_specs=[vmem] * 8,
        out_specs=(vmem, vmem),
        compiler_params=params,
    )(columns.reshape(X * HALF, LANES), orb2, linear, ghost, left, right, index, prolong)
    return adjoint2.reshape(orbitals.shape), updated, applied2.reshape(orbitals.shape)


def solution(mesh):
    axes = jax.sharding.Mesh(mesh.devices.reshape(X, Z, Y, CORES), ("x", "z", "y", "core"))
    in_specs = (
        P(DOM, ORB, None),
        P(DOM, ORB, None),
        P(ORB),
        P(DOM),
        P(DOM, None),
        P(),
        P(DOM, None),
        P(),
        P(),
        P(DOM, None),
        P(DOM),
        P(DOM, None),
    )
    out_specs = (P(DOM, ORB, None), P(DOM, None), P(DOM, ORB, None))
    return jax.shard_map(local, mesh=axes, in_specs=in_specs, out_specs=out_specs, check_vma=False)
```

```python
import jax
import jax.numpy as jnp
import numpy as np
from jax import lax
from jax.experimental import pallas as pl
from jax.experimental.pallas import tpu as pltpu
from jax.sharding import PartitionSpec as P

ITERS = 4
relax = 0.25
step_rate = 0.1

LANES = 128
HALF = 64
NODES = 512
WIDTH = 8
CELLS = 48
HALO = 4
EXT = CELLS + 2 * HALO
F32, BF16 = jnp.float32, jnp.bfloat16


def dot(a, b, contract=((1,), (0,))):
    return lax.dot_general(a, b, (contract, ((), ())), preferred_element_type=F32)


def split(a):
    high = a.astype(BF16)
    return high, (a - high.astype(F32)).astype(BF16)


def lane_below(bound):
    return lax.broadcasted_iota(jnp.int32, (WIDTH, LANES), 1) < bound


SRC_ROWS, ORB_AT, BASE_AT, META_AT, HALO_ROWS = 32, 32, 40, 44, 48
IDX, SCALE, OWNER, SLOT = slice(0, 128), slice(128, 256), slice(256, 384), slice(384, 512)
POT, IDS, EDGE_IDS = CELLS, CELLS + HALF, CELLS + HALF + 12
X, Z, Y, CORES = 4, 16, 4, 2
DOM, ORB, OUTER = ("x", "z"), ("y", "core"), ("x", "y", "core")
COPIES = Y * CORES
STRIP = 3 * HALO
NT = ((1,), (1,))


def tile(e):
    return slice(e * WIDTH, (e + 1) * WIDTH)


def cols(t):
    return slice(t * LANES, (t + 1) * LANES)


def face_rows(perm, wanted_cells):
    twice = jnp.concatenate([perm, perm], 1).astype(F32)
    columns = jnp.transpose(twice)[0:HALF]
    node = lax.broadcasted_iota(jnp.int32, (HALF, LANES), 0).astype(F32)
    lane = lax.broadcasted_iota(jnp.int32, (HALF, LANES), 1).astype(F32)
    low = lax.broadcasted_iota(jnp.int32, (1, LANES), 1) < HALF
    rows = []
    for c in wanted_cells:
        inverse = jnp.sum(jnp.where(columns[:, c : c + 1] == lane, node, 0.0), axis=0, keepdims=True)
        rows.append(jnp.where(low, inverse + HALF, twice[c : c + 1]))
    return rows


def face_tiles(perm):
    half = CELLS // 2
    perm = perm.astype(F32)
    pairs = jnp.concatenate([perm[:half], perm[half:]], 1)
    twice = jnp.concatenate([perm, perm], 1)
    node = lax.broadcasted_iota(jnp.int32, (HALF, LANES), 0).astype(F32)
    row = lax.broadcasted_iota(jnp.int32, (WIDTH, LANES), 0)
    lane = lax.broadcasted_iota(jnp.int32, (WIDTH, LANES), 1)
    counts = jnp.where(lane // HALF == row, lane % HALF, 0).astype(F32).astype(BF16)
    empty = jnp.zeros((HALF, LANES), BF16)
    tiles = [None] * CELLS
    for p in range(half):
        hot = jnp.where(pairs[p : p + 1] == node, 1.0, 0.0).astype(BF16)
        inverse = dot(counts, jnp.concatenate([hot, empty], 0), NT)
        for i, c in enumerate((p, p + half)):
            rows = jnp.where(lane[:1] < HALF, inverse[i : i + 1] + HALF, twice[c : c + 1])
            tiles[c] = jnp.broadcast_to(rows.astype(jnp.int32), (WIDTH, LANES))
    return tiles


def in_hbm(array):
    return pltpu.with_memory_space_constraint(array, pltpu.HBM)


def pack_kernel(scale_hbm, owner_hbm, slot_hbm, src_hbm, orb_hbm, base_hbm, perm_hbm, stiff_hbm, eig_hbm,
                to_mate, to_other, ids_out, factor_out, eig_out, stiff_out,
                scale, owner, slot, src, orb, base, perm, eig, to_left, to_right, sems):
    top, rows = CELLS - WIDTH, CELLS * WIDTH
    copies = [(scale_hbm, scale), (owner_hbm, owner), (slot_hbm, slot)]
    for hbm, here, size, end in (
        (src_hbm, src, SRC_ROWS, rows), (orb_hbm, orb, 16, rows), (base_hbm, base, WIDTH, CELLS), (perm_hbm, perm, WIDTH, CELLS)
    ):
        copies.append((hbm.at[0:size], here.at[0]))
        copies.append((hbm.at[end - size : end], here.at[1]))
    copies += [(eig_hbm, eig), (stiff_hbm, stiff_out)]
    copies = [pltpu.make_async_copy(one, two, sems.at[i]) for i, (one, two) in enumerate(copies)]
    for copy in copies:
        copy.start()
    for copy in copies[:-1]:
        copy.wait()
    row = lax.broadcasted_iota(jnp.int32, (WIDTH, LANES), 0)
    eig_tile = jnp.zeros((WIDTH, LANES), F32)
    for i in range(WIDTH):
        eig_tile = jnp.where(row == i, eig[i], eig_tile)
    eig_out[...] = eig_tile
    for c in range(CELLS):
        factor_out[c : c + 1] = jnp.full((1, LANES), scale[c], F32)
    for end, out in enumerate((to_left, to_right)):
        inner, first = (0, 0) if end == 0 else (HALO, CELLS - HALO)
        edge_cell = end * (CELLS - 1)
        out[0:SRC_ROWS] = src[end].astype(F32)
        out[ORB_AT : ORB_AT + WIDTH] = orb[end].astype(F32)[tile(end)]
        out[BASE_AT : BASE_AT + HALO] = base[end, inner : inner + HALO]
        faces = face_rows(perm[end], range(inner, inner + HALO))
        for i in range(HALO):
            at = slice(META_AT + i, META_AT + i + 1)
            out[at, IDX] = faces[i]
            out[at, SCALE] = jnp.full((1, LANES), scale[first + i], F32)
            out[at, OWNER] = jnp.full((1, LANES), owner[edge_cell].astype(F32), F32)
            mark = slot[edge_cell].astype(F32) if i == end * (HALO - 1) else 1.0
            out[at, SLOT] = jnp.full((1, LANES), mark, F32)
    lane = lax.broadcasted_iota(jnp.int32, (WIDTH, LANES), 1)
    ids = [jnp.zeros((WIDTH, LANES), F32)] * 4
    for c in range(CELLS):
        ids[c % 4] = jnp.where(lane == c, (owner[c] * HALF + slot[c]).astype(F32), ids[c % 4])
    for i, value in enumerate((owner[0], slot[0], owner[CELLS - 1], slot[CELLS - 1])):
        ids[i] = jnp.where(lane == EDGE_IDS + i, value.astype(F32), ids[i])
    ids_out[...] = (ids[0] + ids[1]) + (ids[2] + ids[3])
    even = lax.axis_index("z") % 2 == 0
    to_mate[...] = jnp.where(even, to_right[...], to_left[...])
    to_other[...] = jnp.where(even, to_left[...], to_right[...])
    copies[-1].wait()


def relax_step(strips, x, quarter, shifted, kin, stiff, factor, index, gates):
    low = lane_below(HALF)
    held = [x[strip[0] * WIDTH : (strip[-1] + 1) * WIDTH].astype(BF16) for strip in strips]
    held = held[0] if len(held) == 1 else jnp.concatenate(held, 0)
    kin[0 : held.shape[0]] = dot(held, stiff[...])
    at = 0
    for strip in strips:
        part_before = new_before = None
        for e in strip:
            rows = tile(e)
            scale = factor(e)
            parts, news = [], []
            for t in range(4):
                here = x[rows, cols(t)]
                part = scale * kin[tile(at), cols(t)] + shifted[rows, cols(t)] * here
                parts.append(part)
                news.append(here + quarter[rows, cols(t)] - relax * part)
            at += 1
            if e > strip[0]:
                crossing = jnp.where(low, parts[0], part_before)
                moved = relax * jnp.take_along_axis(crossing, index[tile(e - 1)], axis=1, mode="promise_in_bounds")
                if e in gates:
                    moved = moved * gates[e]
                news[0] = jnp.where(low, news[0] - moved, news[0])
                x[tile(e - 1), cols(3)] = jnp.where(low, new_before, new_before - moved)
            for t in range(3):
                x[rows, cols(t)] = news[t]
            part_before, new_before = parts[3], news[3]
        x[tile(strip[-1]), cols(3)] = new_before


def group_of(row_cells):
    shape = (LANES, len(row_cells) * WIDTH)
    cell = lax.broadcasted_iota(jnp.int32, shape, 0)
    at = lax.broadcasted_iota(jnp.int32, shape, 1) // WIDTH
    gap = [i for i in range(1, len(row_cells)) if row_cells[i] != row_cells[i - 1] + 1]
    owner = at + row_cells[0]
    for i in gap:
        owner = owner + jnp.where(at >= i, row_cells[i] - row_cells[i - 1] - 1, 0)
    return jnp.where(cell == owner, 1.0, 0.0).astype(BF16)


def projection(orb_values, x_values, group, restrict_t):
    high, rest = split(orb_values.astype(F32) * x_values)
    density = dot(group, high) + dot(group, rest)
    high, rest = split(density)
    return dot(restrict_t, high, NT) + dot(restrict_t, rest, NT)


def interior_kernel(owner_hbm, slot_hbm, restrict_hbm, potential_hbm, src, orb, base, perm, factor, eig, stiff,
                    adjoint_out, projected_out, linear_out, index_out, restrict_t,
                    x, quarter, kin, shifted, owner, slot, potential, sems):
    pairs = ((restrict_hbm, restrict_t), (potential_hbm, potential), (owner_hbm, owner), (slot_hbm, slot))
    copies = [pltpu.make_async_copy(one, two, sems.at[i]) for i, (one, two) in enumerate(pairs)]
    for copy in copies:
        copy.start()
    quarter[...] = relax * src[...].astype(F32)
    x[...] = quarter[...]
    faces = face_tiles(perm[...])
    eig_tile = eig[...]

    def scale(c):
        return jnp.broadcast_to(factor[c : c + 1], (WIDTH, LANES))

    for c in range(CELLS):
        for t in range(4):
            shifted[tile(c), cols(t)] = base[c : c + 1, cols(t)] - eig_tile
        index_out[tile(c)] = faces[c]

    def step(_, carry):
        relax_step([range(CELLS)], x, quarter, shifted, kin, stiff, scale, index_out, {})
        return carry

    lax.fori_loop(0, ITERS, step, 0)
    for copy in copies:
        copy.wait()
    inner = slice(HALO * WIDTH, (CELLS - HALO) * WIDTH)
    adjoint_out[...] = x[inner].astype(BF16)
    kin[...] = dot(orb[...], stiff[...])
    for pair in range(CELLS // 2):
        values = orb[pair * 16 : pair * 16 + 16].astype(F32)
        for c in (2 * pair, 2 * pair + 1):
            for t in range(4):
                linear_out[tile(c), cols(t)] = (
                    scale(c) * kin[tile(c), cols(t)] + base[c : c + 1, cols(t)] * values[tile(c % 2), cols(t)]
                )
    row = lax.broadcasted_iota(jnp.int32, (WIDTH, LANES), 0)
    lane = lax.broadcasted_iota(jnp.int32, (WIDTH, LANES), 1)
    at = jnp.where((lane >= IDS) & (lane < EDGE_IDS), row * 12 + lane - IDS, -1)
    ids = jnp.zeros((WIDTH, LANES), F32)
    for c in range(CELLS):
        ids = jnp.where(at == c // 6 * 12 + c % 6, owner[c].astype(F32), ids)
        ids = jnp.where(at == c // 6 * 12 + 6 + c % 6, slot[c].astype(F32), ids)
    turned = jnp.transpose(potential[...])
    static = jnp.concatenate([jnp.zeros((HALF, CELLS), F32), turned, jnp.zeros((HALF, 16), F32)], 1)
    static = (static + jnp.concatenate([ids] * (HALF // WIDTH), 0)) * (1.0 / COPIES)
    projected_out[...] = static - step_rate * projection(
        orb[inner], x[inner], group_of(range(HALO, CELLS - HALO)), restrict_t[...]
    )


def boundary_kernel(src, orb, base, index_own, factor_own, eig, of_mate, of_other, ids_of_x, stiff, restrict_t, adjoint_mid,
                    projected_mid, adjoint_out, projected_out, ghost_out, left, right,
                    x, quarter, kin, shifted, factor, index, adjoint_ends, sems):
    near, edge = 2 * HALO * WIDTH, HALO * WIDTH
    last = CELLS * WIDTH
    copies = [
        pltpu.make_async_copy(adjoint_mid, adjoint_out.at[edge : last - edge], sems.at[0]),
        pltpu.make_async_copy(adjoint_ends.at[0], adjoint_out.at[0:edge], sems.at[1]),
        pltpu.make_async_copy(adjoint_ends.at[1], adjoint_out.at[last - edge : last], sems.at[2]),
    ]
    copies[0].start()
    even = lax.axis_index("z") % 2 == 0
    left[...] = jnp.where(even, of_other[...], of_mate[...])
    right[...] = jnp.where(even, of_mate[...], of_other[...])
    quarter[0:edge] = relax * left[0:SRC_ROWS]
    quarter[edge : edge + near] = relax * src[0:near].astype(F32)
    quarter[edge + near : edge + 2 * near] = relax * src[last - near :].astype(F32)
    quarter[edge + 2 * near :] = relax * right[0:SRC_ROWS]
    x[...] = quarter[...]
    eig_tile = eig[...]
    for e in range(2 * STRIP):
        ghost = left if e < HALO else right if e >= 2 * STRIP - HALO else None
        if ghost is None:
            c = e - HALO if e < STRIP else CELLS - 2 * HALO + e - STRIP
            base_row = base[c : c + 1]
            factor[tile(e)] = jnp.broadcast_to(factor_own[c : c + 1], (WIDTH, LANES))
            index[tile(e)] = index_own[tile(c)]
        else:
            i = e if e < HALO else e - 2 * STRIP + HALO
            base_row = ghost[BASE_AT + i : BASE_AT + i + 1]
            meta_row = ghost[META_AT + i : META_AT + i + 1]
            factor[tile(e)] = jnp.broadcast_to(meta_row[:, SCALE], (WIDTH, LANES))
            index[tile(e)] = jnp.broadcast_to(meta_row[:, IDX].astype(jnp.int32), (WIDTH, LANES))
        for t in range(4):
            shifted[tile(e), cols(t)] = base_row[:, cols(t)] - eig_tile
    gates = {HALO: left[META_AT : META_AT + 1, SLOT], 2 * STRIP - HALO: right[HALO_ROWS - 1 : HALO_ROWS, SLOT]}
    for k in range(ITERS):
        strips = [range(k, STRIP - k), range(STRIP + k, 2 * STRIP - k)]
        relax_step(strips, x, quarter, shifted, kin, stiff, lambda e: factor[tile(e)], index, gates)
    low_cells, high_cells = x[edge : 2 * edge], x[4 * edge : 5 * edge]
    adjoint_ends[0] = low_cells.astype(BF16)
    adjoint_ends[1] = high_cells.astype(BF16)
    copies[1].start()
    copies[2].start()
    own_orb = jnp.concatenate([orb[0:edge], orb[last - edge :]], 0)
    own_x = jnp.concatenate([low_cells, high_cells], 0)
    added = projection(own_orb, own_x, group_of([*range(HALO), *range(CELLS - HALO, CELLS)]), restrict_t[...])
    whole = projected_mid[...] - step_rate * added
    member = lax.axis_index("y") * CORES + lax.axis_index("core")
    x_of_ids = (lax.axis_index("x") + member) % X
    row = lax.broadcasted_iota(jnp.int32, (WIDTH, LANES), 0)
    lane = lax.broadcasted_iota(jnp.int32, (WIDTH, LANES), 1)
    ids = jnp.where(row == x_of_ids, ids_of_x[0:1] * (X / COPIES), 0.0)
    edges = jnp.where(lane >= EDGE_IDS, ids, 0.0)
    for i in range(COPIES):
        projected_out[tile(2 * i)] = whole[tile(i)] + edges
        projected_out[tile(2 * i + 1)] = ids
    ghosts = jnp.concatenate([left[ORB_AT : ORB_AT + WIDTH], right[ORB_AT : ORB_AT + WIDTH]], 0)
    ghost_kin = dot(ghosts.astype(BF16), stiff[...])
    for i, e, base_row in (
        (0, HALO - 1, left[BASE_AT + HALO - 1 : BASE_AT + HALO]),
        (1, 2 * STRIP - HALO, right[BASE_AT : BASE_AT + 1]),
    ):
        for t in range(4):
            ghost_out[tile(i), cols(t)] = (
                factor[tile(e)] * ghost_kin[tile(i), cols(t)] + base_row[:, cols(t)] * ghosts[tile(i), cols(t)]
            )
    for copy in copies:
        copy.wait()


def sum_kernel(gathered, asking, unpack, out):
    high, rest = split(gathered[...])
    ids = dot(high, unpack[...])
    row = lax.broadcasted_iota(jnp.int32, ids.shape, 0) % WIDTH
    lane = lax.broadcasted_iota(jnp.int32, ids.shape, 1)
    ids = jnp.where(lane // 6 == row, ids, 0.0)
    ids = jnp.sum(ids.reshape(Z, WIDTH, LANES), axis=1)
    lane = lax.broadcasted_iota(jnp.int32, ids.shape, 1)
    row = lax.broadcasted_iota(jnp.int32, ids.shape, 0)
    slots = ((lax.axis_index("x") * Z + row) * HALF + lane - POT).astype(F32)
    known = jnp.where(lane < POT, ids, jnp.where(lane < IDS, slots, -1.0))
    known = jnp.transpose(jnp.concatenate([known, jnp.zeros((LANES - Z, LANES), F32)], 0))
    z_at = lax.axis_index("z")
    before = gathered[pl.ds(pl.multiple_of((z_at + Z - 1) % Z * WIDTH, WIDTH), WIDTH)]
    after = gathered[pl.ds(pl.multiple_of((z_at + 1) % Z * WIDTH, WIDTH), WIDTH)]
    before = jnp.where(z_at == 0, pltpu.roll(before, 1, 0), before)
    after = jnp.where(z_at == Z - 1, pltpu.roll(after, WIDTH - 1, 0), after)
    low_id = before[:, EDGE_IDS + 2 : EDGE_IDS + 3] * HALF + before[:, EDGE_IDS + 3 : EDGE_IDS + 4]
    high_id = after[:, EDGE_IDS : EDGE_IDS + 1] * HALF + after[:, EDGE_IDS + 1 : EDGE_IDS + 2]
    lane, row = lane[:WIDTH], row[:WIDTH]
    slots = ((row * Z + z_at) * HALF + lane - POT).astype(F32)
    wanted = jnp.where(lane < POT, asking[...], jnp.where(lane < IDS, slots, -2.0))
    wanted = jnp.where(lane == IDS, low_id, jnp.where(lane == IDS + 1, high_id, wanted))
    total = jnp.zeros((2 * WIDTH, X * LANES), F32)
    for s in range(0, Z, 2):
        hot = [
            jnp.concatenate(
                [jnp.where(known[:, i : i + 1] == wanted[m : m + 1], 1.0, 0.0).astype(BF16) for m in range(X)], 1
            )
            for i in (s, s + 1)
        ]
        both = [jnp.concatenate([high[tile(i)], rest[tile(i)]], 0) for i in (s, s + 1)]
        total = total + dot(jnp.concatenate(both, 1), jnp.concatenate(hot, 0))
    result = total[:WIDTH] + total[WIDTH:]
    for m in range(X):
        for i in range(COPIES):
            out[tile(m * COPIES + i)] = result[:, cols(m)]


def apply_kernel(columns, orb, linear, ghost, left, right, index, prolong, updated_out, applied_out):
    summed = columns[0:HALF]
    for i in range(1, X):
        summed = summed + columns[i * HALF : (i + 1) * HALF]
    table = jnp.transpose(summed)
    updated_out[...] = table[POT:IDS]
    high, rest = split(table)
    node = dot(high, prolong[...]) + dot(rest, prolong[...])
    low = lane_below(HALF)
    part_before = new_before = index_before = None
    finished = []
    for e in range(CELLS + 2):
        c = e - 1
        if e == 0:
            values, start, node_at = left[ORB_AT : ORB_AT + WIDTH], ghost[tile(0)], IDS
        elif e <= CELLS:
            values = orb[c // 2 * 16 : c // 2 * 16 + 16].astype(F32)[tile(c % 2)]
            start, node_at = linear[tile(c)], c
        else:
            values, start, node_at = right[ORB_AT : ORB_AT + WIDTH], ghost[tile(1)], IDS + 1
        whole = start + node[node_at : node_at + 1] * values
        parts = [whole[:, cols(t)] for t in range(4)]
        if e > 0:
            crossing = jnp.where(low, parts[0], part_before)
            moved = jnp.take_along_axis(crossing, index_before, axis=1, mode="promise_in_bounds")
            if e == 1:
                moved = moved * left[META_AT : META_AT + 1, SLOT]
            if e == CELLS + 1:
                moved = moved * right[HALO_ROWS - 1 : HALO_ROWS, SLOT]
            done = jnp.where(low, new_before[3], new_before[3] + moved)
            if e > 1:
                finished.append(jnp.concatenate([*new_before[:3], done], 1))
            news = [jnp.where(low, parts[0] + moved, parts[0]), *parts[1:]]
        else:
            news = parts
        part_before, new_before = parts[3], news
        if e == 0:
            meta_row = left[META_AT + HALO - 1 : META_AT + HALO]
            index_before = jnp.broadcast_to(meta_row[:, IDX].astype(jnp.int32), (WIDTH, LANES))
        elif e <= CELLS:
            index_before = index[tile(c)]
        if len(finished) == 2:
            applied_out[(e - 3) * WIDTH : (e - 1) * WIDTH] = jnp.concatenate(finished, 0).astype(BF16)
            finished = []


def unpack_table():
    table = np.zeros((LANES, LANES), np.float32)
    for k in range(CELLS):
        table[112 + k % 6, k] = 64.0
        table[118 + k % 6, k] = 1.0
    return table


def local(orbitals, adjoint_source, eigenvalues, cell_scale, base_potential, stiffness, face_perm, restrict,
          prolong, owner, pot_slot, potential):
    vmem = pl.BlockSpec(memory_space=pltpu.VMEM)
    params = pltpu.CompilerParams(vmem_limit_bytes=32 * 2**20)
    struct = jax.ShapeDtypeStruct

    orb2 = orbitals.reshape(CELLS * WIDTH, NODES)
    src2 = adjoint_source.reshape(CELLS * WIDTH, NODES)
    owner1 = owner.reshape(CELLS)
    hbm = pl.BlockSpec(memory_space=pltpu.HBM)
    to_mate, to_other, ids, factor, eig, stiff = pl.pallas_call(
        pack_kernel,
        out_shape=(
            struct((HALO_ROWS, NODES), F32),
            struct((HALO_ROWS, NODES), F32),
            struct((WIDTH, LANES), F32),
            struct((CELLS, LANES), F32),
            struct((WIDTH, LANES), F32),
            struct((NODES, NODES), BF16),
        ),
        in_specs=[hbm] * 9,
        out_specs=(vmem,) * 6,
        scratch_shapes=[
            pltpu.SMEM((CELLS,), F32),
            pltpu.SMEM((CELLS,), jnp.int32),
            pltpu.SMEM((CELLS,), jnp.int32),
            pltpu.VMEM((2, SRC_ROWS, NODES), BF16),
            pltpu.VMEM((2, 16, NODES), BF16),
            pltpu.VMEM((2, WIDTH, NODES), F32),
            pltpu.VMEM((2, WIDTH, HALF), jnp.int32),
            pltpu.SMEM((WIDTH,), F32),
            pltpu.VMEM((HALO_ROWS, NODES), F32),
            pltpu.VMEM((HALO_ROWS, NODES), F32),
            pltpu.SemaphoreType.DMA((13,)),
        ],
        compiler_params=params,
    )(*map(in_hbm, (cell_scale, owner1, pot_slot, src2, orb2, base_potential, face_perm, stiffness, eigenvalues)))

    of_mate = lax.ppermute(to_mate, DOM, [(i, i ^ 1) for i in range(X * Z)])
    of_other = lax.ppermute(to_other, DOM, [(i, i + 1 if i % 2 else i - 1) for i in range(1, X * Z - 1)])
    ids_of_x = lax.ppermute(ids, OUTER, [((i // COPIES + i) % X * COPIES + i % COPIES, i) for i in range(X * COPIES)])

    rows = CELLS * WIDTH
    inner = rows - 2 * HALO * WIDTH
    adjoint_mid, projected_mid, linear, index, restrict_t = pl.pallas_call(
        interior_kernel,
        out_shape=(
            struct((inner, NODES), BF16),
            struct((HALF, LANES), F32),
            struct((rows, NODES), F32),
            struct((rows, LANES), jnp.int32),
            struct((HALF, NODES), BF16),
        ),
        in_specs=[hbm] * 4 + [vmem] * 7,
        out_specs=(vmem,) * 5,
        scratch_shapes=[pltpu.VMEM((rows, NODES), F32)] * 4
        + [
            pltpu.SMEM((CELLS,), jnp.int32),
            pltpu.SMEM((CELLS,), jnp.int32),
            pltpu.VMEM((HALF, HALF), F32),
            pltpu.SemaphoreType.DMA((4,)),
        ],
        compiler_params=params,
        cost_estimate=pl.CostEstimate(flops=5 * 2 * rows * NODES * NODES, bytes_accessed=4 * 2**20, transcendentals=0),
    )(*map(in_hbm, (owner1, pot_slot, restrict.T, potential)), src2, orb2, base_potential, face_perm, factor, eig, stiff)

    strip_rows = 2 * STRIP * WIDTH
    adjoint2, projected, ghost, left, right = pl.pallas_call(
        boundary_kernel,
        out_shape=(
            struct((rows, NODES), BF16),
            struct((2 * HALF, LANES), F32),
            struct((2 * WIDTH, NODES), F32),
            struct((HALO_ROWS, NODES), F32),
            struct((HALO_ROWS, NODES), F32),
        ),
        in_specs=[vmem] * 13,
        out_specs=(hbm, vmem, vmem, vmem, vmem),
        scratch_shapes=[pltpu.VMEM((strip_rows, NODES), F32)] * 4
        + [
            pltpu.VMEM((strip_rows, LANES), F32),
            pltpu.VMEM((strip_rows, LANES), jnp.int32),
            pltpu.VMEM((2, HALO * WIDTH, NODES), BF16),
            pltpu.SemaphoreType.DMA((3,)),
        ],
        compiler_params=params,
    )(src2, orb2, base_potential, index, factor, eig, of_mate, of_other, ids_of_x, stiff, restrict_t, adjoint_mid,
      projected_mid)

    def exchanged(array, axes):
        return lax.all_to_all(array, axes, split_axis=0, concat_axis=0, tiled=True)

    tiles = jnp.sum(exchanged(projected.reshape(COPIES, 2 * WIDTH, LANES), ORB), axis=0)
    mine = jnp.broadcast_to(tiles[None, :WIDTH], (Z, WIDTH, LANES))
    mine, asking = lax.optimization_barrier((mine, tiles[WIDTH:]))
    gathered = exchanged(mine, ("z",))
    columns = pl.pallas_call(
        sum_kernel,
        out_shape=struct((X * HALF, LANES), F32),
        in_specs=[vmem] * 3,
        out_specs=vmem,
        compiler_params=params,
    )(gathered.reshape(Z * WIDTH, LANES), asking, jnp.asarray(unpack_table(), BF16))
    columns = exchanged(columns.reshape(X * COPIES, WIDTH, LANES), OUTER)
    updated, applied2 = pl.pallas_call(
        apply_kernel,
        out_shape=(struct((HALF, HALF), F32), struct((rows, NODES), BF16)),
        in_specs=[vmem] * 8,
        out_specs=(vmem, vmem),
        compiler_params=params,
    )(columns.reshape(X * HALF, LANES), orb2, linear, ghost, left, right, index, prolong)
    return adjoint2.reshape(orbitals.shape), updated, applied2.reshape(orbitals.shape)


def solution(mesh):
    axes = jax.sharding.Mesh(mesh.devices.reshape(X, Z, Y, CORES), ("x", "z", "y", "core"))
    in_specs = (
        P(DOM, ORB, None),
        P(DOM, ORB, None),
        P(ORB),
        P(DOM),
        P(DOM, None),
        P(),
        P(DOM, None),
        P(),
        P(),
        P(DOM, None),
        P(DOM),
        P(DOM, None),
    )
    out_specs = (P(DOM, ORB, None), P(DOM, None), P(DOM, ORB, None))
    return jax.shard_map(local, mesh=axes, in_specs=in_specs, out_specs=out_specs, check_vma=False)
```

```python
import jax
import jax.numpy as jnp
import numpy as np
from jax import lax
from jax.experimental import pallas as pl
from jax.experimental.pallas import tpu as pltpu
from jax.sharding import PartitionSpec as P

ITERS = 4
relax = 0.25
step_rate = 0.1

LANES = 128
HALF = 64
NODES = 512
WIDTH = 8
CELLS = 48
HALO = 4
EXT = CELLS + 2 * HALO
F32, BF16 = jnp.float32, jnp.bfloat16


def dot(a, b, contract=((1,), (0,))):
    return lax.dot_general(a, b, (contract, ((), ())), preferred_element_type=F32)


def split(a):
    high = a.astype(BF16)
    return high, (a - high.astype(F32)).astype(BF16)


def lane_below(bound):
    return lax.broadcasted_iota(jnp.int32, (WIDTH, LANES), 1) < bound


SRC_ROWS, ORB_AT, BASE_AT, META_AT, HALO_ROWS = 32, 32, 40, 44, 48
IDX, SCALE, OWNER, SLOT = slice(0, 128), slice(128, 256), slice(256, 384), slice(384, 512)
POT, IDS, EDGE_IDS = CELLS, CELLS + HALF, CELLS + HALF + 12
X, Z, Y, CORES = 4, 16, 4, 2
DOM, ORB, OUTER = ("x", "z"), ("y", "core"), ("x", "y", "core")
COPIES = Y * CORES
STRIP = 3 * HALO
NT = ((1,), (1,))


def tile(e):
    return slice(e * WIDTH, (e + 1) * WIDTH)


def cols(t):
    return slice(t * LANES, (t + 1) * LANES)


def face_rows(perm, wanted_cells):
    twice = jnp.concatenate([perm, perm], 1).astype(F32)
    columns = jnp.transpose(twice)[0:HALF]
    node = lax.broadcasted_iota(jnp.int32, (HALF, LANES), 0).astype(F32)
    lane = lax.broadcasted_iota(jnp.int32, (HALF, LANES), 1).astype(F32)
    low = lax.broadcasted_iota(jnp.int32, (1, LANES), 1) < HALF
    rows = []
    for c in wanted_cells:
        inverse = jnp.sum(jnp.where(columns[:, c : c + 1] == lane, node, 0.0), axis=0, keepdims=True)
        rows.append(jnp.where(low, inverse + HALF, twice[c : c + 1]))
    return rows


def face_tiles(perm):
    half = CELLS // 2
    perm = perm.astype(F32)
    pairs = jnp.concatenate([perm[:half], perm[half:]], 1)
    twice = jnp.concatenate([perm, perm], 1)
    node = lax.broadcasted_iota(jnp.int32, (HALF, LANES), 0).astype(F32)
    row = lax.broadcasted_iota(jnp.int32, (WIDTH, LANES), 0)
    lane = lax.broadcasted_iota(jnp.int32, (WIDTH, LANES), 1)
    counts = jnp.where(lane // HALF == row, lane % HALF, 0).astype(F32).astype(BF16)
    empty = jnp.zeros((HALF, LANES), BF16)
    tiles = [None] * CELLS
    for p in range(half):
        hot = jnp.where(pairs[p : p + 1] == node, 1.0, 0.0).astype(BF16)
        inverse = dot(counts, jnp.concatenate([hot, empty], 0), NT)
        for i, c in enumerate((p, p + half)):
            rows = jnp.where(lane[:1] < HALF, inverse[i : i + 1] + HALF, twice[c : c + 1])
            tiles[c] = jnp.broadcast_to(rows.astype(jnp.int32), (WIDTH, LANES))
    return tiles


def in_hbm(array):
    return pltpu.with_memory_space_constraint(array, pltpu.HBM)


def pack_kernel(scale_hbm, owner_hbm, slot_hbm, src_hbm, orb_hbm, base_hbm, perm_hbm, stiff_hbm, eig_hbm,
                to_mate, to_other, ids_out, factor_out, eig_out, stiff_out,
                scale, owner, slot, src, orb, base, perm, eig, to_left, to_right, sems):
    top, rows = CELLS - WIDTH, CELLS * WIDTH
    copies = [(scale_hbm, scale), (owner_hbm, owner), (slot_hbm, slot)]
    for hbm, here, size, end in (
        (src_hbm, src, SRC_ROWS, rows), (orb_hbm, orb, 16, rows), (base_hbm, base, WIDTH, CELLS), (perm_hbm, perm, WIDTH, CELLS)
    ):
        copies.append((hbm.at[0:size], here.at[0]))
        copies.append((hbm.at[end - size : end], here.at[1]))
    copies += [(eig_hbm, eig), (stiff_hbm, stiff_out)]
    copies = [pltpu.make_async_copy(one, two, sems.at[i]) for i, (one, two) in enumerate(copies)]
    for copy in copies:
        copy.start()
    for copy in copies[:-1]:
        copy.wait()
    row = lax.broadcasted_iota(jnp.int32, (WIDTH, LANES), 0)
    eig_tile = jnp.zeros((WIDTH, LANES), F32)
    for i in range(WIDTH):
        eig_tile = jnp.where(row == i, eig[i], eig_tile)
    eig_out[...] = eig_tile
    for c in range(CELLS):
        factor_out[c : c + 1] = jnp.full((1, LANES), scale[c], F32)
    for end, out in enumerate((to_left, to_right)):
        inner, first = (0, 0) if end == 0 else (HALO, CELLS - HALO)
        edge_cell = end * (CELLS - 1)
        out[0:SRC_ROWS] = src[end].astype(F32)
        out[ORB_AT : ORB_AT + WIDTH] = orb[end].astype(F32)[tile(end)]
        out[BASE_AT : BASE_AT + HALO] = base[end, inner : inner + HALO]
        faces = face_rows(perm[end], range(inner, inner + HALO))
        for i in range(HALO):
            at = slice(META_AT + i, META_AT + i + 1)
            out[at, IDX] = faces[i]
            out[at, SCALE] = jnp.full((1, LANES), scale[first + i], F32)
            out[at, OWNER] = jnp.full((1, LANES), owner[edge_cell].astype(F32), F32)
            mark = slot[edge_cell].astype(F32) if i == end * (HALO - 1) else 1.0
            out[at, SLOT] = jnp.full((1, LANES), mark, F32)
    lane = lax.broadcasted_iota(jnp.int32, (WIDTH, LANES), 1)
    ids = [jnp.zeros((WIDTH, LANES), F32)] * 4
    for c in range(CELLS):
        ids[c % 4] = jnp.where(lane == c, (owner[c] * HALF + slot[c]).astype(F32), ids[c % 4])
    for i, value in enumerate((owner[0], slot[0], owner[CELLS - 1], slot[CELLS - 1])):
        ids[i] = jnp.where(lane == EDGE_IDS + i, value.astype(F32), ids[i])
    ids_out[...] = (ids[0] + ids[1]) + (ids[2] + ids[3])
    even = lax.axis_index("z") % 2 == 0
    to_mate[...] = jnp.where(even, to_right[...], to_left[...])
    to_other[...] = jnp.where(even, to_left[...], to_right[...])
    copies[-1].wait()


def relax_step(strips, x, quarter, shifted, kin, stiff, factor, index, gates):
    low = lane_below(HALF)
    held = [x[strip[0] * WIDTH : (strip[-1] + 1) * WIDTH].astype(BF16) for strip in strips]
    held = held[0] if len(held) == 1 else jnp.concatenate(held, 0)
    kin[0 : held.shape[0]] = dot(held, stiff[...])
    at = 0
    for strip in strips:
        part_before = new_before = None
        for e in strip:
            rows = tile(e)
            scale = factor(e)
            parts, news = [], []
            for t in range(4):
                here = x[rows, cols(t)]
                part = scale * kin[tile(at), cols(t)] + shifted[rows, cols(t)] * here
                parts.append(part)
                news.append(here + quarter[rows, cols(t)] - relax * part)
            at += 1
            if e > strip[0]:
                crossing = jnp.where(low, parts[0], part_before)
                moved = relax * jnp.take_along_axis(crossing, index[tile(e - 1)], axis=1, mode="promise_in_bounds")
                if e in gates:
                    moved = moved * gates[e]
                news[0] = jnp.where(low, news[0] - moved, news[0])
                x[tile(e - 1), cols(3)] = jnp.where(low, new_before, new_before - moved)
            for t in range(3):
                x[rows, cols(t)] = news[t]
            part_before, new_before = parts[3], news[3]
        x[tile(strip[-1]), cols(3)] = new_before


def group_of(row_cells):
    shape = (LANES, len(row_cells) * WIDTH)
    cell = lax.broadcasted_iota(jnp.int32, shape, 0)
    at = lax.broadcasted_iota(jnp.int32, shape, 1) // WIDTH
    gap = [i for i in range(1, len(row_cells)) if row_cells[i] != row_cells[i - 1] + 1]
    owner = at + row_cells[0]
    for i in gap:
        owner = owner + jnp.where(at >= i, row_cells[i] - row_cells[i - 1] - 1, 0)
    return jnp.where(cell == owner, 1.0, 0.0).astype(BF16)


def projection(orb_values, x_values, group, restrict_t):
    high, rest = split(orb_values.astype(F32) * x_values)
    density = dot(group, high) + dot(group, rest)
    high, rest = split(density)
    return dot(restrict_t, high, NT) + dot(restrict_t, rest, NT)


def interior_kernel(owner_hbm, slot_hbm, restrict_hbm, potential_hbm, src, orb, base, perm, factor, eig, stiff,
                    adjoint_out, projected_out, linear_out, index_out, restrict_t,
                    x, quarter, kin, shifted, owner, slot, potential, sems):
    pairs = ((restrict_hbm, restrict_t), (potential_hbm, potential), (owner_hbm, owner), (slot_hbm, slot))
    copies = [pltpu.make_async_copy(one, two, sems.at[i]) for i, (one, two) in enumerate(pairs)]
    for copy in copies:
        copy.start()
    quarter[...] = relax * src[...].astype(F32)
    x[...] = quarter[...]
    faces = face_tiles(perm[...])
    eig_tile = eig[...]

    def scale(c):
        return jnp.broadcast_to(factor[c : c + 1], (WIDTH, LANES))

    for c in range(CELLS):
        for t in range(4):
            shifted[tile(c), cols(t)] = base[c : c + 1, cols(t)] - eig_tile
        index_out[tile(c)] = faces[c]

    def step(_, carry):
        relax_step([range(CELLS)], x, quarter, shifted, kin, stiff, scale, index_out, {})
        return carry

    lax.fori_loop(0, ITERS, step, 0)
    for copy in copies:
        copy.wait()
    inner = slice(HALO * WIDTH, (CELLS - HALO) * WIDTH)
    adjoint_out[...] = x[inner].astype(BF16)
    kin[...] = dot(orb[...], stiff[...])
    for pair in range(CELLS // 2):
        values = orb[pair * 16 : pair * 16 + 16].astype(F32)
        for c in (2 * pair, 2 * pair + 1):
            for t in range(4):
                linear_out[tile(c), cols(t)] = (
                    scale(c) * kin[tile(c), cols(t)] + base[c : c + 1, cols(t)] * values[tile(c % 2), cols(t)]
                )
    row = lax.broadcasted_iota(jnp.int32, (WIDTH, LANES), 0)
    lane = lax.broadcasted_iota(jnp.int32, (WIDTH, LANES), 1)
    at = jnp.where((lane >= IDS) & (lane < EDGE_IDS), row * 12 + lane - IDS, -1)
    ids = jnp.zeros((WIDTH, LANES), F32)
    for c in range(CELLS):
        ids = jnp.where(at == c // 6 * 12 + c % 6, owner[c].astype(F32), ids)
        ids = jnp.where(at == c // 6 * 12 + 6 + c % 6, slot[c].astype(F32), ids)
    turned = jnp.transpose(potential[...])
    static = jnp.concatenate([jnp.zeros((HALF, CELLS), F32), turned, jnp.zeros((HALF, 16), F32)], 1)
    static = (static + jnp.concatenate([ids] * (HALF // WIDTH), 0)) * (1.0 / COPIES)
    projected_out[...] = static - step_rate * projection(
        orb[inner], x[inner], group_of(range(HALO, CELLS - HALO)), restrict_t[...]
    )


def boundary_kernel(src, orb, base, index_own, factor_own, eig, of_mate, of_other, ids_of_x, stiff, restrict_t,
                    projected_mid, adjoint_ends, projected_out, ghost_out, left, right,
                    x, quarter, kin, shifted, factor, index):
    near, edge = 2 * HALO * WIDTH, HALO * WIDTH
    last = CELLS * WIDTH
    even = lax.axis_index("z") % 2 == 0
    left[...] = jnp.where(even, of_other[...], of_mate[...])
    right[...] = jnp.where(even, of_mate[...], of_other[...])
    quarter[0:edge] = relax * left[0:SRC_ROWS]
    quarter[edge : edge + near] = relax * src[0:near].astype(F32)
    quarter[edge + near : edge + 2 * near] = relax * src[last - near :].astype(F32)
    quarter[edge + 2 * near :] = relax * right[0:SRC_ROWS]
    x[...] = quarter[...]
    eig_tile = eig[...]
    for e in range(2 * STRIP):
        ghost = left if e < HALO else right if e >= 2 * STRIP - HALO else None
        if ghost is None:
            c = e - HALO if e < STRIP else CELLS - 2 * HALO + e - STRIP
            base_row = base[c : c + 1]
            factor[tile(e)] = jnp.broadcast_to(factor_own[c : c + 1], (WIDTH, LANES))
            index[tile(e)] = index_own[tile(c)]
        else:
            i = e if e < HALO else e - 2 * STRIP + HALO
            base_row = ghost[BASE_AT + i : BASE_AT + i + 1]
            meta_row = ghost[META_AT + i : META_AT + i + 1]
            factor[tile(e)] = jnp.broadcast_to(meta_row[:, SCALE], (WIDTH, LANES))
            index[tile(e)] = jnp.broadcast_to(meta_row[:, IDX].astype(jnp.int32), (WIDTH, LANES))
        for t in range(4):
            shifted[tile(e), cols(t)] = base_row[:, cols(t)] - eig_tile
    gates = {HALO: left[META_AT : META_AT + 1, SLOT], 2 * STRIP - HALO: right[HALO_ROWS - 1 : HALO_ROWS, SLOT]}
    for k in range(ITERS):
        strips = [range(k, STRIP - k), range(STRIP + k, 2 * STRIP - k)]
        relax_step(strips, x, quarter, shifted, kin, stiff, lambda e: factor[tile(e)], index, gates)
    low_cells, high_cells = x[edge : 2 * edge], x[4 * edge : 5 * edge]
    adjoint_ends[0] = low_cells.astype(BF16)
    adjoint_ends[1] = high_cells.astype(BF16)
    own_orb = jnp.concatenate([orb[0:edge], orb[last - edge :]], 0)
    own_x = jnp.concatenate([low_cells, high_cells], 0)
    added = projection(own_orb, own_x, group_of([*range(HALO), *range(CELLS - HALO, CELLS)]), restrict_t[...])
    whole = projected_mid[...] - step_rate * added
    member = lax.axis_index("y") * CORES + lax.axis_index("core")
    x_of_ids = (lax.axis_index("x") + member) % X
    row = lax.broadcasted_iota(jnp.int32, (WIDTH, LANES), 0)
    lane = lax.broadcasted_iota(jnp.int32, (WIDTH, LANES), 1)
    ids = jnp.where(row == x_of_ids, ids_of_x[0:1] * (X / COPIES), 0.0)
    edges = jnp.where(lane >= EDGE_IDS, ids, 0.0)
    for i in range(COPIES):
        projected_out[tile(2 * i)] = whole[tile(i)] + edges
        projected_out[tile(2 * i + 1)] = ids
    ghosts = jnp.concatenate([left[ORB_AT : ORB_AT + WIDTH], right[ORB_AT : ORB_AT + WIDTH]], 0)
    ghost_kin = dot(ghosts.astype(BF16), stiff[...])
    for i, e, base_row in (
        (0, HALO - 1, left[BASE_AT + HALO - 1 : BASE_AT + HALO]),
        (1, 2 * STRIP - HALO, right[BASE_AT : BASE_AT + 1]),
    ):
        for t in range(4):
            ghost_out[tile(i), cols(t)] = (
                factor[tile(e)] * ghost_kin[tile(i), cols(t)] + base_row[:, cols(t)] * ghosts[tile(i), cols(t)]
            )


def sum_kernel(gathered, asking, unpack, adjoint_mid, adjoint_ends, out, adjoint_out, sems):
    edge, last = HALO * WIDTH, CELLS * WIDTH
    copies = [
        pltpu.make_async_copy(adjoint_mid, adjoint_out.at[edge : last - edge], sems.at[0]),
        pltpu.make_async_copy(adjoint_ends.at[0], adjoint_out.at[0:edge], sems.at[1]),
        pltpu.make_async_copy(adjoint_ends.at[1], adjoint_out.at[last - edge : last], sems.at[2]),
    ]
    for copy in copies:
        copy.start()
    high, rest = split(gathered[...])
    ids = dot(high, unpack[...])
    row = lax.broadcasted_iota(jnp.int32, ids.shape, 0) % WIDTH
    lane = lax.broadcasted_iota(jnp.int32, ids.shape, 1)
    ids = jnp.where(lane // 6 == row, ids, 0.0)
    ids = jnp.sum(ids.reshape(Z, WIDTH, LANES), axis=1)
    lane = lax.broadcasted_iota(jnp.int32, ids.shape, 1)
    row = lax.broadcasted_iota(jnp.int32, ids.shape, 0)
    slots = ((lax.axis_index("x") * Z + row) * HALF + lane - POT).astype(F32)
    known = jnp.where(lane < POT, ids, jnp.where(lane < IDS, slots, -1.0))
    known = jnp.transpose(jnp.concatenate([known, jnp.zeros((LANES - Z, LANES), F32)], 0))
    z_at = lax.axis_index("z")
    before = gathered[pl.ds(pl.multiple_of((z_at + Z - 1) % Z * WIDTH, WIDTH), WIDTH)]
    after = gathered[pl.ds(pl.multiple_of((z_at + 1) % Z * WIDTH, WIDTH), WIDTH)]
    before = jnp.where(z_at == 0, pltpu.roll(before, 1, 0), before)
    after = jnp.where(z_at == Z - 1, pltpu.roll(after, WIDTH - 1, 0), after)
    low_id = before[:, EDGE_IDS + 2 : EDGE_IDS + 3] * HALF + before[:, EDGE_IDS + 3 : EDGE_IDS + 4]
    high_id = after[:, EDGE_IDS : EDGE_IDS + 1] * HALF + after[:, EDGE_IDS + 1 : EDGE_IDS + 2]
    lane, row = lane[:WIDTH], row[:WIDTH]
    slots = ((row * Z + z_at) * HALF + lane - POT).astype(F32)
    wanted = jnp.where(lane < POT, asking[...], jnp.where(lane < IDS, slots, -2.0))
    wanted = jnp.where(lane == IDS, low_id, jnp.where(lane == IDS + 1, high_id, wanted))
    total = jnp.zeros((2 * WIDTH, X * LANES), F32)
    for s in range(0, Z, 2):
        hot = [
            jnp.concatenate(
                [jnp.where(known[:, i : i + 1] == wanted[m : m + 1], 1.0, 0.0).astype(BF16) for m in range(X)], 1
            )
            for i in (s, s + 1)
        ]
        both = [jnp.concatenate([high[tile(i)], rest[tile(i)]], 0) for i in (s, s + 1)]
        total = total + dot(jnp.concatenate(both, 1), jnp.concatenate(hot, 0))
    result = total[:WIDTH] + total[WIDTH:]
    for m in range(X):
        for i in range(COPIES):
            out[tile(m * COPIES + i)] = result[:, cols(m)]
    for copy in copies:
        copy.wait()


def apply_kernel(columns, orb, linear, ghost, left, right, index, prolong, updated_out, applied_out):
    summed = columns[0:HALF]
    for i in range(1, X):
        summed = summed + columns[i * HALF : (i + 1) * HALF]
    table = jnp.transpose(summed)
    updated_out[...] = table[POT:IDS]
    high, rest = split(table)
    node = dot(high, prolong[...]) + dot(rest, prolong[...])
    low = lane_below(HALF)
    part_before = new_before = index_before = None
    finished = []
    for e in range(CELLS + 2):
        c = e - 1
        if e == 0:
            values, start, node_at = left[ORB_AT : ORB_AT + WIDTH], ghost[tile(0)], IDS
        elif e <= CELLS:
            values = orb[c // 2 * 16 : c // 2 * 16 + 16].astype(F32)[tile(c % 2)]
            start, node_at = linear[tile(c)], c
        else:
            values, start, node_at = right[ORB_AT : ORB_AT + WIDTH], ghost[tile(1)], IDS + 1
        whole = start + node[node_at : node_at + 1] * values
        parts = [whole[:, cols(t)] for t in range(4)]
        if e > 0:
            crossing = jnp.where(low, parts[0], part_before)
            moved = jnp.take_along_axis(crossing, index_before, axis=1, mode="promise_in_bounds")
            if e == 1:
                moved = moved * left[META_AT : META_AT + 1, SLOT]
            if e == CELLS + 1:
                moved = moved * right[HALO_ROWS - 1 : HALO_ROWS, SLOT]
            done = jnp.where(low, new_before[3], new_before[3] + moved)
            if e > 1:
                finished.append(jnp.concatenate([*new_before[:3], done], 1))
            news = [jnp.where(low, parts[0] + moved, parts[0]), *parts[1:]]
        else:
            news = parts
        part_before, new_before = parts[3], news
        if e == 0:
            meta_row = left[META_AT + HALO - 1 : META_AT + HALO]
            index_before = jnp.broadcast_to(meta_row[:, IDX].astype(jnp.int32), (WIDTH, LANES))
        elif e <= CELLS:
            index_before = index[tile(c)]
        if len(finished) == 2:
            applied_out[(e - 3) * WIDTH : (e - 1) * WIDTH] = jnp.concatenate(finished, 0).astype(BF16)
            finished = []


def unpack_table():
    table = np.zeros((LANES, LANES), np.float32)
    for k in range(CELLS):
        table[112 + k % 6, k] = 64.0
        table[118 + k % 6, k] = 1.0
    return table


def local(orbitals, adjoint_source, eigenvalues, cell_scale, base_potential, stiffness, face_perm, restrict,
          prolong, owner, pot_slot, potential):
    vmem = pl.BlockSpec(memory_space=pltpu.VMEM)
    params = pltpu.CompilerParams(vmem_limit_bytes=32 * 2**20)
    struct = jax.ShapeDtypeStruct

    orb2 = orbitals.reshape(CELLS * WIDTH, NODES)
    src2 = adjoint_source.reshape(CELLS * WIDTH, NODES)
    owner1 = owner.reshape(CELLS)
    hbm = pl.BlockSpec(memory_space=pltpu.HBM)
    to_mate, to_other, ids, factor, eig, stiff = pl.pallas_call(
        pack_kernel,
        out_shape=(
            struct((HALO_ROWS, NODES), F32),
            struct((HALO_ROWS, NODES), F32),
            struct((WIDTH, LANES), F32),
            struct((CELLS, LANES), F32),
            struct((WIDTH, LANES), F32),
            struct((NODES, NODES), BF16),
        ),
        in_specs=[hbm] * 9,
        out_specs=(vmem,) * 6,
        scratch_shapes=[
            pltpu.SMEM((CELLS,), F32),
            pltpu.SMEM((CELLS,), jnp.int32),
            pltpu.SMEM((CELLS,), jnp.int32),
            pltpu.VMEM((2, SRC_ROWS, NODES), BF16),
            pltpu.VMEM((2, 16, NODES), BF16),
            pltpu.VMEM((2, WIDTH, NODES), F32),
            pltpu.VMEM((2, WIDTH, HALF), jnp.int32),
            pltpu.SMEM((WIDTH,), F32),
            pltpu.VMEM((HALO_ROWS, NODES), F32),
            pltpu.VMEM((HALO_ROWS, NODES), F32),
            pltpu.SemaphoreType.DMA((13,)),
        ],
        compiler_params=params,
    )(*map(in_hbm, (cell_scale, owner1, pot_slot, src2, orb2, base_potential, face_perm, stiffness, eigenvalues)))

    of_mate = lax.ppermute(to_mate, DOM, [(i, i ^ 1) for i in range(X * Z)])
    of_other = lax.ppermute(to_other, DOM, [(i, i + 1 if i % 2 else i - 1) for i in range(1, X * Z - 1)])
    ids_of_x = lax.ppermute(ids, OUTER, [((i // COPIES + i) % X * COPIES + i % COPIES, i) for i in range(X * COPIES)])

    rows = CELLS * WIDTH
    inner = rows - 2 * HALO * WIDTH
    adjoint_mid, projected_mid, linear, index, restrict_t = pl.pallas_call(
        interior_kernel,
        out_shape=(
            struct((inner, NODES), BF16),
            struct((HALF, LANES), F32),
            struct((rows, NODES), F32),
            struct((rows, LANES), jnp.int32),
            struct((HALF, NODES), BF16),
        ),
        in_specs=[hbm] * 4 + [vmem] * 7,
        out_specs=(vmem,) * 5,
        scratch_shapes=[pltpu.VMEM((rows, NODES), F32)] * 4
        + [
            pltpu.SMEM((CELLS,), jnp.int32),
            pltpu.SMEM((CELLS,), jnp.int32),
            pltpu.VMEM((HALF, HALF), F32),
            pltpu.SemaphoreType.DMA((4,)),
        ],
        compiler_params=params,
        cost_estimate=pl.CostEstimate(flops=5 * 2 * rows * NODES * NODES, bytes_accessed=4 * 2**20, transcendentals=0),
    )(*map(in_hbm, (owner1, pot_slot, restrict.T, potential)), src2, orb2, base_potential, face_perm, factor, eig, stiff)

    strip_rows = 2 * STRIP * WIDTH
    adjoint_ends, projected, ghost, left, right = pl.pallas_call(
        boundary_kernel,
        out_shape=(
            struct((2, HALO * WIDTH, NODES), BF16),
            struct((2 * HALF, LANES), F32),
            struct((2 * WIDTH, NODES), F32),
            struct((HALO_ROWS, NODES), F32),
            struct((HALO_ROWS, NODES), F32),
        ),
        in_specs=[vmem] * 12,
        out_specs=(vmem,) * 5,
        scratch_shapes=[pltpu.VMEM((strip_rows, NODES), F32)] * 4
        + [
            pltpu.VMEM((strip_rows, LANES), F32),
            pltpu.VMEM((strip_rows, LANES), jnp.int32),
        ],
        compiler_params=params,
    )(src2, orb2, base_potential, index, factor, eig, of_mate, of_other, ids_of_x, stiff, restrict_t,
      projected_mid)

    def exchanged(array, axes):
        return lax.all_to_all(array, axes, split_axis=0, concat_axis=0, tiled=True)

    tiles = jnp.sum(exchanged(projected.reshape(COPIES, 2 * WIDTH, LANES), ORB), axis=0)
    mine = jnp.broadcast_to(tiles[None, :WIDTH], (Z, WIDTH, LANES))
    mine, asking = lax.optimization_barrier((mine, tiles[WIDTH:]))
    gathered = exchanged(mine, ("z",))
    columns, adjoint2 = pl.pallas_call(
        sum_kernel,
        out_shape=(struct((X * HALF, LANES), F32), struct((rows, NODES), BF16)),
        in_specs=[vmem] * 5,
        out_specs=(vmem, hbm),
        scratch_shapes=[pltpu.SemaphoreType.DMA((3,))],
        compiler_params=params,
    )(gathered.reshape(Z * WIDTH, LANES), asking, jnp.asarray(unpack_table(), BF16),
      adjoint_mid, adjoint_ends)
    columns = exchanged(columns.reshape(X * COPIES, WIDTH, LANES), OUTER)
    updated, applied2 = pl.pallas_call(
        apply_kernel,
        out_shape=(struct((HALF, HALF), F32), struct((rows, NODES), BF16)),
        in_specs=[vmem] * 8,
        out_specs=(vmem, vmem),
        compiler_params=params,
    )(columns.reshape(X * HALF, LANES), orb2, linear, ghost, left, right, index, prolong)
    return adjoint2.reshape(orbitals.shape), updated, applied2.reshape(orbitals.shape)


def solution(mesh):
    axes = jax.sharding.Mesh(mesh.devices.reshape(X, Z, Y, CORES), ("x", "z", "y", "core"))
    in_specs = (
        P(DOM, ORB, None),
        P(DOM, ORB, None),
        P(ORB),
        P(DOM),
        P(DOM, None),
        P(),
        P(DOM, None),
        P(),
        P(),
        P(DOM, None),
        P(DOM),
        P(DOM, None),
    )
    out_specs = (P(DOM, ORB, None), P(DOM, None), P(DOM, ORB, None))
    return jax.shard_map(local, mesh=axes, in_specs=in_specs, out_specs=out_specs, check_vma=False)
```

```python
import jax
import jax.numpy as jnp
import numpy as np
from jax import lax
from jax.experimental import pallas as pl
from jax.experimental.pallas import tpu as pltpu
from jax.sharding import PartitionSpec as P

ITERS = 4
relax = 0.25
step_rate = 0.1

LANES = 128
HALF = 64
NODES = 512
WIDTH = 8
CELLS = 48
HALO = 4
EXT = CELLS + 2 * HALO
F32, BF16 = jnp.float32, jnp.bfloat16


def dot(a, b, contract=((1,), (0,))):
    return lax.dot_general(a, b, (contract, ((), ())), preferred_element_type=F32)


def split(a):
    high = a.astype(BF16)
    return high, (a - high.astype(F32)).astype(BF16)


def lane_below(bound):
    return lax.broadcasted_iota(jnp.int32, (WIDTH, LANES), 1) < bound


SRC_ROWS, ORB_AT, BASE_AT, META_AT, HALO_ROWS = 32, 32, 40, 44, 48
IDX, SCALE, OWNER, SLOT = slice(0, 128), slice(128, 256), slice(256, 384), slice(384, 512)
POT, IDS, EDGE_IDS = CELLS, CELLS + HALF, CELLS + HALF + 12
X, Z, Y, CORES = 4, 16, 4, 2
DOM, ORB, OUTER = ("x", "z"), ("y", "core"), ("x", "y", "core")
COPIES = Y * CORES
STRIP = 3 * HALO
NT = ((1,), (1,))


def tile(e):
    return slice(e * WIDTH, (e + 1) * WIDTH)


def cols(t):
    return slice(t * LANES, (t + 1) * LANES)


def face_rows(perm, wanted_cells):
    twice = jnp.concatenate([perm, perm], 1).astype(F32)
    columns = jnp.transpose(twice)[0:HALF]
    node = lax.broadcasted_iota(jnp.int32, (HALF, LANES), 0).astype(F32)
    lane = lax.broadcasted_iota(jnp.int32, (HALF, LANES), 1).astype(F32)
    low = lax.broadcasted_iota(jnp.int32, (1, LANES), 1) < HALF
    rows = []
    for c in wanted_cells:
        inverse = jnp.sum(jnp.where(columns[:, c : c + 1] == lane, node, 0.0), axis=0, keepdims=True)
        rows.append(jnp.where(low, inverse + HALF, twice[c : c + 1]))
    return rows


def face_tiles(perm):
    half = CELLS // 2
    perm = perm.astype(F32)
    pairs = jnp.concatenate([perm[:half], perm[half:]], 1)
    twice = jnp.concatenate([perm, perm], 1)
    node = lax.broadcasted_iota(jnp.int32, (HALF, LANES), 0).astype(F32)
    row = lax.broadcasted_iota(jnp.int32, (WIDTH, LANES), 0)
    lane = lax.broadcasted_iota(jnp.int32, (WIDTH, LANES), 1)
    counts = jnp.where(lane // HALF == row, lane % HALF, 0).astype(F32).astype(BF16)
    empty = jnp.zeros((HALF, LANES), BF16)
    tiles = [None] * CELLS
    for p in range(half):
        hot = jnp.where(pairs[p : p + 1] == node, 1.0, 0.0).astype(BF16)
        inverse = dot(counts, jnp.concatenate([hot, empty], 0), NT)
        for i, c in enumerate((p, p + half)):
            rows = jnp.where(lane[:1] < HALF, inverse[i : i + 1] + HALF, twice[c : c + 1])
            tiles[c] = jnp.broadcast_to(rows.astype(jnp.int32), (WIDTH, LANES))
    return tiles


def in_hbm(array):
    return pltpu.with_memory_space_constraint(array, pltpu.HBM)


def pack_kernel(scale_hbm, owner_hbm, slot_hbm, src_hbm, orb_hbm, base_hbm, perm_hbm, stiff_hbm, eig_hbm,
                to_mate, to_other, ids_out, factor_out, eig_out, stiff_out,
                scale, owner, slot, src, orb, base, perm, eig, to_left, to_right, sems):
    top, rows = CELLS - WIDTH, CELLS * WIDTH
    copies = [(scale_hbm, scale), (owner_hbm, owner), (slot_hbm, slot)]
    for hbm, here, size, end in (
        (src_hbm, src, SRC_ROWS, rows), (orb_hbm, orb, 16, rows), (base_hbm, base, WIDTH, CELLS), (perm_hbm, perm, WIDTH, CELLS)
    ):
        copies.append((hbm.at[0:size], here.at[0]))
        copies.append((hbm.at[end - size : end], here.at[1]))
    copies += [(eig_hbm, eig), (stiff_hbm, stiff_out)]
    copies = [pltpu.make_async_copy(one, two, sems.at[i]) for i, (one, two) in enumerate(copies)]
    for copy in copies:
        copy.start()
    for copy in copies[:-1]:
        copy.wait()
    row = lax.broadcasted_iota(jnp.int32, (WIDTH, LANES), 0)
    eig_tile = jnp.zeros((WIDTH, LANES), F32)
    for i in range(WIDTH):
        eig_tile = jnp.where(row == i, eig[i], eig_tile)
    eig_out[...] = eig_tile
    for c in range(CELLS):
        factor_out[c : c + 1] = jnp.full((1, LANES), scale[c], F32)
    for end, out in enumerate((to_left, to_right)):
        inner, first = (0, 0) if end == 0 else (HALO, CELLS - HALO)
        edge_cell = end * (CELLS - 1)
        out[0:SRC_ROWS] = src[end].astype(F32)
        out[ORB_AT : ORB_AT + WIDTH] = orb[end].astype(F32)[tile(end)]
        out[BASE_AT : BASE_AT + HALO] = base[end, inner : inner + HALO]
        faces = face_rows(perm[end], range(inner, inner + HALO))
        for i in range(HALO):
            at = slice(META_AT + i, META_AT + i + 1)
            out[at, IDX] = faces[i]
            out[at, SCALE] = jnp.full((1, LANES), scale[first + i], F32)
            out[at, OWNER] = jnp.full((1, LANES), owner[edge_cell].astype(F32), F32)
            mark = slot[edge_cell].astype(F32) if i == end * (HALO - 1) else 1.0
            out[at, SLOT] = jnp.full((1, LANES), mark, F32)
    lane = lax.broadcasted_iota(jnp.int32, (1, LANES), 1)
    ids = [jnp.zeros((1, LANES), F32)] * 4
    for c in range(CELLS):
        ids[c % 4] = jnp.where(lane == c, (owner[c] * HALF + slot[c]).astype(F32), ids[c % 4])
    for i, value in enumerate((owner[0], slot[0], owner[CELLS - 1], slot[CELLS - 1])):
        ids[i] = jnp.where(lane == EDGE_IDS + i, value.astype(F32), ids[i])
    ids_out[...] = (ids[0] + ids[1]) + (ids[2] + ids[3])
    even = lax.axis_index("z") % 2 == 0
    to_mate[...] = jnp.where(even, to_right[...], to_left[...])
    to_other[...] = jnp.where(even, to_left[...], to_right[...])
    copies[-1].wait()


def relax_step(strips, x, quarter, shifted, kin, stiff, factor, index, gates):
    low = lane_below(HALF)
    held = [x[strip[0] * WIDTH : (strip[-1] + 1) * WIDTH].astype(BF16) for strip in strips]
    held = held[0] if len(held) == 1 else jnp.concatenate(held, 0)
    kin[0 : held.shape[0]] = dot(held, stiff[...])
    at = 0
    for strip in strips:
        part_before = new_before = None
        for e in strip:
            rows = tile(e)
            scale = factor(e)
            parts, news = [], []
            for t in range(4):
                here = x[rows, cols(t)]
                part = scale * kin[tile(at), cols(t)] + shifted[rows, cols(t)] * here
                parts.append(part)
                news.append(here + quarter[rows, cols(t)] - relax * part)
            at += 1
            if e > strip[0]:
                crossing = jnp.where(low, parts[0], part_before)
                moved = relax * jnp.take_along_axis(crossing, index[tile(e - 1)], axis=1, mode="promise_in_bounds")
                if e in gates:
                    moved = moved * gates[e]
                news[0] = jnp.where(low, news[0] - moved, news[0])
                x[tile(e - 1), cols(3)] = jnp.where(low, new_before, new_before - moved)
            for t in range(3):
                x[rows, cols(t)] = news[t]
            part_before, new_before = parts[3], news[3]
        x[tile(strip[-1]), cols(3)] = new_before


def group_of(row_cells):
    shape = (LANES, len(row_cells) * WIDTH)
    cell = lax.broadcasted_iota(jnp.int32, shape, 0)
    at = lax.broadcasted_iota(jnp.int32, shape, 1) // WIDTH
    gap = [i for i in range(1, len(row_cells)) if row_cells[i] != row_cells[i - 1] + 1]
    owner = at + row_cells[0]
    for i in gap:
        owner = owner + jnp.where(at >= i, row_cells[i] - row_cells[i - 1] - 1, 0)
    return jnp.where(cell == owner, 1.0, 0.0).astype(BF16)


def projection(orb_values, x_values, group, restrict_t):
    high, rest = split(orb_values.astype(F32) * x_values)
    density = dot(group, high) + dot(group, rest)
    high, rest = split(density)
    return dot(restrict_t, high, NT) + dot(restrict_t, rest, NT)


def interior_kernel(owner_hbm, slot_hbm, restrict_hbm, potential_hbm, src, orb, base, perm, factor, eig, stiff,
                    adjoint_out, projected_out, linear_out, index_out, restrict_t,
                    x, quarter, kin, shifted, owner, slot, potential, sems):
    pairs = ((restrict_hbm, restrict_t), (potential_hbm, potential), (owner_hbm, owner), (slot_hbm, slot))
    copies = [pltpu.make_async_copy(one, two, sems.at[i]) for i, (one, two) in enumerate(pairs)]
    for copy in copies:
        copy.start()
    quarter[...] = relax * src[...].astype(F32)
    x[...] = quarter[...]
    faces = face_tiles(perm[...])
    eig_tile = eig[...]

    def scale(c):
        return jnp.broadcast_to(factor[c : c + 1], (WIDTH, LANES))

    for c in range(CELLS):
        for t in range(4):
            shifted[tile(c), cols(t)] = base[c : c + 1, cols(t)] - eig_tile
        index_out[tile(c)] = faces[c]

    def step(_, carry):
        relax_step([range(CELLS)], x, quarter, shifted, kin, stiff, scale, index_out, {})
        return carry

    lax.fori_loop(0, ITERS, step, 0)
    for copy in copies:
        copy.wait()
    inner = slice(HALO * WIDTH, (CELLS - HALO) * WIDTH)
    adjoint_out[...] = x[inner].astype(BF16)
    kin[...] = dot(orb[...], stiff[...])
    for pair in range(CELLS // 2):
        values = orb[pair * 16 : pair * 16 + 16].astype(F32)
        for c in (2 * pair, 2 * pair + 1):
            for t in range(4):
                linear_out[tile(c), cols(t)] = (
                    scale(c) * kin[tile(c), cols(t)] + base[c : c + 1, cols(t)] * values[tile(c % 2), cols(t)]
                )
    row = lax.broadcasted_iota(jnp.int32, (WIDTH, LANES), 0)
    lane = lax.broadcasted_iota(jnp.int32, (WIDTH, LANES), 1)
    at = jnp.where((lane >= IDS) & (lane < EDGE_IDS), row * 12 + lane - IDS, -1)
    ids = jnp.zeros((WIDTH, LANES), F32)
    for c in range(CELLS):
        ids = jnp.where(at == c // 6 * 12 + c % 6, owner[c].astype(F32), ids)
        ids = jnp.where(at == c // 6 * 12 + 6 + c % 6, slot[c].astype(F32), ids)
    turned = jnp.transpose(potential[...])
    static = jnp.concatenate([jnp.zeros((HALF, CELLS), F32), turned, jnp.zeros((HALF, 16), F32)], 1)
    static = (static + jnp.concatenate([ids] * (HALF // WIDTH), 0)) * (1.0 / COPIES)
    projected_out[...] = static - step_rate * projection(
        orb[inner], x[inner], group_of(range(HALO, CELLS - HALO)), restrict_t[...]
    )


def boundary_kernel(src, orb, base, index_own, factor_own, eig, of_mate, of_other, ids_of_x, stiff, restrict_t,
                    projected_mid, adjoint_ends, projected_out, ghost_out, left, right,
                    x, quarter, kin, shifted, factor, index):
    near, edge = 2 * HALO * WIDTH, HALO * WIDTH
    last = CELLS * WIDTH
    even = lax.axis_index("z") % 2 == 0
    left[...] = jnp.where(even, of_other[...], of_mate[...])
    right[...] = jnp.where(even, of_mate[...], of_other[...])
    quarter[0:edge] = relax * left[0:SRC_ROWS]
    quarter[edge : edge + near] = relax * src[0:near].astype(F32)
    quarter[edge + near : edge + 2 * near] = relax * src[last - near :].astype(F32)
    quarter[edge + 2 * near :] = relax * right[0:SRC_ROWS]
    x[...] = quarter[...]
    eig_tile = eig[...]
    for e in range(2 * STRIP):
        ghost = left if e < HALO else right if e >= 2 * STRIP - HALO else None
        if ghost is None:
            c = e - HALO if e < STRIP else CELLS - 2 * HALO + e - STRIP
            base_row = base[c : c + 1]
            factor[tile(e)] = jnp.broadcast_to(factor_own[c : c + 1], (WIDTH, LANES))
            index[tile(e)] = index_own[tile(c)]
        else:
            i = e if e < HALO else e - 2 * STRIP + HALO
            base_row = ghost[BASE_AT + i : BASE_AT + i + 1]
            meta_row = ghost[META_AT + i : META_AT + i + 1]
            factor[tile(e)] = jnp.broadcast_to(meta_row[:, SCALE], (WIDTH, LANES))
            index[tile(e)] = jnp.broadcast_to(meta_row[:, IDX].astype(jnp.int32), (WIDTH, LANES))
        for t in range(4):
            shifted[tile(e), cols(t)] = base_row[:, cols(t)] - eig_tile
    gates = {HALO: left[META_AT : META_AT + 1, SLOT], 2 * STRIP - HALO: right[HALO_ROWS - 1 : HALO_ROWS, SLOT]}
    for k in range(ITERS):
        strips = [range(k, STRIP - k), range(STRIP + k, 2 * STRIP - k)]
        relax_step(strips, x, quarter, shifted, kin, stiff, lambda e: factor[tile(e)], index, gates)
    low_cells, high_cells = x[edge : 2 * edge], x[4 * edge : 5 * edge]
    adjoint_ends[0] = low_cells.astype(BF16)
    adjoint_ends[1] = high_cells.astype(BF16)
    own_orb = jnp.concatenate([orb[0:edge], orb[last - edge :]], 0)
    own_x = jnp.concatenate([low_cells, high_cells], 0)
    added = projection(own_orb, own_x, group_of([*range(HALO), *range(CELLS - HALO, CELLS)]), restrict_t[...])
    whole = projected_mid[...] - step_rate * added
    member = lax.axis_index("y") * CORES + lax.axis_index("core")
    x_of_ids = (lax.axis_index("x") + member) % X
    row = lax.broadcasted_iota(jnp.int32, (WIDTH, LANES), 0)
    lane = lax.broadcasted_iota(jnp.int32, (WIDTH, LANES), 1)
    ids = jnp.where(row == x_of_ids, ids_of_x[...] * (X / COPIES), 0.0)
    edges = jnp.where(lane >= EDGE_IDS, ids, 0.0)
    for i in range(COPIES):
        projected_out[tile(2 * i)] = whole[tile(i)] + edges
        projected_out[tile(2 * i + 1)] = ids
    ghosts = jnp.concatenate([left[ORB_AT : ORB_AT + WIDTH], right[ORB_AT : ORB_AT + WIDTH]], 0)
    ghost_kin = dot(ghosts.astype(BF16), stiff[...])
    for i, e, base_row in (
        (0, HALO - 1, left[BASE_AT + HALO - 1 : BASE_AT + HALO]),
        (1, 2 * STRIP - HALO, right[BASE_AT : BASE_AT + 1]),
    ):
        for t in range(4):
            ghost_out[tile(i), cols(t)] = (
                factor[tile(e)] * ghost_kin[tile(i), cols(t)] + base_row[:, cols(t)] * ghosts[tile(i), cols(t)]
            )


def sum_kernel(gathered, asking, unpack, adjoint_mid, adjoint_ends, out, adjoint_out, sems):
    edge, last = HALO * WIDTH, CELLS * WIDTH
    copies = [
        pltpu.make_async_copy(adjoint_mid, adjoint_out.at[edge : last - edge], sems.at[0]),
        pltpu.make_async_copy(adjoint_ends.at[0], adjoint_out.at[0:edge], sems.at[1]),
        pltpu.make_async_copy(adjoint_ends.at[1], adjoint_out.at[last - edge : last], sems.at[2]),
    ]
    for copy in copies:
        copy.start()
    high, rest = split(gathered[...])
    ids = dot(high, unpack[...])
    row = lax.broadcasted_iota(jnp.int32, ids.shape, 0) % WIDTH
    lane = lax.broadcasted_iota(jnp.int32, ids.shape, 1)
    ids = jnp.where(lane // 6 == row, ids, 0.0)
    ids = jnp.sum(ids.reshape(Z, WIDTH, LANES), axis=1)
    lane = lax.broadcasted_iota(jnp.int32, ids.shape, 1)
    row = lax.broadcasted_iota(jnp.int32, ids.shape, 0)
    slots = ((lax.axis_index("x") * Z + row) * HALF + lane - POT).astype(F32)
    known = jnp.where(lane < POT, ids, jnp.where(lane < IDS, slots, -1.0))
    known = jnp.transpose(jnp.concatenate([known, jnp.zeros((LANES - Z, LANES), F32)], 0))
    z_at = lax.axis_index("z")
    before = gathered[pl.ds(pl.multiple_of((z_at + Z - 1) % Z * WIDTH, WIDTH), WIDTH)]
    after = gathered[pl.ds(pl.multiple_of((z_at + 1) % Z * WIDTH, WIDTH), WIDTH)]
    before = jnp.where(z_at == 0, pltpu.roll(before, 1, 0), before)
    after = jnp.where(z_at == Z - 1, pltpu.roll(after, WIDTH - 1, 0), after)
    low_id = before[:, EDGE_IDS + 2 : EDGE_IDS + 3] * HALF + before[:, EDGE_IDS + 3 : EDGE_IDS + 4]
    high_id = after[:, EDGE_IDS : EDGE_IDS + 1] * HALF + after[:, EDGE_IDS + 1 : EDGE_IDS + 2]
    lane, row = lane[:WIDTH], row[:WIDTH]
    slots = ((row * Z + z_at) * HALF + lane - POT).astype(F32)
    wanted = jnp.where(lane < POT, asking[...], jnp.where(lane < IDS, slots, -2.0))
    wanted = jnp.where(lane == IDS, low_id, jnp.where(lane == IDS + 1, high_id, wanted))
    total = jnp.zeros((2 * WIDTH, X * LANES), F32)
    for s in range(0, Z, 2):
        hot = [
            jnp.concatenate(
                [jnp.where(known[:, i : i + 1] == wanted[m : m + 1], 1.0, 0.0).astype(BF16) for m in range(X)], 1
            )
            for i in (s, s + 1)
        ]
        both = [jnp.concatenate([high[tile(i)], rest[tile(i)]], 0) for i in (s, s + 1)]
        total = total + dot(jnp.concatenate(both, 1), jnp.concatenate(hot, 0))
    result = total[:WIDTH] + total[WIDTH:]
    for m in range(X):
        for i in range(COPIES):
            out[tile(m * COPIES + i)] = result[:, cols(m)]
    for copy in copies:
        copy.wait()


def apply_kernel(columns, orb, linear, ghost, left, right, index, prolong, updated_out, applied_out):
    summed = columns[0:HALF]
    for i in range(1, X):
        summed = summed + columns[i * HALF : (i + 1) * HALF]
    table = jnp.transpose(summed)
    updated_out[...] = table[POT:IDS]
    high, rest = split(table)
    node = dot(high, prolong[...]) + dot(rest, prolong[...])
    low = lane_below(HALF)
    part_before = new_before = index_before = None
    finished = []
    for e in range(CELLS + 2):
        c = e - 1
        if e == 0:
            values, start, node_at = left[ORB_AT : ORB_AT + WIDTH], ghost[tile(0)], IDS
        elif e <= CELLS:
            values = orb[c // 2 * 16 : c // 2 * 16 + 16].astype(F32)[tile(c % 2)]
            start, node_at = linear[tile(c)], c
        else:
            values, start, node_at = right[ORB_AT : ORB_AT + WIDTH], ghost[tile(1)], IDS + 1
        whole = start + node[node_at : node_at + 1] * values
        parts = [whole[:, cols(t)] for t in range(4)]
        if e > 0:
            crossing = jnp.where(low, parts[0], part_before)
            moved = jnp.take_along_axis(crossing, index_before, axis=1, mode="promise_in_bounds")
            if e == 1:
                moved = moved * left[META_AT : META_AT + 1, SLOT]
            if e == CELLS + 1:
                moved = moved * right[HALO_ROWS - 1 : HALO_ROWS, SLOT]
            done = jnp.where(low, new_before[3], new_before[3] + moved)
            if e > 1:
                finished.append(jnp.concatenate([*new_before[:3], done], 1))
            news = [jnp.where(low, parts[0] + moved, parts[0]), *parts[1:]]
        else:
            news = parts
        part_before, new_before = parts[3], news
        if e == 0:
            meta_row = left[META_AT + HALO - 1 : META_AT + HALO]
            index_before = jnp.broadcast_to(meta_row[:, IDX].astype(jnp.int32), (WIDTH, LANES))
        elif e <= CELLS:
            index_before = index[tile(c)]
        if len(finished) == 2:
            applied_out[(e - 3) * WIDTH : (e - 1) * WIDTH] = jnp.concatenate(finished, 0).astype(BF16)
            finished = []


def unpack_table():
    table = np.zeros((LANES, LANES), np.float32)
    for k in range(CELLS):
        table[112 + k % 6, k] = 64.0
        table[118 + k % 6, k] = 1.0
    return table


def local(orbitals, adjoint_source, eigenvalues, cell_scale, base_potential, stiffness, face_perm, restrict,
          prolong, owner, pot_slot, potential):
    vmem = pl.BlockSpec(memory_space=pltpu.VMEM)
    params = pltpu.CompilerParams(vmem_limit_bytes=32 * 2**20)
    struct = jax.ShapeDtypeStruct

    orb2 = orbitals.reshape(CELLS * WIDTH, NODES)
    src2 = adjoint_source.reshape(CELLS * WIDTH, NODES)
    owner1 = owner.reshape(CELLS)
    hbm = pl.BlockSpec(memory_space=pltpu.HBM)
    to_mate, to_other, ids, factor, eig, stiff = pl.pallas_call(
        pack_kernel,
        out_shape=(
            struct((HALO_ROWS, NODES), F32),
            struct((HALO_ROWS, NODES), F32),
            struct((1, LANES), F32),
            struct((CELLS, LANES), F32),
            struct((WIDTH, LANES), F32),
            struct((NODES, NODES), BF16),
        ),
        in_specs=[hbm] * 9,
        out_specs=(vmem,) * 6,
        scratch_shapes=[
            pltpu.SMEM((CELLS,), F32),
            pltpu.SMEM((CELLS,), jnp.int32),
            pltpu.SMEM((CELLS,), jnp.int32),
            pltpu.VMEM((2, SRC_ROWS, NODES), BF16),
            pltpu.VMEM((2, 16, NODES), BF16),
            pltpu.VMEM((2, WIDTH, NODES), F32),
            pltpu.VMEM((2, WIDTH, HALF), jnp.int32),
            pltpu.SMEM((WIDTH,), F32),
            pltpu.VMEM((HALO_ROWS, NODES), F32),
            pltpu.VMEM((HALO_ROWS, NODES), F32),
            pltpu.SemaphoreType.DMA((13,)),
        ],
        compiler_params=params,
    )(*map(in_hbm, (cell_scale, owner1, pot_slot, src2, orb2, base_potential, face_perm, stiffness, eigenvalues)))

    of_mate = lax.ppermute(to_mate, DOM, [(i, i ^ 1) for i in range(X * Z)])
    of_other = lax.ppermute(to_other, DOM, [(i, i + 1 if i % 2 else i - 1) for i in range(1, X * Z - 1)])
    ids_of_x = lax.ppermute(ids, OUTER, [((i // COPIES + i) % X * COPIES + i % COPIES, i) for i in range(X * COPIES)])

    rows = CELLS * WIDTH
    inner = rows - 2 * HALO * WIDTH
    adjoint_mid, projected_mid, linear, index, restrict_t = pl.pallas_call(
        interior_kernel,
        out_shape=(
            struct((inner, NODES), BF16),
            struct((HALF, LANES), F32),
            struct((rows, NODES), F32),
            struct((rows, LANES), jnp.int32),
            struct((HALF, NODES), BF16),
        ),
        in_specs=[hbm] * 4 + [vmem] * 7,
        out_specs=(vmem,) * 5,
        scratch_shapes=[pltpu.VMEM((rows, NODES), F32)] * 4
        + [
            pltpu.SMEM((CELLS,), jnp.int32),
            pltpu.SMEM((CELLS,), jnp.int32),
            pltpu.VMEM((HALF, HALF), F32),
            pltpu.SemaphoreType.DMA((4,)),
        ],
        compiler_params=params,
        cost_estimate=pl.CostEstimate(flops=5 * 2 * rows * NODES * NODES, bytes_accessed=4 * 2**20, transcendentals=0),
    )(*map(in_hbm, (owner1, pot_slot, restrict.T, potential)), src2, orb2, base_potential, face_perm, factor, eig, stiff)

    strip_rows = 2 * STRIP * WIDTH
    adjoint_ends, projected, ghost, left, right = pl.pallas_call(
        boundary_kernel,
        out_shape=(
            struct((2, HALO * WIDTH, NODES), BF16),
            struct((2 * HALF, LANES), F32),
            struct((2 * WIDTH, NODES), F32),
            struct((HALO_ROWS, NODES), F32),
            struct((HALO_ROWS, NODES), F32),
        ),
        in_specs=[vmem] * 12,
        out_specs=(vmem,) * 5,
        scratch_shapes=[pltpu.VMEM((strip_rows, NODES), F32)] * 4
        + [
            pltpu.VMEM((strip_rows, LANES), F32),
            pltpu.VMEM((strip_rows, LANES), jnp.int32),
        ],
        compiler_params=params,
    )(src2, orb2, base_potential, index, factor, eig, of_mate, of_other, ids_of_x, stiff, restrict_t,
      projected_mid)

    def exchanged(array, axes):
        return lax.all_to_all(array, axes, split_axis=0, concat_axis=0, tiled=True)

    tiles = jnp.sum(exchanged(projected.reshape(COPIES, 2 * WIDTH, LANES), ORB), axis=0)
    mine = jnp.broadcast_to(tiles[None, :WIDTH], (Z, WIDTH, LANES))
    mine, asking = lax.optimization_barrier((mine, tiles[WIDTH:]))
    gathered = exchanged(mine, ("z",))
    columns, adjoint2 = pl.pallas_call(
        sum_kernel,
        out_shape=(struct((X * HALF, LANES), F32), struct((rows, NODES), BF16)),
        in_specs=[vmem] * 5,
        out_specs=(vmem, hbm),
        scratch_shapes=[pltpu.SemaphoreType.DMA((3,))],
        compiler_params=params,
    )(gathered.reshape(Z * WIDTH, LANES), asking, jnp.asarray(unpack_table(), BF16),
      adjoint_mid, adjoint_ends)
    columns = exchanged(columns.reshape(X * COPIES, WIDTH, LANES), OUTER)
    updated, applied2 = pl.pallas_call(
        apply_kernel,
        out_shape=(struct((HALF, HALF), F32), struct((rows, NODES), BF16)),
        in_specs=[vmem] * 8,
        out_specs=(vmem, vmem),
        compiler_params=params,
    )(columns.reshape(X * HALF, LANES), orb2, linear, ghost, left, right, index, prolong)
    return adjoint2.reshape(orbitals.shape), updated, applied2.reshape(orbitals.shape)


def solution(mesh):
    axes = jax.sharding.Mesh(mesh.devices.reshape(X, Z, Y, CORES), ("x", "z", "y", "core"))
    in_specs = (
        P(DOM, ORB, None),
        P(DOM, ORB, None),
        P(ORB),
        P(DOM),
        P(DOM, None),
        P(),
        P(DOM, None),
        P(),
        P(),
        P(DOM, None),
        P(DOM),
        P(DOM, None),
    )
    out_specs = (P(DOM, ORB, None), P(DOM, None), P(DOM, ORB, None))
    return jax.shard_map(local, mesh=axes, in_specs=in_specs, out_specs=out_specs, check_vma=False)
```
